32 devices in a mesh: dp: 4 (over x, core), ctx: 8 (over z, y).
Axes of the slice: x: 2, y: 2, z: 4, core: 2. Of those that a mesh axis runs over, the one named last changes fastest.
Arguments:
- feats: bfloat16 [4, 1024, 12288], P('dp', 'ctx'), may hold values from -6 to 6
- short_weight: float32 [3, 12288], replicated, may hold values from -3 to 3
- grad_out: bfloat16 [4, 1024, 4096], P('dp', 'ctx'), may hold values from -6 to 6
- filt: float32 [1024, 4096], P(None, 'ctx'), may hold values from -6 to 6
Outputs:
- grad_feats: bfloat16 [4, 1024, 12288], P('dp', 'ctx')
- grad_filt: float32 [1024, 4096], P('dp', 'ctx')
The draws below stay inside these ranges and needn't reach their ends.
All inputs are finite; a program needn't handle non-finite values.
Results may differ from the reference program's by a relative error of at most 0.0057.
Values may be sent and summed in bfloat16 or wider, within the bound.
No kernel may reach another device: no remote copies, remote signals or barrier semaphores. Data moves between devices by JAX's collectives and lax.ppermute only.
A program may use at most 128 MiB of HBM per device.

```python
import math
import jax
import jax.numpy as jnp
from jax import lax

D = 4096
LEN = 1024
SEQS = 4


def block_scale(own_key, dims, cuts, smallest, top_value):
    gain, own = 1.0, jax.random.fold_in(own_key, 6)
    for dim, blocks in cuts:
        draws = jnp.exp(jax.random.uniform(jax.random.fold_in(own, dim), (blocks,), jnp.float32, smallest / len(cuts), top_value / len(cuts)))
        gain = gain * jnp.repeat(draws, dims[dim] // blocks).reshape([-1 if axis == dim else 1 for axis in range(len(dims))])
    return gain


def normal_values(key, dims, spread, most, shards=(), held_as=jnp.bfloat16):
    array = jax.random.normal(key, dims, jnp.float32) * spread
    if len(shards) > 0:
        array = block_scale(key, dims, shards, -0.22, 0.18) * array
    return jnp.clip(array, min=-most, max=most).astype(held_as)


def setup_inputs(seed: int = 0) -> dict:
    keys = jax.random.split(jax.random.key(seed), 5)
    feats = normal_values(keys[0], (SEQS, LEN, 3 * D), 1.0, 6.0, ((0, 4), (1, 8)))
    short_weight = normal_values(keys[1], (3, 3 * D), 0.6, 3.0, (), jnp.float32)
    grad_out = normal_values(keys[2], (SEQS, LEN, D), 1.0, 6.0, ((0, 4), (1, 8)))
    filt = normal_values(keys[3], (LEN, D), 1.0, 6.0, ((1, 8),), jnp.float32)
    return {"feats": feats, "short_weight": short_weight, "grad_out": grad_out, "filt": filt}


block_width = 256

def reference(feats, short_weight, grad_out, filt):
    nblk = D // block_width
    scale_inv = 1.0 / math.sqrt(LEN)
    total = 2 * LEN
    inputs = feats.reshape(SEQS, LEN, 3, nblk, block_width).transpose(3, 2, 0, 1, 4)
    weights = short_weight.reshape(3, 3, nblk, block_width).transpose(2, 1, 0, 3)
    cotan = grad_out.reshape(SEQS, LEN, nblk, block_width).transpose(2, 0, 1, 3)
    filters = filt.reshape(LEN, nblk, block_width).transpose(1, 0, 2)

    def one_block(items):
        feat_blk, taps, cot_blk, filt_blk = items
        values = feat_blk.astype(jnp.float32)
        back1 = jnp.pad(values, ((0, 0), (0, 0), (1, 0), (0, 0)))[:, :, :LEN]
        back2 = jnp.pad(values, ((0, 0), (0, 0), (2, 0), (0, 0)))[:, :, :LEN]
        mixed = taps[:, 0][:, None, None, :] * values + taps[:, 1][:, None, None, :] * back1 + taps[:, 2][:, None, None, :] * back2
        query_rows, key_rows, value_rows = (mixed[0], mixed[1], mixed[2])
        gated = (key_rows * value_rows).astype(jnp.bfloat16)
        out_grad = cot_blk.astype(jnp.float32)
        conv_grad = (out_grad * query_rows).astype(jnp.bfloat16)
        filter_now = filt_blk * scale_inv
        spec_g = jnp.fft.rfft(gated.astype(jnp.float32), n=total, axis=1)
        spec_d = jnp.fft.rfft(conv_grad.astype(jnp.float32), n=total, axis=1)
        spec_h = jnp.fft.rfft(filter_now, n=total, axis=0)[None]
        conv_out = jnp.fft.irfft(spec_h * spec_g, n=total, axis=1)[:, :LEN].astype(jnp.bfloat16)
        gated_grad = jnp.fft.irfft(jnp.conj(spec_h) * spec_d, n=total, axis=1)[:, :LEN].astype(jnp.bfloat16)
        filt_spec = lax.optimization_barrier(jnp.sum(jnp.conj(spec_g) * spec_d, axis=0))
        grad_filt = jnp.fft.irfft(filt_spec, n=total, axis=0)[:LEN] * scale_inv
        grad_q = out_grad * conv_out.astype(jnp.float32)
        grad_k = gated_grad.astype(jnp.float32) * value_rows
        grad_v = gated_grad.astype(jnp.float32) * key_rows
        grad_z = jnp.stack([grad_q, grad_k, grad_v], axis=0)
        ahead1 = jnp.pad(grad_z, ((0, 0), (0, 0), (0, 1), (0, 0)))[:, :, 1:]
        ahead2 = jnp.pad(grad_z, ((0, 0), (0, 0), (0, 2), (0, 0)))[:, :, 2:]
        grad_in = taps[:, 0][:, None, None, :] * grad_z + taps[:, 1][:, None, None, :] * ahead1 + taps[:, 2][:, None, None, :] * ahead2
        return (grad_in.astype(jnp.bfloat16), grad_filt.astype(jnp.float32))
    grad_in, grad_filt = lax.map(one_block, (inputs, weights, cotan, filters))
    grad_feats = grad_in.transpose(2, 3, 1, 0, 4).reshape(SEQS, LEN, 3 * D)
    grad_filt = grad_filt.transpose(1, 0, 2).reshape(LEN, D)
    return (grad_feats, grad_filt)
```

```python
import functools
import math

import jax
import jax.numpy as jnp
import numpy as np
from jax import lax
from jax.experimental import pallas as pl
from jax.experimental.pallas import tpu as pltpu
from jax.sharding import PartitionSpec as P

CHUNKS = 2
EXTRA = 8
TILE = 256
VMEM_LIMIT = 48 * 1024 * 1024


def odd_tables(length):
    freq = 2 * np.arange(length, dtype=np.int64)[:, None] + 1
    spot = np.arange(length, dtype=np.int64)[None, :]
    theta = (freq * spot % (4 * length)).astype(np.float64) * (2.0 * math.pi / (4 * length))
    full = np.concatenate([np.cos(theta), -np.sin(theta)], axis=0).astype(np.float32)
    high = full.astype(jnp.bfloat16)
    low = (full - high.astype(np.float32)).astype(jnp.bfloat16)
    return high, low


def conv_rows(values, before, taps):
    rows = values.shape[0]
    ext = jnp.concatenate([before, values], axis=0)
    off = ext.shape[0] - rows
    return (
        taps[0:1] * values
        + taps[1:2] * ext[off - 1 : off - 1 + rows]
        + taps[2:3] * ext[off - 2 : off - 2 + rows]
    )


def gate_kernel(count, me_ref, q_ref, k_ref, v_ref, bq_ref, bk_ref, bv_ref, tq_ref, tk_ref, tv_ref, go_ref, *outs):
    step = pl.program_id(0)

    def mixed(x_ref, b_ref, t_ref):
        return conv_rows(x_ref[...].astype(jnp.float32), b_ref[...].astype(jnp.float32), t_ref[...])

    query = mixed(q_ref, bq_ref, tq_ref)
    key = mixed(k_ref, bk_ref, tk_ref)
    value = mixed(v_ref, bv_ref, tv_ref)
    gated = (key * value).astype(jnp.bfloat16)
    grad = (go_ref[...].astype(jnp.float32) * query).astype(jnp.bfloat16)
    both = jnp.concatenate([gated, grad], axis=1)
    for j in range(count):

        @pl.when(step == j)
        def _(j=j):
            outs[j][...] = both


def gate(me, feats, before, taps, grad_out, chunk, chunks, count, cols):
    rows = feats.shape[0]
    parts = count * chunks

    def at(region):
        return lambda k, m: (0, region * parts + (m[0] ^ k) * chunks + chunk)

    spec = pltpu.PrefetchScalarGridSpec(
        num_scalar_prefetch=1,
        grid=(count,),
        in_specs=[pl.BlockSpec((rows, cols), at(r)) for r in range(3)]
        + [pl.BlockSpec((before.shape[0], cols), at(r)) for r in range(3)]
        + [pl.BlockSpec((3, cols), at(r)) for r in range(3)]
        + [pl.BlockSpec((rows, cols), at(0))],
        out_specs=[pl.BlockSpec((rows, 2 * cols), lambda k, m: (0, 0))] * count,
    )
    return pl.pallas_call(
        functools.partial(gate_kernel, count),
        grid_spec=spec,
        out_shape=[jax.ShapeDtypeStruct((rows, 2 * cols), jnp.bfloat16)] * count,
        compiler_params=pltpu.CompilerParams(vmem_limit_bytes=VMEM_LIMIT),
        cost_estimate=pl.CostEstimate(
            flops=20 * rows * cols * count, bytes_accessed=12 * rows * cols * count, transcendentals=0
        ),
        name=f"gate{chunk}",
    )(me, feats, feats, feats, before, before, before, taps, taps, taps, grad_out)


def filter_kernel(scale, filt_ref, high_ref, low_ref, out_ref):
    now = filt_ref[...] * scale
    high = now.astype(jnp.bfloat16)
    low = (now - high.astype(jnp.float32)).astype(jnp.bfloat16)

    def dot(a, b):
        return jnp.dot(a, b, preferred_element_type=jnp.float32)

    out_ref[...] = dot(high_ref[...], high) + dot(high_ref[...], low) + dot(low_ref[...], high)


def filter_spectrum(filt, high, low, scale):
    length, cols = filt.shape
    rows = high.shape[0]
    return pl.pallas_call(
        functools.partial(filter_kernel, scale),
        grid=(rows // TILE,),
        in_specs=[
            pl.BlockSpec((length, cols), lambda i: (0, 0)),
            pl.BlockSpec((TILE, length), lambda i: (i, 0)),
            pl.BlockSpec((TILE, length), lambda i: (i, 0)),
        ],
        out_specs=pl.BlockSpec((TILE, cols), lambda i: (i, 0)),
        out_shape=jax.ShapeDtypeStruct((rows, cols), jnp.float32),
        compiler_params=pltpu.CompilerParams(vmem_limit_bytes=VMEM_LIMIT),
        cost_estimate=pl.CostEstimate(
            flops=6 * rows * length * cols,
            bytes_accessed=4 * length * cols + 4 * rows * length + 4 * rows * cols,
            transcendentals=0,
        ),
        name="filter_spectrum",
    )(filt, high, low)


def spectral_kernel(count, rows, scale, me_ref, spec_ref, forward_ref, inverse_ref, *rest):
    pieces = rest[:count]
    outs = rest[count : 2 * count]
    corr_send, corr_keep = rest[2 * count : 2 * count + 2]
    data, fwd, inv, prod, res, corr, piece_sem, fwd_sem, inv_sem = rest[2 * count + 2 :]
    me = me_ref[0]
    core = me_ref[1]
    length = data.shape[0]
    cols = data.shape[1] // 2

    def piece_copy(j):
        place = pl.multiple_of((me ^ j) * rows, rows)
        return pltpu.make_async_copy(pieces[j], data.at[pl.ds(place, rows)], piece_sem.at[j])

    fwd_copy = pltpu.make_async_copy(forward_ref, fwd, fwd_sem)
    inv_copy = pltpu.make_async_copy(inverse_ref, inv, inv_sem)
    for j in range(count):
        piece_copy(j).start()
    fwd_copy.start()
    inv_copy.start()
    for j in range(count):
        piece_copy(j).wait()
    fwd_copy.wait()

    def forward(i, carry):
        low = pl.ds(pl.multiple_of(i * TILE, TILE), TILE)
        high = pl.ds(pl.multiple_of(length + i * TILE, TILE), TILE)
        re = jnp.dot(fwd[low, :], data[...], preferred_element_type=jnp.float32)
        im = jnp.dot(fwd[high, :], data[...], preferred_element_type=jnp.float32)
        g_re, d_re = re[:, :cols], re[:, cols:]
        g_im, d_im = im[:, :cols], im[:, cols:]
        h_re, h_im = spec_ref[low, :], spec_ref[high, :]
        prod[low, :cols] = (h_re * g_re - h_im * g_im).astype(jnp.bfloat16)
        prod[high, :cols] = (h_re * g_im + h_im * g_re).astype(jnp.bfloat16)
        prod[low, cols : 2 * cols] = (h_re * d_re + h_im * d_im).astype(jnp.bfloat16)
        prod[high, cols : 2 * cols] = (h_re * d_im - h_im * d_re).astype(jnp.bfloat16)
        prod[low, 2 * cols :] = (g_re * d_re + g_im * d_im).astype(jnp.bfloat16)
        prod[high, 2 * cols :] = (g_re * d_im - g_im * d_re).astype(jnp.bfloat16)
        return carry

    lax.fori_loop(0, length // TILE, forward, 0)
    inv_copy.wait()

    def inverse(i, carry):
        here = pl.ds(pl.multiple_of(i * TILE, TILE), TILE)
        out = jnp.dot(inv[here, :], prod[...], preferred_element_type=jnp.float32)
        res[here, :] = out[:, : 2 * cols].astype(jnp.bfloat16)
        corr[here, :] = out[:, 2 * cols :] * scale
        return carry

    lax.fori_loop(0, length // TILE, inverse, 0)
    res[length:, :] = jnp.zeros((res.shape[0] - length, 2 * cols), jnp.bfloat16)
    for j in range(count):
        place = pl.multiple_of((me ^ j) * rows, rows)
        outs[j][:rows, :] = res[pl.ds(place, rows), :]
        outs[j][rows:, :] = res[pl.ds(place + rows, 16), :][:EXTRA]
    half = corr_send.shape[0] // 2
    for x in range(2):
        corr_keep[x * half : (x + 1) * half, :] = corr[
            pl.ds(pl.multiple_of((2 * x + core) * half, half), half), :
        ]
        corr_send[x * half : (x + 1) * half, :] = corr[
            pl.ds(pl.multiple_of((2 * x + 1 - core) * half, half), half), :
        ]


def spectral(place, spectrum, forward, inverse, pieces, chunk, scale):
    count = len(pieces)
    rows, width = pieces[0].shape
    cols = width // 2
    length = count * rows
    vmem = pl.BlockSpec(memory_space=pltpu.VMEM)
    return pl.pallas_call(
        functools.partial(spectral_kernel, count, rows, scale),
        grid=(1,),
        in_specs=[
            pl.BlockSpec(memory_space=pltpu.SMEM),
            pl.BlockSpec((2 * length, cols), lambda i: (0, chunk)),
        ]
        + [pl.BlockSpec(memory_space=pl.ANY)] * (2 + count),
        out_specs=[vmem] * (count + 2),
        out_shape=[jax.ShapeDtypeStruct((rows + EXTRA, width), jnp.bfloat16)] * count
        + [jax.ShapeDtypeStruct((length // 2, cols), jnp.float32)] * 2,
        scratch_shapes=[
            pltpu.VMEM((length, width), jnp.bfloat16),
            pltpu.VMEM((2 * length, length), jnp.bfloat16),
            pltpu.VMEM((length, 2 * length), jnp.bfloat16),
            pltpu.VMEM((2 * length, 3 * cols), jnp.bfloat16),
            pltpu.VMEM((length + 16, width), jnp.bfloat16),
            pltpu.VMEM((length, cols), jnp.float32),
            pltpu.SemaphoreType.DMA((count,)),
            pltpu.SemaphoreType.DMA,
            pltpu.SemaphoreType.DMA,
        ],
        compiler_params=pltpu.CompilerParams(vmem_limit_bytes=VMEM_LIMIT),
        cost_estimate=pl.CostEstimate(
            flops=20 * length * length * cols,
            bytes_accessed=8 * length * length + 20 * length * cols,
            transcendentals=0,
        ),
        name=f"spectral{chunk}",
    )(place, spectrum, forward, inverse, *pieces)


def final_kernel(count, cols, width, chunk, chunks, aliased, *refs):
    me_ref = refs[0]
    k_ref, v_ref, bk_ref, bv_ref, ak_ref, av_ref, go_ref, ag_ref, tq_ref, tk_ref, tv_ref = refs[1:12]
    pieces = refs[12 : 12 + count]
    refs = refs[12 + count + (1 if aliased else 0) :]
    out_ref, back, stage, in_sem, out_sem = refs
    step = pl.program_id(0)
    me = me_ref[0]
    rows = k_ref.shape[0]

    def in_copy(j):
        return pltpu.make_async_copy(pieces[j], back.at[j], in_sem.at[j])

    @pl.when(step == 0)
    def _():
        for j in range(count):
            in_copy(j).start()

    def out_copy(j, region):
        col = pl.multiple_of(region * width + ((me ^ j) * chunks + chunk) * cols, cols)
        return pltpu.make_async_copy(
            stage.at[j, region], out_ref.at[:, pl.ds(col, cols)], out_sem.at[j, region]
        )

    def wide(x_ref, b_ref, a_ref):
        return jnp.concatenate(
            [b_ref[...], x_ref[...], a_ref[...], jnp.zeros((EXTRA - 2, cols), jnp.bfloat16)], axis=0
        ).astype(jnp.float32)

    def mixed(ext, taps):
        n = rows + EXTRA
        return taps[0:1] * ext[2 : n + 2] + taps[1:2] * ext[1 : n + 1] + taps[2:3] * ext[:n]

    def unmixed(dz, taps):
        return (
            taps[0:1] * dz[:rows] + taps[1:2] * dz[1 : rows + 1] + taps[2:3] * dz[2 : rows + 2]
        ).astype(jnp.bfloat16)

    key = mixed(wide(k_ref, bk_ref, ak_ref), tk_ref[...])
    value = mixed(wide(v_ref, bv_ref, av_ref), tv_ref[...])
    cotan = jnp.concatenate(
        [go_ref[...], ag_ref[...], jnp.zeros((EXTRA - 2, cols), jnp.bfloat16)], axis=0
    ).astype(jnp.float32)
    for j in range(count):

        @pl.when(step == j)
        def _(j=j):
            in_copy(j).wait()

    both = back[step].astype(jnp.float32)
    conv, grad = both[:, :cols], both[:, cols:]
    stage[step, 0] = unmixed(cotan * conv, tq_ref[...])
    stage[step, 1] = unmixed(grad * value, tk_ref[...])
    stage[step, 2] = unmixed(grad * key, tv_ref[...])
    for region in range(3):
        out_copy(step, region).start()

    @pl.when(step == count - 1)
    def _():
        for j in range(count):
            for region in range(3):
                out_copy(j, region).wait()


def final(me, feats, before, after, grad_out, after_out, taps, pieces, so_far, chunk, chunks):
    count = len(pieces)
    rows = feats.shape[0]
    cols = pieces[0].shape[1] // 2
    parts = count * chunks
    width = parts * cols

    def at(region):
        return lambda k, m: (0, region * parts + (m[0] ^ k) * chunks + chunk)

    any_spec = pl.BlockSpec(memory_space=pl.ANY)
    in_specs = (
        [pl.BlockSpec((rows, cols), at(r)) for r in (1, 2)]
        + [pl.BlockSpec((before.shape[0], cols), at(r)) for r in (1, 2)]
        + [pl.BlockSpec((after.shape[0], cols), at(r)) for r in (1, 2)]
        + [pl.BlockSpec((rows, cols), at(0)), pl.BlockSpec((after_out.shape[0], cols), at(0))]
        + [pl.BlockSpec((3, cols), at(r)) for r in range(3)]
        + [any_spec] * count
    )
    args = [me, feats, feats, before, before, after, after, grad_out, after_out, taps, taps, taps, *pieces]
    aliases = {}
    if so_far is not None:
        in_specs.append(any_spec)
        args.append(so_far)
        aliases = {len(args) - 1: 0}
    return pl.pallas_call(
        functools.partial(final_kernel, count, cols, width, chunk, chunks, so_far is not None),
        grid_spec=pltpu.PrefetchScalarGridSpec(
            num_scalar_prefetch=1,
            grid=(count,),
            in_specs=in_specs,
            out_specs=any_spec,
            scratch_shapes=[
                pltpu.VMEM((count, rows + EXTRA, 2 * cols), jnp.bfloat16),
                pltpu.VMEM((count, 3, rows, cols), jnp.bfloat16),
                pltpu.SemaphoreType.DMA((count,)),
                pltpu.SemaphoreType.DMA((count, 3)),
            ],
        ),
        out_shape=jax.ShapeDtypeStruct((rows, 3 * width), jnp.bfloat16),
        input_output_aliases=aliases,
        compiler_params=pltpu.CompilerParams(vmem_limit_bytes=VMEM_LIMIT),
        cost_estimate=pl.CostEstimate(
            flops=30 * rows * cols * count, bytes_accessed=16 * rows * cols * count, transcendentals=0
        ),
        name=f"final{chunk}",
    )(*args)


def exchange(pieces, axis):
    devices = range(lax.axis_size(axis))
    return [pieces[0]] + [
        lax.ppermute(pieces[j], axis, [(i, i ^ j) for i in devices]) for j in range(1, len(pieces))
    ]


def dense_shards(feats, short_weight, grad_out, filt):
    length, block = filt.shape
    count = lax.axis_size("ctx")
    feats, grad_out = feats[0], grad_out[0]
    rows = feats.shape[0]
    chunks = CHUNKS
    cols = block // chunks
    scale_inv = 1.0 / math.sqrt(length)
    high, low = odd_tables(length)
    inverse = np.ascontiguousarray(high.T)
    me = lax.axis_index("ctx")
    dp = lax.axis_index("dp")
    core, x = dp % 2, dp // 2
    place = jnp.stack([me, core]).astype(jnp.int32)
    before = from_behind(feats[rows - 2 :], "ctx", 1)
    after = from_behind(feats[:2], "ctx", -1)
    after_out = from_behind(grad_out[:2], "ctx", -1)
    spectrum = filter_spectrum(filt, high, low, scale_inv / length)

    backs, filts = [], []
    for c in range(chunks):
        pieces = gate(place, feats, before, short_weight, grad_out, c, chunks, count, cols)
        pieces = exchange(pieces, "ctx")
        *outs, send, keep = spectral(place, spectrum, high, inverse, pieces, c, scale_inv / length)
        backs.append(exchange(outs, "ctx"))
        summed = keep + lax.ppermute(send, "dp", [(i, i ^ 1) for i in range(4)])
        half = length // 4
        other = lax.dynamic_slice_in_dim(summed, (1 - x) * half, half, 0)
        mine = lax.dynamic_slice_in_dim(summed, x * half, half, 0)
        filts.append(mine + lax.ppermute(other, "dp", [(i, i ^ 2) for i in range(4)]))
    result = None
    for c in range(chunks):
        result = final(
            place, feats, before, after, grad_out, after_out, short_weight, backs[c], result, c, chunks
        )
    return (result[None], jnp.concatenate(filts, axis=1))


full_precision = lax.Precision.HIGHEST
split_precision = lax.Precision.HIGH


def from_behind(block, axis, distance):
    devices = range(lax.axis_size(axis))
    route = [(i - distance, i) for i in devices if i - distance in devices]
    return lax.ppermute(block, axis, route)


def angle_table(count_rows, count_cols, period):
    product = (
        jnp.arange(count_rows, dtype=jnp.int32)[:, None]
        * jnp.arange(count_cols, dtype=jnp.int32)[None, :]
        % period
    )
    theta = product.astype(jnp.float32) * (2.0 * math.pi / period)
    return (jnp.cos(theta), jnp.sin(theta))


def make_tables(length):
    total = 2 * length
    outer = 128
    inner = total // outer
    half = outer // 2
    freq = jnp.arange(outer, dtype=jnp.int32)[:, None, None]
    spot = (
        jnp.arange(half, dtype=jnp.int32)[None, :, None] * inner
        + jnp.arange(inner, dtype=jnp.int32)[None, None, :]
    )
    theta = (freq * spot % total).astype(jnp.float32) * (2.0 * math.pi / total)
    first = jnp.stack([jnp.cos(theta), -jnp.sin(theta)], axis=0)
    cos_b, sin_b = angle_table(inner, inner, inner)
    forward_b = jnp.stack(
        [jnp.stack([cos_b, -sin_b], axis=1), jnp.stack([sin_b, cos_b], axis=1)], axis=0
    )
    inverse_b = jnp.stack(
        [jnp.stack([cos_b, sin_b], axis=1), jnp.stack([-sin_b, cos_b], axis=1)], axis=0
    )
    return (first, forward_b, inverse_b)


def finish_forward(partial_spec, tables, accuracy):
    return jnp.einsum("sckrb,rbxq->sckxq", partial_spec, tables[1], precision=accuracy)


def data_forward(signal, tables, accuracy):
    first = tables[0]
    inner = first.shape[3]
    seqs, chans, length = signal.shape
    grid = signal.reshape(seqs, chans, length // inner, inner)
    partial_spec = jnp.einsum("rknb,scnb->sckrb", first, grid, precision=accuracy)
    return finish_forward(partial_spec, tables, accuracy)


def filter_forward(columns, tables):
    first = tables[0]
    inner = first.shape[3]
    length, chans = columns.shape
    grid = columns.reshape(length // inner, inner, chans)
    partial_spec = jnp.einsum("rknb,nbc->ckrb", first, grid, precision=full_precision)[None]
    return finish_forward(partial_spec, tables, full_precision)


def start_inverse(spectrum, tables):
    return jnp.einsum("sckxq,xqrb->sckrb", spectrum, tables[2], precision=full_precision)


def data_inverse(spectrum, tables, length):
    partial_sig = start_inverse(spectrum, tables)
    signal = jnp.einsum("sckrb,rknb->scnb", partial_sig, tables[0], precision=full_precision)
    return signal.reshape(signal.shape[0], signal.shape[1], length) / (2.0 * length)


def filter_inverse(spectrum, tables, length):
    partial_sig = start_inverse(spectrum, tables)[0]
    signal = jnp.einsum("ckrb,rknb->nbc", partial_sig, tables[0], precision=full_precision)
    return signal.reshape(length, signal.shape[2]) / (2.0 * length)


def long_spectral(gated_sig, grad_sig, filter_cols, tables, length):
    g_spec = data_forward(gated_sig, tables, split_precision)
    d_spec = data_forward(grad_sig, tables, split_precision)
    h_spec = filter_forward(filter_cols, tables)
    g_re, g_im = (g_spec[:, :, :, 0], g_spec[:, :, :, 1])
    d_re, d_im = (d_spec[:, :, :, 0], d_spec[:, :, :, 1])
    h_re, h_im = (h_spec[:, :, :, 0], h_spec[:, :, :, 1])
    conv_spec = jnp.stack([h_re * g_re - h_im * g_im, h_re * g_im + h_im * g_re], axis=3)
    grad_spec = jnp.stack([h_re * d_re + h_im * d_im, h_re * d_im - h_im * d_re], axis=3)
    prod_re = jnp.sum(g_re * d_re + g_im * d_im, axis=0, keepdims=True)
    prod_im = jnp.sum(g_re * d_im - g_im * d_re, axis=0, keepdims=True)
    prod_spec = jnp.stack([prod_re, prod_im], axis=3)
    conv_out = data_inverse(conv_spec, tables, length)
    gated_grad = data_inverse(grad_spec, tables, length)
    filt_grad = filter_inverse(prod_spec, tables, length)
    return (conv_out, gated_grad, filt_grad)


def long_shards(feats, short_weight, grad_out, filt):
    rows = feats.shape[1]
    width = feats.shape[2] // 3
    length = filt.shape[0]
    block = filt.shape[1]
    ctx_count = lax.axis_size("ctx")
    replicas = lax.axis_size("dp")
    scale_inv = 1.0 / math.sqrt(length)
    tables = make_tables(length)
    prior = from_behind(feats[:, rows - 2 :, :], "ctx", 1)
    extended = jnp.concatenate([prior, feats], axis=1).astype(jnp.float32)
    mixed = (
        short_weight[0] * extended[:, 2:]
        + short_weight[1] * extended[:, 1 : rows + 1]
        + short_weight[2] * extended[:, :rows]
    )
    query_rows = mixed[:, :, :width]
    key_rows = mixed[:, :, width : 2 * width]
    value_rows = mixed[:, :, 2 * width :]
    gated = (key_rows * value_rows).astype(jnp.bfloat16)
    out_grad = grad_out.astype(jnp.float32)
    conv_grad = (out_grad * query_rows).astype(jnp.bfloat16)
    narrow = block // replicas

    def spread(array):
        return array[0].reshape(rows, ctx_count, replicas, narrow).transpose(1, 2, 3, 0)[:, :, None]

    wide_gated, wide_grad = (
        lax.all_to_all(
            lax.all_to_all(spread(gated), "dp", split_axis=1, concat_axis=2, tiled=True),
            "ctx",
            split_axis=0,
            concat_axis=4,
            tiled=True,
        ),
        lax.all_to_all(
            lax.all_to_all(spread(conv_grad), "dp", split_axis=1, concat_axis=2, tiled=True),
            "ctx",
            split_axis=0,
            concat_axis=4,
            tiled=True,
        ),
    )
    wide_gated = wide_gated.reshape(replicas, narrow, length)
    wide_grad = wide_grad.reshape(replicas, narrow, length)
    offset = lax.axis_index("dp") * narrow
    filt_cols = lax.dynamic_slice_in_dim(filt, offset, narrow, 1)
    conv_out, gated_grad, filt_grad = long_spectral(
        wide_gated, wide_grad, filt_cols * scale_inv, tables, length
    )
    back_conv, back_grad = (
        lax.all_to_all(
            lax.all_to_all(
                conv_out.astype(jnp.bfloat16)[None, None],
                "dp",
                split_axis=2,
                concat_axis=1,
                tiled=True,
            ),
            "ctx",
            split_axis=4,
            concat_axis=0,
            tiled=True,
        ),
        lax.all_to_all(
            lax.all_to_all(
                gated_grad.astype(jnp.bfloat16)[None, None],
                "dp",
                split_axis=2,
                concat_axis=1,
                tiled=True,
            ),
            "ctx",
            split_axis=4,
            concat_axis=0,
            tiled=True,
        ),
    )

    def gather_positions(array):
        return (
            array.reshape(ctx_count, replicas, narrow, rows)
            .transpose(3, 0, 1, 2)
            .reshape(1, rows, width)
        )

    conv_rows = gather_positions(back_conv)
    grad_rows = gather_positions(back_grad)
    parts = filt_grad.reshape(replicas, length // replicas, 1, narrow)
    owned = lax.all_to_all(parts, "dp", split_axis=0, concat_axis=2, tiled=True)
    filt_out = owned.reshape(length // replicas, block) * scale_inv
    grad_query = out_grad * conv_rows.astype(jnp.float32)
    grad_key = grad_rows.astype(jnp.float32) * value_rows
    grad_value = grad_rows.astype(jnp.float32) * key_rows
    grad_mixed = jnp.concatenate([grad_query, grad_key, grad_value], axis=2)
    following = from_behind(grad_mixed[:, :2, :].astype(jnp.bfloat16), "ctx", -1).astype(
        jnp.float32
    )
    ahead = jnp.concatenate([grad_mixed, following], axis=1)
    grad_in = (
        short_weight[0] * grad_mixed
        + short_weight[1] * ahead[:, 1 : rows + 1]
        + short_weight[2] * ahead[:, 2 : rows + 2]
    )
    return (grad_in.astype(jnp.bfloat16), filt_out)


def shards(feats, short_weight, grad_out, filt):
    count = lax.axis_size("ctx")
    length, block = filt.shape
    fits = (
        length <= 1024
        and length % (2 * TILE) == 0
        and count & (count - 1) == 0
        and feats.shape[1] % 128 == 0
        and block % (128 * CHUNKS) == 0
        and lax.axis_size("dp") == 4
    )
    plan = dense_shards if fits else long_shards
    return plan(feats, short_weight, grad_out, filt)


def solution(mesh):
    return jax.shard_map(
        shards,
        mesh=mesh,
        in_specs=(P("dp", "ctx", None), P(), P("dp", "ctx", None), P(None, "ctx")),
        out_specs=(P("dp", "ctx", None), P("dp", "ctx")),
        check_vma=False,
    )
```

```python
import functools
import math

import jax
import jax.numpy as jnp
import numpy as np
from jax import lax
from jax.experimental import pallas as pl
from jax.experimental.pallas import tpu as pltpu
from jax.sharding import PartitionSpec as P

VMEM_LIMIT = 56 * 1024 * 1024
STEP = 128


def params():
    return pltpu.CompilerParams(vmem_limit_bytes=VMEM_LIMIT)


def cost(flops, moved):
    return pl.CostEstimate(flops=flops, bytes_accessed=moved, transcendentals=0)


def odd_tables(size):
    freq = 2 * np.arange(size, dtype=np.int64)[:, None] + 1
    spot = np.arange(size, dtype=np.int64)[None, :]
    theta = (freq * spot % (4 * size)).astype(np.float64) * (2.0 * math.pi / (4 * size))
    full = np.concatenate([np.cos(theta), -np.sin(theta)], axis=0).astype(np.float32)
    high = full.astype(jnp.bfloat16)
    low = (full - high.astype(np.float32)).astype(jnp.bfloat16)
    return high, low


def dot(a, b):
    return jnp.dot(a, b, preferred_element_type=jnp.float32)


def conv_rows(x_ref, before_ref, taps_ref):
    rows = x_ref.shape[0]
    ext = jnp.concatenate([before_ref[...].astype(jnp.float32), x_ref[...].astype(jnp.float32)], axis=0)
    return (
        taps_ref[0:1] * ext[2 : 2 + rows]
        + taps_ref[1:2] * ext[1 : 1 + rows]
        + taps_ref[2:3] * ext[:rows]
    )


def gate_kernel(hc, crossing, m_ref, q_ref, k_ref, v_ref, bq_ref, bk_ref, bv_ref, tq_ref, tk_ref, tv_ref, go_ref, *outs):
    step = pl.program_id(0)
    query = conv_rows(q_ref, bq_ref, tq_ref)
    key = conv_rows(k_ref, bk_ref, tk_ref)
    value = conv_rows(v_ref, bv_ref, tv_ref)
    gated = (key * value).astype(jnp.bfloat16)
    grad = (go_ref[...].astype(jnp.float32) * query).astype(jnp.bfloat16)
    cols = gated.shape[1]
    for j in range(hc):

        @pl.when(step == j)
        def _(j=j):
            outs[j][:, :cols] = gated
            outs[j][:, cols:] = grad

        if crossing:

            @pl.when((step == j) & (m_ref[1] == 0))
            def _(j=j):
                outs[hc + j][...] = gated

            @pl.when((step == j) & (m_ref[1] == 1))
            def _(j=j):
                outs[hc + j][...] = grad


def block_at(region, count, base):
    return lambda k, m: (0, region * count + (m[0] ^ (k + base)))


def gate(place, feats, before, taps, grad_out, count, cols, base):
    rows = feats.shape[0]
    hc = count // 2
    crossing = base > 0

    def at(region):
        return block_at(region, count, base)

    shapes = [jax.ShapeDtypeStruct((rows, 2 * cols), jnp.bfloat16)] * hc
    if crossing:
        shapes = shapes + [jax.ShapeDtypeStruct((rows, cols), jnp.bfloat16)] * hc
    spec = pltpu.PrefetchScalarGridSpec(
        num_scalar_prefetch=1,
        grid=(hc,),
        in_specs=[pl.BlockSpec((rows, cols), at(r)) for r in range(3)]
        + [pl.BlockSpec((before.shape[0], cols), at(r)) for r in range(3)]
        + [pl.BlockSpec((3, cols), at(r)) for r in range(3)]
        + [pl.BlockSpec((rows, cols), at(0))],
        out_specs=[pl.BlockSpec(s.shape, lambda k, m: (0, 0)) for s in shapes],
    )
    return pl.pallas_call(
        functools.partial(gate_kernel, hc, crossing),
        grid_spec=spec,
        out_shape=shapes,
        compiler_params=params(),
        cost_estimate=cost(20 * rows * cols * hc, 12 * rows * cols * hc),
        name="gate_other" if crossing else "gate_home",
    )(place, feats, feats, feats, before, before, before, taps, taps, taps, grad_out)


def signs(first, rows):
    odd = (lax.broadcasted_iota(jnp.int32, (rows, 1), 0) + first) % 2
    return 1.0 - 2.0 * odd.astype(jnp.float32)


def filter_home_kernel(scale, filt_ref, high_ref, low_ref, near_ref, far_ref):
    size = filt_ref.shape[0] // 2

    def spectrum(part):
        now = part * scale
        high = now.astype(jnp.bfloat16)
        low = (now - high.astype(jnp.float32)).astype(jnp.bfloat16)
        return dot(high_ref[...], high) + dot(high_ref[...], low) + dot(low_ref[...], high)

    near = spectrum(filt_ref[:size, :])
    far = spectrum(filt_ref[size:, :])
    near_ref[...] = near
    sign = signs(0, size)
    far_ref[:size, :] = far[:size] - sign * near[size:]
    far_ref[size:, :] = far[size:] + sign * near[:size]


def filter_home(filt, high, low, scale):
    length, cols = filt.shape
    out = jax.ShapeDtypeStruct((length, cols), jnp.float32)
    return pl.pallas_call(
        functools.partial(filter_home_kernel, scale),
        out_shape=[out, out],
        compiler_params=params(),
        cost_estimate=cost(6 * length * length * cols, 12 * length * cols + 2 * length * length),
        name="filter_home",
    )(filt, high, low)


def filter_other_kernel(filt_ref, high_ref, low_ref, near_ref):
    near_ref[...] = dot(high_ref[...], filt_ref[...]) + dot(low_ref[...], filt_ref[...])


def filter_other(part, high, low):
    size, cols = part.shape
    return pl.pallas_call(
        filter_other_kernel,
        out_shape=jax.ShapeDtypeStruct((2 * size, cols), jnp.float32),
        compiler_params=params(),
        cost_estimate=cost(8 * size * size * cols, 10 * size * cols + 8 * size * size),
        name="filter_other",
    )(part, high, low)


def times(a_re, a_im, b_re, b_im):
    return a_re * b_re - a_im * b_im, a_re * b_im + a_im * b_re


def conj_times(a_re, a_im, b_re, b_im):
    return a_re * b_re + a_im * b_im, a_re * b_im - a_im * b_re


def spectral_kernel(hc, rows, home, scale, *refs):
    m_ref, near_ref = refs[:2]
    refs = refs[2:]
    far_ref = None
    if home:
        far_ref, refs = refs[0], refs[1:]
    forward_ref, inverse_ref, refs = refs[0], refs[1], refs[2:]
    pieces, refs = refs[:hc], refs[hc:]
    crosses = ()
    if home:
        crosses, refs = refs[:hc], refs[hc:]
    outs, refs = refs[:hc], refs[hc:]
    cross_outs = ()
    if home:
        cross_outs, refs = refs[:hc], refs[hc:]
    corr_send, corr_keep, data, spec, prod, res, piece_sem = refs
    me, half, core = m_ref[0], m_ref[1], m_ref[2]
    spot = me % hc
    size = data.shape[0]
    cols = near_ref.shape[1]

    def place(j):
        return pl.ds(pl.multiple_of((spot ^ j) * rows, rows), rows)

    copies = [
        pltpu.make_async_copy(pieces[j], data.at[place(j), : 2 * cols], piece_sem.at[j]) for j in range(hc)
    ] + [
        pltpu.make_async_copy(crosses[j], data.at[place(j), 2 * cols :], piece_sem.at[hc + j])
        for j in range(len(crosses))
    ]
    for copy in copies:
        copy.start()
    for copy in copies:
        copy.wait()
    for part in range(data.shape[1] // cols):
        here = slice(part * cols, (part + 1) * cols)
        spec[:, here] = dot(forward_ref[...], data[:, here])

    def products(side):
        def body(i, carry):
            low = pl.ds(pl.multiple_of(i * STEP, STEP), STEP)
            high = pl.ds(pl.multiple_of(size + i * STEP, STEP), STEP)

            def get(part):
                here = slice(part * cols, (part + 1) * cols)
                return spec[low, here], spec[high, here]

            def put(part, value):
                here = slice(part * cols, (part + 1) * cols)
                prod[low, here] = value[0].astype(jnp.bfloat16)
                prod[high, here] = value[1].astype(jnp.bfloat16)

            g, d = get(0), get(1)
            h = near_ref[low, :], near_ref[high, :]
            conv = times(*h, *g)
            grad = conj_times(*h, *d)
            corr = conj_times(*g, *d)
            if home:
                f = far_ref[low, :], far_ref[high, :]
                gx, dx = (g, get(2)) if side == 0 else (get(2), d)
                far_conv = times(*f, *gx)
                far_grad = conj_times(*f, *dx)
                if side == 0:
                    grad = (grad[0] + far_grad[0], grad[1] + far_grad[1])
                else:
                    conv = (conv[0] + far_conv[0], conv[1] + far_conv[1])
                put(2, far_conv if side == 0 else far_grad)
                far_corr = conj_times(*gx, *dx)
                sign = signs(0, STEP)
                corr = (corr[0] + sign * far_corr[1], corr[1] - sign * far_corr[0])
                put(4, far_corr)
                put(3, corr)
            else:
                put(2, corr)
            put(0, conv)
            put(1, grad)
            return carry

        lax.fori_loop(0, size // STEP, body, 0)

    if home:

        @pl.when(half == 0)
        def _():
            products(0)

        @pl.when(half == 1)
        def _():
            products(1)

    else:
        products(0)

    def back(part):
        return dot(inverse_ref[...], prod[:, part * cols : (part + 1) * cols])

    res[:, :cols] = back(0).astype(jnp.bfloat16)
    res[:, cols : 2 * cols] = back(1).astype(jnp.bfloat16)
    for j in range(hc):
        outs[j][...] = res[place(j), : 2 * cols]
    quarter = size // 2

    def share(which, part):
        return part[which * quarter : (which + 1) * quarter]

    if home:
        res[:, 2 * cols :] = back(2).astype(jnp.bfloat16)
        for j in range(hc):
            cross_outs[j][...] = res[place(j), 2 * cols :]
        parts = [back(3) * scale, back(4) * scale]
    else:
        parts = [back(2) * scale]
    for core_now in range(2):

        @pl.when(core == core_now)
        def _(core_now=core_now):
            for x, part in enumerate(parts):
                here = slice(x * quarter, (x + 1) * quarter)
                corr_keep[here, :] = share(core_now, part)
                corr_send[here, :] = share(1 - core_now, part)


def spectral(place, near, far, forward, inverse, pieces, crosses, scale):
    hc = len(pieces)
    rows, width = pieces[0].shape
    cols = width // 2
    size = hc * rows
    home = far is not None
    vmem = pl.BlockSpec(memory_space=pltpu.VMEM)
    hbm = pl.BlockSpec(memory_space=pl.ANY)
    tables = [near, far, forward, inverse] if home else [near, forward, inverse]
    arrived = [*pieces, *crosses]
    ins = 3 if home else 2
    parts = 5 if home else 3
    shapes = [jax.ShapeDtypeStruct((rows, width), jnp.bfloat16)] * hc
    if home:
        shapes = shapes + [jax.ShapeDtypeStruct((rows, cols), jnp.bfloat16)] * hc
    corr = jax.ShapeDtypeStruct((size if home else size // 2, cols), jnp.float32)
    return pl.pallas_call(
        functools.partial(spectral_kernel, hc, rows, home, scale),
        in_specs=[pl.BlockSpec(memory_space=pltpu.SMEM)] + [vmem] * len(tables) + [hbm] * len(arrived),
        out_specs=[vmem] * (len(shapes) + 2),
        out_shape=shapes + [corr, corr],
        scratch_shapes=[
            pltpu.VMEM((size, ins * cols), jnp.bfloat16),
            pltpu.VMEM((2 * size, ins * cols), jnp.float32),
            pltpu.VMEM((2 * size, parts * cols), jnp.bfloat16),
            pltpu.VMEM((size, ins * cols), jnp.bfloat16),
            pltpu.SemaphoreType.DMA((len(arrived),)),
        ],
        compiler_params=params(),
        cost_estimate=cost(4 * size * size * cols * (ins + parts), 8 * size * size + 30 * size * cols),
        name="spectral_home" if home else "spectral_other",
    )(place, *tables, *arrived)


def final_kernel(hc, count, base, width, aliased, *refs):
    m_ref = refs[0]
    k_ref, v_ref, bk_ref, bv_ref, go_ref, tq_ref, tk_ref, tv_ref = refs[1:9]
    pieces, refs = refs[9 : 9 + hc], refs[9 + hc :]
    crosses = ()
    if base > 0:
        crosses, refs = refs[:hc], refs[hc:]
    if aliased:
        refs = refs[1:]
    out_ref, edge_ref, last_ref, back, stage, in_sem, out_sem = refs
    step = pl.program_id(0)
    me, half = m_ref[0], m_ref[1]
    rows, cols = k_ref.shape

    def in_copies(j):
        copies = [pltpu.make_async_copy(pieces[j], back.at[j, :, : 2 * cols], in_sem.at[j])]
        if base > 0:
            copies.append(pltpu.make_async_copy(crosses[j], back.at[j, :, 2 * cols :], in_sem.at[hc + j]))
        return copies

    @pl.when(step == 0)
    def _():
        for j in range(hc):
            for copy in in_copies(j):
                copy.start()

    def out_copy(j, region):
        col = pl.multiple_of(region * width + (me ^ (j + base)) * cols, cols)
        return pltpu.make_async_copy(
            stage.at[j, region], out_ref.at[:, pl.ds(col, cols)], out_sem.at[j, region]
        )

    def unmixed(region, dz, taps):
        ext = jnp.concatenate([dz, jnp.zeros((8, cols), jnp.float32)], axis=0)
        out = taps[0:1] * dz + taps[1:2] * ext[1 : rows + 1] + taps[2:3] * ext[2 : rows + 2]
        edge_ref[0, region] = dz[:2].astype(jnp.bfloat16)
        last_ref[0, region] = out[rows - 16 :]
        stage[step, region] = out.astype(jnp.bfloat16)

    key = conv_rows(k_ref, bk_ref, tk_ref)
    value = conv_rows(v_ref, bv_ref, tv_ref)
    for j in range(hc):

        @pl.when(step == j)
        def _(j=j):
            for copy in in_copies(j):
                copy.wait()

    conv = back[step, :, :cols].astype(jnp.float32)
    grad = back[step, :, cols : 2 * cols].astype(jnp.float32)
    if base > 0:
        extra = back[step, :, 2 * cols :].astype(jnp.float32)
        conv = jnp.where(half == 1, conv + extra, conv)
        grad = jnp.where(half == 0, grad + extra, grad)
    unmixed(0, go_ref[...].astype(jnp.float32) * conv, tq_ref)
    unmixed(1, grad * value, tk_ref)
    unmixed(2, grad * key, tv_ref)
    for region in range(3):
        out_copy(step, region).start()

    @pl.when(step == hc - 1)
    def _():
        for j in range(hc):
            for region in range(3):
                out_copy(j, region).wait()


def final(place, feats, before, grad_out, taps, pieces, crosses, so_far, count, base):
    hc = len(pieces)
    rows = feats.shape[0]
    cols = pieces[0].shape[1] // 2
    width = count * cols

    def at(region):
        return block_at(region, count, base)

    hbm = pl.BlockSpec(memory_space=pl.ANY)
    arrived = [*pieces, *crosses]
    in_specs = (
        [pl.BlockSpec((rows, cols), at(r)) for r in (1, 2)]
        + [pl.BlockSpec((before.shape[0], cols), at(r)) for r in (1, 2)]
        + [pl.BlockSpec((rows, cols), at(0))]
        + [pl.BlockSpec((3, cols), at(r)) for r in range(3)]
        + [hbm] * len(arrived)
    )
    args = [place, feats, feats, before, before, grad_out, taps, taps, taps, *arrived]
    aliases = {}
    if so_far is not None:
        in_specs.append(hbm)
        args.append(so_far)
        aliases = {len(args) - 1: 0}

    def own(k, m):
        return ((m[0] ^ k) % hc, 0, 0, 0)

    return pl.pallas_call(
        functools.partial(final_kernel, hc, count, base, width, so_far is not None),
        grid_spec=pltpu.PrefetchScalarGridSpec(
            num_scalar_prefetch=1,
            grid=(hc,),
            in_specs=in_specs,
            out_specs=[
                hbm,
                pl.BlockSpec((1, 3, 2, cols), own),
                pl.BlockSpec((1, 3, 16, cols), own),
            ],
            scratch_shapes=[
                pltpu.VMEM((hc, rows, (3 if base > 0 else 2) * cols), jnp.bfloat16),
                pltpu.VMEM((hc, 3, rows, cols), jnp.bfloat16),
                pltpu.SemaphoreType.DMA((len(arrived),)),
                pltpu.SemaphoreType.DMA((hc, 3)),
            ],
        ),
        out_shape=[
            jax.ShapeDtypeStruct((rows, 3 * width), jnp.bfloat16),
            jax.ShapeDtypeStruct((hc, 3, 2, cols), jnp.bfloat16),
            jax.ShapeDtypeStruct((hc, 3, 16, cols), jnp.float32),
        ],
        input_output_aliases=aliases,
        compiler_params=params(),
        cost_estimate=cost(30 * rows * cols * hc, 16 * rows * cols * hc),
        name="final_other" if base > 0 else "final_home",
    )(*args)


def fix_kernel(hc, m_ref, taps_ref, eh_ref, eo_ref, lh_ref, lo_ref, _, out_ref, stage, sem):
    me, half = m_ref[0], m_ref[1]
    cols = eh_ref.shape[3]
    width = out_ref.shape[1] // 3
    turn = me == hc - 1
    spot = lax.broadcasted_iota(jnp.int32, (16, 1), 0)
    for slot, last in enumerate((lh_ref, lo_ref)):
        mine, swapped = (eh_ref, eo_ref) if slot == 0 else (eo_ref, eh_ref)
        first = jnp.where(half == slot, 0, hc)
        for j in range(hc):
            for region in range(3):
                col = pl.ds(pl.multiple_of(region * width + (first + j) * cols, cols), cols)
                ahead = jnp.where(
                    turn, swapped[j, region].astype(jnp.float32), mine[j, region].astype(jnp.float32)
                )
                one, two = taps_ref[1:2, col], taps_ref[2:3, col]
                add = jnp.where(
                    spot == 14,
                    two * ahead[0:1],
                    jnp.where(spot == 15, one * ahead[0:1] + two * ahead[1:2], 0.0),
                )
                stage[:, col] = (last[j, region] + add).astype(jnp.bfloat16)
    copy = pltpu.make_async_copy(stage, out_ref.at[pl.ds(out_ref.shape[0] - 16, 16)], sem)
    copy.start()
    copy.wait()


def fix(place, taps, edge_home, edge_other, last_home, last_other, result):
    hc = edge_home.shape[0]
    vmem = pl.BlockSpec(memory_space=pltpu.VMEM)
    hbm = pl.BlockSpec(memory_space=pl.ANY)
    return pl.pallas_call(
        functools.partial(fix_kernel, hc),
        in_specs=[pl.BlockSpec(memory_space=pltpu.SMEM)] + [vmem] * 5 + [hbm],
        out_specs=hbm,
        out_shape=jax.ShapeDtypeStruct(result.shape, result.dtype),
        scratch_shapes=[pltpu.VMEM((16, result.shape[1]), jnp.bfloat16), pltpu.SemaphoreType.DMA],
        input_output_aliases={6: 0},
        compiler_params=params(),
        cost_estimate=cost(16 * 8 * result.shape[1], 128 * result.shape[1]),
        name="fix",
    )(place, taps, edge_home, edge_other, last_home, last_other, result)


def exchange(pieces, base):
    devices = range(lax.axis_size("ctx"))
    return [
        piece if base + j == 0 else lax.ppermute(piece, "ctx", [(i, i ^ (base + j)) for i in devices])
        for j, piece in enumerate(pieces)
    ]


def half_shards(feats, short_weight, grad_out, filt):
    length, block = filt.shape
    count = lax.axis_size("ctx")
    hc = count // 2
    size = length // 2
    quarter = length // 4
    feats, grad_out = feats[0], grad_out[0]
    rows = feats.shape[0]
    high, low = odd_tables(size)
    inverse = np.ascontiguousarray(high.T)
    scale = 1.0 / (math.sqrt(length) * size)
    me = lax.axis_index("ctx")
    dp = lax.axis_index("dp")
    core, x = dp % 2, dp // 2
    place = jnp.stack([me, me // hc, core]).astype(jnp.int32)
    before = from_behind(feats[rows - 2 :], "ctx", 1)

    share = size // 4
    part = (lax.dynamic_slice_in_dim(filt, dp * share, share, 0) * scale).astype(jnp.bfloat16)
    part = lax.ppermute(part, "ctx", [(i, i ^ hc) for i in range(count)])
    part = lax.all_gather(part, "dp", axis=0, tiled=True)

    near, far = filter_home(filt, high, low, scale)
    gated = gate(place, feats, before, short_weight, grad_out, count, block, hc)
    home_pieces = gate(place, feats, before, short_weight, grad_out, count, block, 0)
    home_pieces = exchange(home_pieces, 0)
    crosses = exchange(gated[hc:], hc)
    other_pieces = exchange(gated[:hc], 0)
    near_other = filter_other(part, high, low)

    outs = spectral(place, near, far, high, inverse, home_pieces, crosses, scale)
    home_back = exchange(outs[:hc], 0)
    cross_back = exchange(outs[hc : 2 * hc], hc)
    send, keep = outs[2 * hc :]
    summed = keep + lax.ppermute(send, "dp", [(i, i ^ 1) for i in range(4)])
    there = lax.dynamic_slice_in_dim(summed, (1 - x) * quarter, quarter, 0).astype(jnp.bfloat16)
    here = lax.dynamic_slice_in_dim(summed, x * quarter, quarter, 0)
    filt_home = here + lax.ppermute(there, "dp", [(i, i ^ 2) for i in range(4)]).astype(jnp.float32)

    outs = spectral(place, near_other, None, high, inverse, other_pieces, (), scale)
    other_back = exchange(outs[:hc], 0)
    send, keep = outs[hc:]
    summed = keep + lax.ppermute(send, "dp", [(i, i ^ 1) for i in range(4)])
    summed = summed + lax.ppermute(summed.astype(jnp.bfloat16), "dp", [(2, 0), (3, 1)]).astype(jnp.float32)
    owners = [(d * count + i, d * count + (i ^ hc)) for d in range(2) for i in range(count)]
    filt_other = lax.ppermute(summed.astype(jnp.bfloat16), ("dp", "ctx"), owners).astype(jnp.float32)
    filt_out = filt_home + filt_other

    result, edge_home, last_home = final(
        place, feats, before, grad_out, short_weight, home_back, (), None, count, 0
    )
    result, edge_other, last_other = final(
        place, feats, before, grad_out, short_weight, other_back, cross_back, result, count, hc
    )
    edge_home = from_behind(edge_home, "ctx", -1)
    edge_other = from_behind(edge_other, "ctx", -1)
    result = fix(place, short_weight, edge_home, edge_other, last_home, last_other, result)
    return (result[None], filt_out)


full_precision = lax.Precision.HIGHEST
split_precision = lax.Precision.HIGH


def from_behind(block, axis, distance):
    devices = range(lax.axis_size(axis))
    route = [(i - distance, i) for i in devices if i - distance in devices]
    return lax.ppermute(block, axis, route)


def angle_table(count_rows, count_cols, period):
    product = (
        jnp.arange(count_rows, dtype=jnp.int32)[:, None]
        * jnp.arange(count_cols, dtype=jnp.int32)[None, :]
        % period
    )
    theta = product.astype(jnp.float32) * (2.0 * math.pi / period)
    return (jnp.cos(theta), jnp.sin(theta))


def make_tables(length):
    total = 2 * length
    outer = 128
    inner = total // outer
    half = outer // 2
    freq = jnp.arange(outer, dtype=jnp.int32)[:, None, None]
    spot = (
        jnp.arange(half, dtype=jnp.int32)[None, :, None] * inner
        + jnp.arange(inner, dtype=jnp.int32)[None, None, :]
    )
    theta = (freq * spot % total).astype(jnp.float32) * (2.0 * math.pi / total)
    first = jnp.stack([jnp.cos(theta), -jnp.sin(theta)], axis=0)
    cos_b, sin_b = angle_table(inner, inner, inner)
    forward_b = jnp.stack(
        [jnp.stack([cos_b, -sin_b], axis=1), jnp.stack([sin_b, cos_b], axis=1)], axis=0
    )
    inverse_b = jnp.stack(
        [jnp.stack([cos_b, sin_b], axis=1), jnp.stack([-sin_b, cos_b], axis=1)], axis=0
    )
    return (first, forward_b, inverse_b)


def finish_forward(partial_spec, tables, accuracy):
    return jnp.einsum("sckrb,rbxq->sckxq", partial_spec, tables[1], precision=accuracy)


def data_forward(signal, tables, accuracy):
    first = tables[0]
    inner = first.shape[3]
    seqs, chans, length = signal.shape
    grid = signal.reshape(seqs, chans, length // inner, inner)
    partial_spec = jnp.einsum("rknb,scnb->sckrb", first, grid, precision=accuracy)
    return finish_forward(partial_spec, tables, accuracy)


def filter_forward(columns, tables):
    first = tables[0]
    inner = first.shape[3]
    length, chans = columns.shape
    grid = columns.reshape(length // inner, inner, chans)
    partial_spec = jnp.einsum("rknb,nbc->ckrb", first, grid, precision=full_precision)[None]
    return finish_forward(partial_spec, tables, full_precision)


def start_inverse(spectrum, tables):
    return jnp.einsum("sckxq,xqrb->sckrb", spectrum, tables[2], precision=full_precision)


def data_inverse(spectrum, tables, length):
    partial_sig = start_inverse(spectrum, tables)
    signal = jnp.einsum("sckrb,rknb->scnb", partial_sig, tables[0], precision=full_precision)
    return signal.reshape(signal.shape[0], signal.shape[1], length) / (2.0 * length)


def filter_inverse(spectrum, tables, length):
    partial_sig = start_inverse(spectrum, tables)[0]
    signal = jnp.einsum("ckrb,rknb->nbc", partial_sig, tables[0], precision=full_precision)
    return signal.reshape(length, signal.shape[2]) / (2.0 * length)


def long_spectral(gated_sig, grad_sig, filter_cols, tables, length):
    g_spec = data_forward(gated_sig, tables, split_precision)
    d_spec = data_forward(grad_sig, tables, split_precision)
    h_spec = filter_forward(filter_cols, tables)
    g_re, g_im = (g_spec[:, :, :, 0], g_spec[:, :, :, 1])
    d_re, d_im = (d_spec[:, :, :, 0], d_spec[:, :, :, 1])
    h_re, h_im = (h_spec[:, :, :, 0], h_spec[:, :, :, 1])
    conv_spec = jnp.stack([h_re * g_re - h_im * g_im, h_re * g_im + h_im * g_re], axis=3)
    grad_spec = jnp.stack([h_re * d_re + h_im * d_im, h_re * d_im - h_im * d_re], axis=3)
    prod_re = jnp.sum(g_re * d_re + g_im * d_im, axis=0, keepdims=True)
    prod_im = jnp.sum(g_re * d_im - g_im * d_re, axis=0, keepdims=True)
    prod_spec = jnp.stack([prod_re, prod_im], axis=3)
    conv_out = data_inverse(conv_spec, tables, length)
    gated_grad = data_inverse(grad_spec, tables, length)
    filt_grad = filter_inverse(prod_spec, tables, length)
    return (conv_out, gated_grad, filt_grad)


def long_shards(feats, short_weight, grad_out, filt):
    rows = feats.shape[1]
    width = feats.shape[2] // 3
    length = filt.shape[0]
    block = filt.shape[1]
    ctx_count = lax.axis_size("ctx")
    replicas = lax.axis_size("dp")
    scale_inv = 1.0 / math.sqrt(length)
    tables = make_tables(length)
    prior = from_behind(feats[:, rows - 2 :, :], "ctx", 1)
    extended = jnp.concatenate([prior, feats], axis=1).astype(jnp.float32)
    mixed = (
        short_weight[0] * extended[:, 2:]
        + short_weight[1] * extended[:, 1 : rows + 1]
        + short_weight[2] * extended[:, :rows]
    )
    query_rows = mixed[:, :, :width]
    key_rows = mixed[:, :, width : 2 * width]
    value_rows = mixed[:, :, 2 * width :]
    gated = (key_rows * value_rows).astype(jnp.bfloat16)
    out_grad = grad_out.astype(jnp.float32)
    conv_grad = (out_grad * query_rows).astype(jnp.bfloat16)
    narrow = block // replicas

    def spread(array):
        return array[0].reshape(rows, ctx_count, replicas, narrow).transpose(1, 2, 3, 0)[:, :, None]

    wide_gated, wide_grad = (
        lax.all_to_all(
            lax.all_to_all(spread(gated), "dp", split_axis=1, concat_axis=2, tiled=True),
            "ctx",
            split_axis=0,
            concat_axis=4,
            tiled=True,
        ),
        lax.all_to_all(
            lax.all_to_all(spread(conv_grad), "dp", split_axis=1, concat_axis=2, tiled=True),
            "ctx",
            split_axis=0,
            concat_axis=4,
            tiled=True,
        ),
    )
    wide_gated = wide_gated.reshape(replicas, narrow, length)
    wide_grad = wide_grad.reshape(replicas, narrow, length)
    offset = lax.axis_index("dp") * narrow
    filt_cols = lax.dynamic_slice_in_dim(filt, offset, narrow, 1)
    conv_out, gated_grad, filt_grad = long_spectral(
        wide_gated, wide_grad, filt_cols * scale_inv, tables, length
    )
    back_conv, back_grad = (
        lax.all_to_all(
            lax.all_to_all(
                conv_out.astype(jnp.bfloat16)[None, None],
                "dp",
                split_axis=2,
                concat_axis=1,
                tiled=True,
            ),
            "ctx",
            split_axis=4,
            concat_axis=0,
            tiled=True,
        ),
        lax.all_to_all(
            lax.all_to_all(
                gated_grad.astype(jnp.bfloat16)[None, None],
                "dp",
                split_axis=2,
                concat_axis=1,
                tiled=True,
            ),
            "ctx",
            split_axis=4,
            concat_axis=0,
            tiled=True,
        ),
    )

    def gather_positions(array):
        return (
            array.reshape(ctx_count, replicas, narrow, rows)
            .transpose(3, 0, 1, 2)
            .reshape(1, rows, width)
        )

    conv_rows = gather_positions(back_conv)
    grad_rows = gather_positions(back_grad)
    parts = filt_grad.reshape(replicas, length // replicas, 1, narrow)
    owned = lax.all_to_all(parts, "dp", split_axis=0, concat_axis=2, tiled=True)
    filt_out = owned.reshape(length // replicas, block) * scale_inv
    grad_query = out_grad * conv_rows.astype(jnp.float32)
    grad_key = grad_rows.astype(jnp.float32) * value_rows
    grad_value = grad_rows.astype(jnp.float32) * key_rows
    grad_mixed = jnp.concatenate([grad_query, grad_key, grad_value], axis=2)
    following = from_behind(grad_mixed[:, :2, :].astype(jnp.bfloat16), "ctx", -1).astype(
        jnp.float32
    )
    ahead = jnp.concatenate([grad_mixed, following], axis=1)
    grad_in = (
        short_weight[0] * grad_mixed
        + short_weight[1] * ahead[:, 1 : rows + 1]
        + short_weight[2] * ahead[:, 2 : rows + 2]
    )
    return (grad_in.astype(jnp.bfloat16), filt_out)


def shards(feats, short_weight, grad_out, filt):
    count = lax.axis_size("ctx")
    length, block = filt.shape
    fits = (
        length <= 1024
        and length % (4 * STEP) == 0
        and count > 1
        and count & (count - 1) == 0
        and feats.shape[1] % 128 == 0
        and block % 128 == 0
        and lax.axis_size("dp") == 4
    )
    plan = half_shards if fits else long_shards
    return plan(feats, short_weight, grad_out, filt)


def solution(mesh):
    return jax.shard_map(
        shards,
        mesh=mesh,
        in_specs=(P("dp", "ctx", None), P(), P("dp", "ctx", None), P(None, "ctx")),
        out_specs=(P("dp", "ctx", None), P("dp", "ctx")),
        check_vma=False,
    )
```

```python
import functools
import math

import jax
import jax.numpy as jnp
import numpy as np
from jax import lax
from jax.experimental import pallas as pl
from jax.experimental.pallas import tpu as pltpu
from jax.sharding import PartitionSpec as P

VMEM_LIMIT = 56 * 1024 * 1024
STEP = 128
STRIP = 128


def params():
    return pltpu.CompilerParams(vmem_limit_bytes=VMEM_LIMIT)


def cost(flops, moved):
    return pl.CostEstimate(flops=flops, bytes_accessed=moved, transcendentals=0)


def odd_tables(size):
    freq = 2 * np.arange(size, dtype=np.int64)[:, None] + 1
    spot = np.arange(size, dtype=np.int64)[None, :]
    theta = (freq * spot % (4 * size)).astype(np.float64) * (2.0 * math.pi / (4 * size))
    full = np.concatenate([np.cos(theta), -np.sin(theta)], axis=0).astype(np.float32)
    high = full.astype(jnp.bfloat16)
    low = (full - high.astype(np.float32)).astype(jnp.bfloat16)
    return high, low


def dot(a, b):
    return jnp.dot(a, b, preferred_element_type=jnp.float32)


def run(copies):
    for copy in copies:
        copy.start()
    return copies


def finish(copies):
    for copy in copies:
        copy.wait()


def behind(values, before):
    spot = lax.broadcasted_iota(jnp.int32, (values.shape[0], 1), 0)
    one = jnp.where(spot == 0, before[1:2], pltpu.roll(values, 1, 0))
    two = jnp.where(spot == 0, before[0:1], jnp.where(spot == 1, before[1:2], pltpu.roll(values, 2, 0)))
    return one, two


def conv_rows(values, before, taps):
    values = values.astype(jnp.float32)
    one, two = behind(values, before.astype(jnp.float32))
    return taps[0:1] * values + taps[1:2] * one + taps[2:3] * two


def where(hc):
    me = lax.axis_index("ctx")
    return me, me // hc, lax.axis_index("dp") % 2


def strips(cols):
    return [slice(c, c + STRIP) for c in range(0, cols, STRIP)]


def gate_kernel(hc, count, base, feats_ref, before, taps_ref, grad_ref, *refs):
    outs, refs = refs[:hc], refs[hc:]
    parts, taps, stage, in_sem, small_sem, out_sem = refs
    rows, cols = parts.shape[2:]
    me, half, core = where(hc)

    def column(region, j):
        return pl.ds(pl.multiple_of((region * count + (me ^ (base + j))) * cols, cols), cols)

    small = run([pltpu.make_async_copy(taps_ref, taps, small_sem)])
    loads = [
        run(
            [
                pltpu.make_async_copy(feats_ref.at[:, column(r, j)], parts.at[j, r], in_sem.at[j, r])
                for r in range(3)
            ]
            + [pltpu.make_async_copy(grad_ref.at[:, column(0, j)], parts.at[j, 3], in_sem.at[j, 3])]
        )
        for j in range(hc)
    ]
    finish(small)
    stores = []
    for j in range(hc):
        finish(loads[j])
        mine = [(before[:, column(r, j)], taps[:, column(r, j)]) for r in range(3)]
        for strip in strips(cols):
            query, key, value = (
                conv_rows(parts[j, r, :, strip], mine[r][0][:, strip], mine[r][1][:, strip])
                for r in range(3)
            )
            stage[j, :, strip] = (key * value).astype(jnp.bfloat16)
            stage[j, :, cols + strip.start : cols + strip.stop] = (
                parts[j, 3, :, strip].astype(jnp.float32) * query
            ).astype(jnp.bfloat16)
        stores += run([pltpu.make_async_copy(stage.at[j], outs[j], out_sem.at[j])])
    finish(stores)


def gate(feats, before, taps, grad_out, count, cols, base):
    rows = feats.shape[0]
    hc = count // 2
    shapes = [jax.ShapeDtypeStruct((rows, 2 * cols), jnp.bfloat16)] * hc
    hbm = pl.BlockSpec(memory_space=pl.ANY)
    return pl.pallas_call(
        functools.partial(gate_kernel, hc, count, base),
        in_specs=[hbm, pl.BlockSpec(memory_space=pltpu.VMEM), hbm, hbm],
        out_specs=[hbm] * len(shapes),
        out_shape=shapes,
        scratch_shapes=[
            pltpu.VMEM((hc, 4, rows, cols), jnp.bfloat16),
            pltpu.VMEM(taps.shape, taps.dtype),
            pltpu.VMEM((hc, rows, 2 * cols), jnp.bfloat16),
            pltpu.SemaphoreType.DMA((hc, 4)),
            pltpu.SemaphoreType.DMA,
            pltpu.SemaphoreType.DMA((len(shapes),)),
        ],
        compiler_params=params(),
        cost_estimate=cost(20 * rows * cols * hc, 12 * rows * cols * hc),
        name="gate_other",
    )(feats, before, taps, grad_out)


def signs(first, rows):
    odd = (lax.broadcasted_iota(jnp.int32, (rows, 1), 0) + first) % 2
    return 1.0 - 2.0 * odd.astype(jnp.float32)


def filter_home_kernel(scale, filt_ref, high_ref, low_ref, near_ref, far_ref):
    size = filt_ref.shape[0] // 2

    def spectrum(part):
        now = part * scale
        high = now.astype(jnp.bfloat16)
        low = (now - high.astype(jnp.float32)).astype(jnp.bfloat16)
        return dot(high_ref[...], high) + dot(high_ref[...], low) + dot(low_ref[...], high)

    near = spectrum(filt_ref[:size, :])
    far = spectrum(filt_ref[size:, :])
    near_ref[...] = near
    sign = signs(0, size)
    far_ref[:size, :] = far[:size] - sign * near[size:]
    far_ref[size:, :] = far[size:] + sign * near[:size]


def prepare_kernel(hc, count, scale, *refs):
    filters, refs = refs[:3], refs[3:]
    gate_in, refs = refs[:4], refs[4:]
    gate_out, refs = refs[:hc], refs[hc:]
    gate_kernel(hc, count, 0, *gate_in, *gate_out, *refs[2:])
    filter_home_kernel(scale, *filters, *refs[:2])


def prepare(filt, high, low, feats, before, taps, grad_out, scale, count):
    rows = feats.shape[0]
    length, cols = filt.shape
    hc = count // 2
    shapes = [jax.ShapeDtypeStruct((rows, 2 * cols), jnp.bfloat16)] * hc
    spectra = [jax.ShapeDtypeStruct((length, cols), jnp.float32)] * 2
    hbm = pl.BlockSpec(memory_space=pl.ANY)
    vmem = pl.BlockSpec(memory_space=pltpu.VMEM)
    return pl.pallas_call(
        functools.partial(prepare_kernel, hc, count, scale),
        in_specs=[vmem] * 3 + [hbm, vmem, hbm, hbm],
        out_specs=[hbm] * hc + [vmem] * 2,
        out_shape=shapes + spectra,
        scratch_shapes=[
            pltpu.VMEM((hc, 4, rows, cols), jnp.bfloat16),
            pltpu.VMEM(taps.shape, taps.dtype),
            pltpu.VMEM((hc, rows, 2 * cols), jnp.bfloat16),
            pltpu.SemaphoreType.DMA((hc, 4)),
            pltpu.SemaphoreType.DMA,
            pltpu.SemaphoreType.DMA((len(shapes),)),
        ],
        compiler_params=params(),
        cost_estimate=cost(8 * length * length * cols, 20 * length * cols),
        name="prepare",
    )(filt, high, low, feats, before, taps, grad_out)


def assemble_kernel(hc, *refs):
    pieces, out_ref, stage, in_sem, out_sem = refs[:hc], *refs[hc:]
    rows = pieces[0].shape[0]
    cols = pieces[0].shape[1] // 2
    me, half, _ = where(hc)
    side = pl.ds(pl.multiple_of(half * cols, cols), cols)
    loads = run([pltpu.make_async_copy(pieces[j].at[:, side], stage.at[j], in_sem.at[j]) for j in range(hc)])
    stores = []
    for j in range(hc):
        finish([loads[j]])
        place = pl.ds(pl.multiple_of(((me % hc) ^ j) * rows, rows), rows)
        stores += run([pltpu.make_async_copy(stage.at[j], out_ref.at[place], out_sem.at[j])])
    finish(stores)


def assemble(pieces):
    hc = len(pieces)
    rows, width = pieces[0].shape
    hbm = pl.BlockSpec(memory_space=pl.ANY)
    return pl.pallas_call(
        functools.partial(assemble_kernel, hc),
        in_specs=[hbm] * hc,
        out_specs=hbm,
        out_shape=jax.ShapeDtypeStruct((hc * rows, width // 2), jnp.bfloat16),
        scratch_shapes=[
            pltpu.VMEM((hc, rows, width // 2), jnp.bfloat16),
            pltpu.SemaphoreType.DMA((hc,)),
            pltpu.SemaphoreType.DMA((hc,)),
        ],
        compiler_params=params(),
        cost_estimate=cost(0, 2 * hc * rows * width),
        name="assemble",
    )(*pieces)


def times(a_re, a_im, b_re, b_im):
    return a_re * b_re - a_im * b_im, a_re * b_im + a_im * b_re


def conj_times(a_re, a_im, b_re, b_im):
    return a_re * b_re + a_im * b_im, a_re * b_im - a_im * b_re


def spectral_kernel(hc, rows, home, scale, *refs):
    tables, refs = refs[: 4 if home else 5], refs[4 if home else 5 :]
    pieces, refs = refs[:hc], refs[hc:]
    cross_ref = None
    if home:
        cross_ref, refs = refs[0], refs[1:]
    outs, refs = refs[:hc], refs[hc:]
    cross_outs = ()
    if home:
        cross_outs, refs = refs[:hc], refs[hc:]
    corr_send, corr_keep, refs = refs[0], refs[1], refs[2:]
    held, refs = refs[: len(tables)], refs[len(tables) :]
    data, spec, prod, res, corr, piece_sem, table_sem, out_sem, corr_sem = refs[:9]
    forward_ref, inverse_ref = held[:2]
    near_ref, far_ref = (held[2], held[3]) if home else (refs[-1], None)
    me, half, core = where(hc)
    spot = me % hc
    size = data.shape[0]
    cols = res.shape[1] // (3 if home else 2)

    def place(j):
        return pl.ds(pl.multiple_of((spot ^ j) * rows, rows), rows)

    def load(i):
        return run([pltpu.make_async_copy(tables[i], held[i], table_sem.at[i])])

    forward_copy = load(0)
    piece_copies = run(
        [pltpu.make_async_copy(pieces[j], data.at[place(j), : 2 * cols], piece_sem.at[j]) for j in range(hc)]
    )
    cross_copies = []
    if home:
        cross_copies = run([pltpu.make_async_copy(cross_ref, data.at[:, 2 * cols :], piece_sem.at[hc])])
    filter_copies = [copy for i in range(2, len(tables)) for copy in load(i)]
    inverse_copy = load(1)
    finish(forward_copy)
    finish(piece_copies)
    for part in range(data.shape[1] // cols):
        if part == 2:
            finish(cross_copies)
        here = slice(part * cols, (part + 1) * cols)
        spec[:, here] = dot(forward_ref[...], data[:, here])
    finish(filter_copies)
    if not home:
        low_ref, mine_ref, theirs_ref = held[2:]
        share = mine_ref.shape[0]
        mine = pl.ds(pl.multiple_of(core * share, share), share)
        theirs = pl.ds(pl.multiple_of((1 - core) * share, share), share)
        near_ref[...] = (
            dot(forward_ref[:, mine], mine_ref[...])
            + dot(forward_ref[:, theirs], theirs_ref[...])
            + dot(low_ref[:, mine], mine_ref[...])
            + dot(low_ref[:, theirs], theirs_ref[...])
        )

    def products(side):
        def body(i, carry):
            low = pl.ds(pl.multiple_of(i * STEP, STEP), STEP)
            high = pl.ds(pl.multiple_of(size + i * STEP, STEP), STEP)

            def get(part):
                here = slice(part * cols, (part + 1) * cols)
                return spec[low, here], spec[high, here]

            def put(part, value):
                here = slice(part * cols, (part + 1) * cols)
                prod[low, here] = value[0].astype(jnp.bfloat16)
                prod[high, here] = value[1].astype(jnp.bfloat16)

            g, d = get(0), get(1)
            h = near_ref[low, :], near_ref[high, :]
            conv = times(*h, *g)
            grad = conj_times(*h, *d)
            corr = conj_times(*g, *d)
            if home:
                f = far_ref[low, :], far_ref[high, :]
                gx, dx = (g, get(2)) if side == 0 else (get(2), d)
                far_conv = times(*f, *gx)
                far_grad = conj_times(*f, *dx)
                if side == 0:
                    grad = (grad[0] + far_grad[0], grad[1] + far_grad[1])
                else:
                    conv = (conv[0] + far_conv[0], conv[1] + far_conv[1])
                put(2, far_conv if side == 0 else far_grad)
                far_corr = conj_times(*gx, *dx)
                sign = signs(0, STEP)
                corr = (corr[0] + sign * far_corr[1], corr[1] - sign * far_corr[0])
                put(4, far_corr)
                put(3, corr)
            else:
                put(2, corr)
            put(0, conv)
            put(1, grad)
            return carry

        lax.fori_loop(0, size // STEP, body, 0)

    if home:

        @pl.when(half == 0)
        def _():
            products(0)

        @pl.when(half == 1)
        def _():
            products(1)

    else:
        products(0)

    def back(part):
        return dot(inverse_ref[...], prod[:, part * cols : (part + 1) * cols])

    finish(inverse_copy)
    res[:, :cols] = back(0).astype(jnp.bfloat16)
    res[:, cols : 2 * cols] = back(1).astype(jnp.bfloat16)
    stores = run(
        [pltpu.make_async_copy(res.at[place(j), : 2 * cols], outs[j], out_sem.at[j]) for j in range(hc)]
    )
    if home:
        res[:, 2 * cols :] = back(2).astype(jnp.bfloat16)
        stores += run(
            [
                pltpu.make_async_copy(res.at[place(j), 2 * cols :], cross_outs[j], out_sem.at[hc + j])
                for j in range(hc)
            ]
        )
    quarter = size // 2
    for x in range(2 if home else 1):
        corr[x] = back((3 if home else 2) + x) * scale
        for i, (ref, which) in enumerate(((corr_send, 1 - core), (corr_keep, core))):
            lags = pl.ds(pl.multiple_of(which * quarter, quarter), quarter)
            stores += run(
                [
                    pltpu.make_async_copy(
                        corr.at[x, lags], ref.at[x * quarter : (x + 1) * quarter], corr_sem.at[x, i]
                    )
                ]
            )
    finish(stores)


def spectral(forward, inverse, filters, pieces, cross, scale):
    hc = len(pieces)
    rows, width = pieces[0].shape
    cols = width // 2
    size = hc * rows
    home = cross is not None
    hbm = pl.BlockSpec(memory_space=pl.ANY)
    tables = [forward, inverse, *filters]
    arrived = [*pieces, cross] if home else pieces
    ins = 3 if home else 2
    parts = 5 if home else 3
    shapes = [jax.ShapeDtypeStruct((rows, width), jnp.bfloat16)] * hc
    if home:
        shapes = shapes + [jax.ShapeDtypeStruct((rows, cols), jnp.bfloat16)] * hc
    corr = jax.ShapeDtypeStruct((size if home else size // 2, cols), jnp.float32)
    return pl.pallas_call(
        functools.partial(spectral_kernel, hc, rows, home, scale),
        in_specs=[hbm] * (len(tables) + len(arrived)),
        out_specs=[hbm] * (len(shapes) + 2),
        out_shape=shapes + [corr, corr],
        scratch_shapes=[pltpu.VMEM(t.shape, t.dtype) for t in tables]
        + [
            pltpu.VMEM((size, ins * cols), jnp.bfloat16),
            pltpu.VMEM((2 * size, ins * cols), jnp.float32),
            pltpu.VMEM((2 * size, parts * cols), jnp.bfloat16),
            pltpu.VMEM((size, ins * cols), jnp.bfloat16),
            pltpu.VMEM((2 if home else 1, size, cols), jnp.float32),
            pltpu.SemaphoreType.DMA((len(arrived),)),
            pltpu.SemaphoreType.DMA((len(tables),)),
            pltpu.SemaphoreType.DMA((len(shapes),)),
            pltpu.SemaphoreType.DMA((2, 2)),
        ]
        + ([] if home else [pltpu.VMEM((2 * size, cols), jnp.float32)]),
        compiler_params=params(),
        cost_estimate=cost(4 * size * size * cols * (ins + parts), 8 * size * size + 30 * size * cols),
        name="spectral_home" if home else "spectral_other",
    )(*tables, *arrived)


def final_kernel(hc, count, base, top, aliased, *refs):
    feats_ref, before, grad_ref, taps_ref = refs[:4]
    pieces, refs = refs[4 : 4 + hc], refs[4 + hc :]
    crosses = ()
    if base > 0:
        crosses, refs = refs[:hc], refs[hc:]
    if aliased:
        refs = refs[1:]
    out_ref = last_ref = stage = last = None
    if top:
        edge_ref, parts, taps, back, edge, in_sem, small_sem, back_sem, end_sem = refs
    else:
        out_ref, edge_ref, last_ref, parts, taps, back, edge, last, stage = refs[:9]
        in_sem, small_sem, back_sem, end_sem, out_sem = refs[9:]
    me, half, _ = where(hc)
    rows, cols = parts.shape[2:]

    def column(region, j):
        return pl.ds(pl.multiple_of((region * count + (me ^ (base + j))) * cols, cols), cols)

    small = run([pltpu.make_async_copy(taps_ref, taps, small_sem)])
    loads = []
    for j in range(hc):
        copies = [
            pltpu.make_async_copy(source.at[:rows, column(r, j)], parts.at[j, r], in_sem.at[j, r])
            for r, source in enumerate((grad_ref, feats_ref, feats_ref))
        ]
        copies.append(
            pltpu.make_async_copy(pieces[j].at[:rows], back.at[j, :, : 2 * cols], back_sem.at[j])
        )
        if base > 0:
            copies.append(
                pltpu.make_async_copy(crosses[j].at[:rows], back.at[j, :, 2 * cols :], back_sem.at[hc + j])
            )
        loads.append(run(copies))
    finish(small)
    stores = []
    spot = lax.broadcasted_iota(jnp.int32, (rows, 1), 0)
    for j in range(hc):
        finish(loads[j])
        near_taps = [taps[:, column(r, j)] for r in range(3)]
        near_before = [before[:, column(r, j)] for r in range(3)]
        slot = (me ^ (base + j)) % hc
        for strip in strips(cols):

            def unmixed(region, dz):
                edge[slot, region, :, strip] = dz[:2].astype(jnp.bfloat16)
                if top:
                    return
                weights = near_taps[region][:, strip]
                one = jnp.where(spot < rows - 1, pltpu.roll(dz, rows - 1, 0), 0.0)
                two = jnp.where(spot < rows - 2, pltpu.roll(dz, rows - 2, 0), 0.0)
                out = weights[0:1] * dz + weights[1:2] * one + weights[2:3] * two
                last[slot, region, :, strip] = out[rows - 16 :]
                stage[j, region, :, strip] = out.astype(jnp.bfloat16)

            key, value = (
                conv_rows(parts[j, r, :, strip], near_before[r][:, strip], near_taps[r][:, strip])
                for r in (1, 2)
            )
            conv = back[j, :, strip].astype(jnp.float32)
            grad = back[j, :, cols + strip.start : cols + strip.stop].astype(jnp.float32)
            if base > 0:
                extra = back[j, :, 2 * cols + strip.start : 2 * cols + strip.stop].astype(jnp.float32)
                conv = jnp.where(half == 1, conv + extra, conv)
                grad = jnp.where(half == 0, grad + extra, grad)
            unmixed(0, parts[j, 0, :, strip].astype(jnp.float32) * conv)
            unmixed(1, grad * value)
            unmixed(2, grad * key)
        if not top:
            stores += run(
                [
                    pltpu.make_async_copy(stage.at[j, r], out_ref.at[:, column(r, j)], out_sem.at[j, r])
                    for r in range(3)
                ]
            )
    stores += run([pltpu.make_async_copy(edge, edge_ref, end_sem.at[0])])
    if not top:
        stores += run([pltpu.make_async_copy(last, last_ref, end_sem.at[1])])
    finish(stores)


def final(feats, before, grad_out, taps, pieces, crosses, so_far, count, base, top=False):
    hc = len(pieces)
    rows = 16 if top else feats.shape[0]
    cols = pieces[0].shape[1] // 2
    hbm = pl.BlockSpec(memory_space=pl.ANY)
    arrived = [*pieces, *crosses]
    args = [feats, before, grad_out, taps, *arrived]
    aliases = {}
    if so_far is not None:
        args.append(so_far)
        aliases = {len(args) - 1: 0}
    edge = jax.ShapeDtypeStruct((hc, 3, 2, cols), jnp.bfloat16)
    last = jax.ShapeDtypeStruct((hc, 3, 16, cols), jnp.float32)
    shapes = [edge] if top else [jax.ShapeDtypeStruct(feats.shape, jnp.bfloat16), edge, last]
    scratch = [
        pltpu.VMEM((hc, 3, rows, cols), jnp.bfloat16),
        pltpu.VMEM(taps.shape, taps.dtype),
        pltpu.VMEM((hc, rows, (3 if base > 0 else 2) * cols), jnp.bfloat16),
        pltpu.VMEM(edge.shape, edge.dtype),
    ]
    if not top:
        scratch += [
            pltpu.VMEM(last.shape, last.dtype),
            pltpu.VMEM((hc, 3, rows, cols), jnp.bfloat16),
        ]
    scratch += [
        pltpu.SemaphoreType.DMA((hc, 3)),
        pltpu.SemaphoreType.DMA,
        pltpu.SemaphoreType.DMA((len(arrived),)),
        pltpu.SemaphoreType.DMA((2,)),
    ]
    if not top:
        scratch.append(pltpu.SemaphoreType.DMA((hc, 3)))
    name = ("edge_" if top else "final_") + ("other" if base > 0 else "home")
    return pl.pallas_call(
        functools.partial(final_kernel, hc, count, base, top, so_far is not None),
        in_specs=[hbm, pl.BlockSpec(memory_space=pltpu.VMEM)] + [hbm] * (len(args) - 2),
        out_specs=[hbm] * len(shapes),
        scratch_shapes=scratch,
        out_shape=shapes,
        input_output_aliases=aliases,
        compiler_params=params(),
        cost_estimate=cost(30 * rows * cols * hc, 16 * rows * cols * hc),
        name=name,
    )(*args)


def fix_kernel(hc, taps_ref, eh_ref, eo_ref, lh_ref, lo_ref, _, out_ref, stage, sem):
    me, half, _ = where(hc)
    cols = eh_ref.shape[3]
    width = out_ref.shape[1] // 3
    turn = me == hc - 1
    spot = lax.broadcasted_iota(jnp.int32, (16, 1), 0)
    for slot, last in enumerate((lh_ref, lo_ref)):
        mine, swapped = (eh_ref, eo_ref) if slot == 0 else (eo_ref, eh_ref)
        first = jnp.where(half == slot, 0, hc)
        for j in range(hc):
            for region in range(3):
                col = pl.ds(pl.multiple_of(region * width + (first + j) * cols, cols), cols)
                ahead = jnp.where(
                    turn, swapped[j, region].astype(jnp.float32), mine[j, region].astype(jnp.float32)
                )
                one, two = taps_ref[1:2, col], taps_ref[2:3, col]
                add = jnp.where(
                    spot == 14,
                    two * ahead[0:1],
                    jnp.where(spot == 15, one * ahead[0:1] + two * ahead[1:2], 0.0),
                )
                stage[:, col] = (last[j, region] + add).astype(jnp.bfloat16)
    copy = pltpu.make_async_copy(stage, out_ref.at[pl.ds(out_ref.shape[0] - 16, 16)], sem)
    copy.start()
    copy.wait()


def fix(taps, edge_home, edge_other, last_home, last_other, result):
    hc = edge_home.shape[0]
    vmem = pl.BlockSpec(memory_space=pltpu.VMEM)
    hbm = pl.BlockSpec(memory_space=pl.ANY)
    return pl.pallas_call(
        functools.partial(fix_kernel, hc),
        in_specs=[vmem] * 5 + [hbm],
        out_specs=hbm,
        out_shape=jax.ShapeDtypeStruct(result.shape, result.dtype),
        scratch_shapes=[pltpu.VMEM((16, result.shape[1]), jnp.bfloat16), pltpu.SemaphoreType.DMA],
        input_output_aliases={5: 0},
        compiler_params=params(),
        cost_estimate=cost(16 * 8 * result.shape[1], 128 * result.shape[1]),
        name="fix",
    )(taps, edge_home, edge_other, last_home, last_other, result)


def exchange(pieces, base):
    devices = range(lax.axis_size("ctx"))
    return [
        piece if base + j == 0 else lax.ppermute(piece, "ctx", [(i, i ^ (base + j)) for i in devices])
        for j, piece in enumerate(pieces)
    ]


def half_shards(feats, short_weight, grad_out, filt):
    length, block = filt.shape
    count = lax.axis_size("ctx")
    hc = count // 2
    size = length // 2
    quarter = length // 4
    feats, grad_out = feats[0], grad_out[0]
    rows = feats.shape[0]
    high, low = odd_tables(size)
    inverse = np.ascontiguousarray(high.T)
    scale = 1.0 / (math.sqrt(length) * size)
    me = lax.axis_index("ctx")
    dp = lax.axis_index("dp")
    core, x = dp % 2, dp // 2
    tie = lax.optimization_barrier
    cores = [(i, i ^ 1) for i in range(4)]

    late, source = tie((feats[rows - 2 :], filt))
    before = from_behind(late, "ctx", 1)
    share = size // 2
    part = (lax.dynamic_slice_in_dim(source, core * share, share, 0) * scale).astype(jnp.bfloat16)
    part = lax.ppermute(part, "ctx", [(i, i ^ hc) for i in range(count)])
    gated = gate(feats, before, short_weight, grad_out, count, block, hc)

    ready, gated = tie((before, gated))
    other_pieces = exchange(gated, 0)
    outs = prepare(filt, high, low, feats, ready, short_weight, grad_out, scale, count)
    outs, other_pieces, part = tie((outs, other_pieces, part))
    near, far = outs[hc:]

    home_pieces = exchange(outs[:hc], 0)
    cross, part = tie((assemble(other_pieces), part))
    cross = lax.ppermute(cross, "ctx", [(i, i ^ hc) for i in range(count)])
    rest = lax.ppermute(part, "dp", cores)
    outs = spectral(high, inverse, (low, part, rest), other_pieces, None, scale)
    outs, home_pieces, cross = tie((outs, home_pieces, cross))

    other_back = exchange(outs[:hc], 0)
    send, keep = outs[hc:]
    summed = keep + lax.ppermute(send, "dp", cores)
    summed = summed + lax.ppermute(summed.astype(jnp.bfloat16), "dp", [(2, 0), (3, 1)]).astype(jnp.float32)
    crossing = summed.astype(jnp.bfloat16)
    outs = spectral(high, inverse, (near, far), home_pieces, cross, scale)
    outs, other_back, crossing = tie((outs, other_back, crossing))

    home_back = exchange(outs[:hc], 0)
    cross_outs = outs[hc : 2 * hc]
    early = exchange(cross_outs[: hc // 2], hc)
    late, sums, home_back, early, crossing = tie(
        (cross_outs[hc // 2 :], outs[2 * hc :], home_back, early, crossing)
    )

    cross_back = list(early) + exchange(late, hc + hc // 2)
    owners = [(d * count + i, d * count + (i ^ hc)) for d in range(2) for i in range(count)]
    filt_other = lax.ppermute(crossing, ("dp", "ctx"), owners)
    send, keep = sums
    came = lax.ppermute(send, "dp", cores)
    result, edge_home, last_home = final(
        feats, before, grad_out, short_weight, home_back, (), None, count, 0
    )
    keep, came, edge_home = tie((keep, came, edge_home))
    summed = keep + came
    there = lax.dynamic_slice_in_dim(summed, (1 - x) * quarter, quarter, 0).astype(jnp.bfloat16)
    here = lax.dynamic_slice_in_dim(summed, x * quarter, quarter, 0)
    cross_back, there, edge_home = tie((cross_back, there, edge_home))

    there = lax.ppermute(there, "dp", [(i, i ^ 2) for i in range(4)])
    filt_out = here + there.astype(jnp.float32) + filt_other.astype(jnp.float32)
    edge_home = from_behind(edge_home, "ctx", -1)
    (edge_other,) = final(
        feats, before, grad_out, short_weight, other_back, cross_back, None, count, hc, True
    )
    edge_other = from_behind(edge_other, "ctx", -1)
    result, _, last_other = final(
        feats, before, grad_out, short_weight, other_back, cross_back, result, count, hc
    )
    result = fix(short_weight, edge_home, edge_other, last_home, last_other, result)
    return (result[None], filt_out)


full_precision = lax.Precision.HIGHEST
split_precision = lax.Precision.HIGH


def from_behind(block, axis, distance):
    devices = range(lax.axis_size(axis))
    route = [(i - distance, i) for i in devices if i - distance in devices]
    return lax.ppermute(block, axis, route)


def angle_table(count_rows, count_cols, period):
    product = (
        jnp.arange(count_rows, dtype=jnp.int32)[:, None]
        * jnp.arange(count_cols, dtype=jnp.int32)[None, :]
        % period
    )
    theta = product.astype(jnp.float32) * (2.0 * math.pi / period)
    return (jnp.cos(theta), jnp.sin(theta))


def make_tables(length):
    total = 2 * length
    outer = 128
    inner = total // outer
    half = outer // 2
    freq = jnp.arange(outer, dtype=jnp.int32)[:, None, None]
    spot = (
        jnp.arange(half, dtype=jnp.int32)[None, :, None] * inner
        + jnp.arange(inner, dtype=jnp.int32)[None, None, :]
    )
    theta = (freq * spot % total).astype(jnp.float32) * (2.0 * math.pi / total)
    first = jnp.stack([jnp.cos(theta), -jnp.sin(theta)], axis=0)
    cos_b, sin_b = angle_table(inner, inner, inner)
    forward_b = jnp.stack(
        [jnp.stack([cos_b, -sin_b], axis=1), jnp.stack([sin_b, cos_b], axis=1)], axis=0
    )
    inverse_b = jnp.stack(
        [jnp.stack([cos_b, sin_b], axis=1), jnp.stack([-sin_b, cos_b], axis=1)], axis=0
    )
    return (first, forward_b, inverse_b)


def finish_forward(partial_spec, tables, accuracy):
    return jnp.einsum("sckrb,rbxq->sckxq", partial_spec, tables[1], precision=accuracy)


def data_forward(signal, tables, accuracy):
    first = tables[0]
    inner = first.shape[3]
    seqs, chans, length = signal.shape
    grid = signal.reshape(seqs, chans, length // inner, inner)
    partial_spec = jnp.einsum("rknb,scnb->sckrb", first, grid, precision=accuracy)
    return finish_forward(partial_spec, tables, accuracy)


def filter_forward(columns, tables):
    first = tables[0]
    inner = first.shape[3]
    length, chans = columns.shape
    grid = columns.reshape(length // inner, inner, chans)
    partial_spec = jnp.einsum("rknb,nbc->ckrb", first, grid, precision=full_precision)[None]
    return finish_forward(partial_spec, tables, full_precision)


def start_inverse(spectrum, tables):
    return jnp.einsum("sckxq,xqrb->sckrb", spectrum, tables[2], precision=full_precision)


def data_inverse(spectrum, tables, length):
    partial_sig = start_inverse(spectrum, tables)
    signal = jnp.einsum("sckrb,rknb->scnb", partial_sig, tables[0], precision=full_precision)
    return signal.reshape(signal.shape[0], signal.shape[1], length) / (2.0 * length)


def filter_inverse(spectrum, tables, length):
    partial_sig = start_inverse(spectrum, tables)[0]
    signal = jnp.einsum("ckrb,rknb->nbc", partial_sig, tables[0], precision=full_precision)
    return signal.reshape(length, signal.shape[2]) / (2.0 * length)


def long_spectral(gated_sig, grad_sig, filter_cols, tables, length):
    g_spec = data_forward(gated_sig, tables, split_precision)
    d_spec = data_forward(grad_sig, tables, split_precision)
    h_spec = filter_forward(filter_cols, tables)
    g_re, g_im = (g_spec[:, :, :, 0], g_spec[:, :, :, 1])
    d_re, d_im = (d_spec[:, :, :, 0], d_spec[:, :, :, 1])
    h_re, h_im = (h_spec[:, :, :, 0], h_spec[:, :, :, 1])
    conv_spec = jnp.stack([h_re * g_re - h_im * g_im, h_re * g_im + h_im * g_re], axis=3)
    grad_spec = jnp.stack([h_re * d_re + h_im * d_im, h_re * d_im - h_im * d_re], axis=3)
    prod_re = jnp.sum(g_re * d_re + g_im * d_im, axis=0, keepdims=True)
    prod_im = jnp.sum(g_re * d_im - g_im * d_re, axis=0, keepdims=True)
    prod_spec = jnp.stack([prod_re, prod_im], axis=3)
    conv_out = data_inverse(conv_spec, tables, length)
    gated_grad = data_inverse(grad_spec, tables, length)
    filt_grad = filter_inverse(prod_spec, tables, length)
    return (conv_out, gated_grad, filt_grad)


def long_shards(feats, short_weight, grad_out, filt):
    rows = feats.shape[1]
    width = feats.shape[2] // 3
    length = filt.shape[0]
    block = filt.shape[1]
    ctx_count = lax.axis_size("ctx")
    replicas = lax.axis_size("dp")
    scale_inv = 1.0 / math.sqrt(length)
    tables = make_tables(length)
    prior = from_behind(feats[:, rows - 2 :, :], "ctx", 1)
    extended = jnp.concatenate([prior, feats], axis=1).astype(jnp.float32)
    mixed = (
        short_weight[0] * extended[:, 2:]
        + short_weight[1] * extended[:, 1 : rows + 1]
        + short_weight[2] * extended[:, :rows]
    )
    query_rows = mixed[:, :, :width]
    key_rows = mixed[:, :, width : 2 * width]
    value_rows = mixed[:, :, 2 * width :]
    gated = (key_rows * value_rows).astype(jnp.bfloat16)
    out_grad = grad_out.astype(jnp.float32)
    conv_grad = (out_grad * query_rows).astype(jnp.bfloat16)
    narrow = block // replicas

    def spread(array):
        return array[0].reshape(rows, ctx_count, replicas, narrow).transpose(1, 2, 3, 0)[:, :, None]

    wide_gated, wide_grad = (
        lax.all_to_all(
            lax.all_to_all(spread(gated), "dp", split_axis=1, concat_axis=2, tiled=True),
            "ctx",
            split_axis=0,
            concat_axis=4,
            tiled=True,
        ),
        lax.all_to_all(
            lax.all_to_all(spread(conv_grad), "dp", split_axis=1, concat_axis=2, tiled=True),
            "ctx",
            split_axis=0,
            concat_axis=4,
            tiled=True,
        ),
    )
    wide_gated = wide_gated.reshape(replicas, narrow, length)
    wide_grad = wide_grad.reshape(replicas, narrow, length)
    offset = lax.axis_index("dp") * narrow
    filt_cols = lax.dynamic_slice_in_dim(filt, offset, narrow, 1)
    conv_out, gated_grad, filt_grad = long_spectral(
        wide_gated, wide_grad, filt_cols * scale_inv, tables, length
    )
    back_conv, back_grad = (
        lax.all_to_all(
            lax.all_to_all(
                conv_out.astype(jnp.bfloat16)[None, None],
                "dp",
                split_axis=2,
                concat_axis=1,
                tiled=True,
            ),
            "ctx",
            split_axis=4,
            concat_axis=0,
            tiled=True,
        ),
        lax.all_to_all(
            lax.all_to_all(
                gated_grad.astype(jnp.bfloat16)[None, None],
                "dp",
                split_axis=2,
                concat_axis=1,
                tiled=True,
            ),
            "ctx",
            split_axis=4,
            concat_axis=0,
            tiled=True,
        ),
    )

    def gather_positions(array):
        return (
            array.reshape(ctx_count, replicas, narrow, rows)
            .transpose(3, 0, 1, 2)
            .reshape(1, rows, width)
        )

    conv_rows = gather_positions(back_conv)
    grad_rows = gather_positions(back_grad)
    parts = filt_grad.reshape(replicas, length // replicas, 1, narrow)
    owned = lax.all_to_all(parts, "dp", split_axis=0, concat_axis=2, tiled=True)
    filt_out = owned.reshape(length // replicas, block) * scale_inv
    grad_query = out_grad * conv_rows.astype(jnp.float32)
    grad_key = grad_rows.astype(jnp.float32) * value_rows
    grad_value = grad_rows.astype(jnp.float32) * key_rows
    grad_mixed = jnp.concatenate([grad_query, grad_key, grad_value], axis=2)
    following = from_behind(grad_mixed[:, :2, :].astype(jnp.bfloat16), "ctx", -1).astype(
        jnp.float32
    )
    ahead = jnp.concatenate([grad_mixed, following], axis=1)
    grad_in = (
        short_weight[0] * grad_mixed
        + short_weight[1] * ahead[:, 1 : rows + 1]
        + short_weight[2] * ahead[:, 2 : rows + 2]
    )
    return (grad_in.astype(jnp.bfloat16), filt_out)


def shards(feats, short_weight, grad_out, filt):
    count = lax.axis_size("ctx")
    length, block = filt.shape
    fits = (
        length <= 1024
        and length % (4 * STEP) == 0
        and count > 1
        and count & (count - 1) == 0
        and feats.shape[1] % 128 == 0
        and block % 128 == 0
        and lax.axis_size("dp") == 4
    )
    plan = half_shards if fits else long_shards
    return plan(feats, short_weight, grad_out, filt)


def solution(mesh):
    return jax.shard_map(
        shards,
        mesh=mesh,
        in_specs=(P("dp", "ctx", None), P(), P("dp", "ctx", None), P(None, "ctx")),
        out_specs=(P("dp", "ctx", None), P("dp", "ctx")),
        check_vma=False,
    )
```

```python
import functools
import math

import jax
import jax.numpy as jnp
import numpy as np
from jax import lax
from jax.experimental import pallas as pl
from jax.experimental.pallas import tpu as pltpu
from jax.sharding import PartitionSpec as P

STEP = 128
STRIP = 128


def params(mebibytes):
    return pltpu.CompilerParams(vmem_limit_bytes=mebibytes * 1024 * 1024)


def cost(flops, moved):
    return pl.CostEstimate(flops=flops, bytes_accessed=moved, transcendentals=0)


def odd_tables(size):
    freq = 2 * np.arange(size, dtype=np.int64)[:, None] + 1
    spot = np.arange(size, dtype=np.int64)[None, :]
    theta = (freq * spot % (4 * size)).astype(np.float64) * (2.0 * math.pi / (4 * size))
    full = np.concatenate([np.cos(theta), -np.sin(theta)], axis=0).astype(np.float32)
    high = full.astype(jnp.bfloat16)
    low = (full - high.astype(np.float32)).astype(jnp.bfloat16)
    return high, low


def dot(a, b):
    return jnp.dot(a, b, preferred_element_type=jnp.float32)


def run(copies):
    for copy in copies:
        copy.start()
    return copies


def finish(copies):
    for copy in copies:
        copy.wait()


def behind(values, before):
    spot = lax.broadcasted_iota(jnp.int32, (values.shape[0], 1), 0)
    one = jnp.where(spot == 0, before[1:2], pltpu.roll(values, 1, 0))
    two = jnp.where(spot == 0, before[0:1], jnp.where(spot == 1, before[1:2], pltpu.roll(values, 2, 0)))
    return one, two


def conv_rows(values, before, taps):
    values = values.astype(jnp.float32)
    one, two = behind(values, before.astype(jnp.float32))
    return taps[0:1] * values + taps[1:2] * one + taps[2:3] * two


def where(hc):
    me = lax.axis_index("ctx")
    return me, me // hc, lax.axis_index("dp") % 2


def strips(cols):
    return [slice(c, c + STRIP) for c in range(0, cols, STRIP)]


def gate_kernel(hc, count, base, feats_ref, before, taps_ref, grad_ref, *refs):
    crossing = base > 0
    outs, refs = refs[: hc * (2 if crossing else 1)], refs[hc * (2 if crossing else 1) :]
    parts, taps, stage, in_sem, small_sem, out_sem = refs
    rows, cols = parts.shape[2:]
    me, half, core = where(hc)

    def column(region, j):
        return pl.ds(pl.multiple_of((region * count + (me ^ (base + j))) * cols, cols), cols)

    small = run([pltpu.make_async_copy(taps_ref, taps, small_sem)])
    loads = [
        run(
            [
                pltpu.make_async_copy(feats_ref.at[:, column(r, j)], parts.at[j, r], in_sem.at[j, r])
                for r in range(3)
            ]
            + [pltpu.make_async_copy(grad_ref.at[:, column(0, j)], parts.at[j, 3], in_sem.at[j, 3])]
        )
        for j in range(hc)
    ]
    finish(small)
    stores = []
    for j in range(hc):
        finish(loads[j])
        mine = [(before[:, column(r, j)], taps[:, column(r, j)]) for r in range(3)]
        for strip in strips(cols):
            query, key, value = (
                conv_rows(parts[j, r, :, strip], mine[r][0][:, strip], mine[r][1][:, strip])
                for r in range(3)
            )
            stage[j, :, strip] = (key * value).astype(jnp.bfloat16)
            stage[j, :, cols + strip.start : cols + strip.stop] = (
                parts[j, 3, :, strip].astype(jnp.float32) * query
            ).astype(jnp.bfloat16)
        stores += run([pltpu.make_async_copy(stage.at[j], outs[j], out_sem.at[j])])
        if crossing:
            crossed = stage.at[j, :, pl.ds(pl.multiple_of(half * cols, cols), cols)]
            stores += run([pltpu.make_async_copy(crossed, outs[hc + j], out_sem.at[hc + j])])
    finish(stores)


def gate(feats, before, taps, grad_out, count, cols, base):
    rows = feats.shape[0]
    hc = count // 2
    shapes = [jax.ShapeDtypeStruct((rows, 2 * cols), jnp.bfloat16)] * hc
    shapes = shapes + [jax.ShapeDtypeStruct((rows, cols), jnp.bfloat16)] * hc
    hbm = pl.BlockSpec(memory_space=pl.ANY)
    return pl.pallas_call(
        functools.partial(gate_kernel, hc, count, base),
        in_specs=[hbm, pl.BlockSpec(memory_space=pltpu.VMEM), hbm, hbm],
        out_specs=[hbm] * len(shapes),
        out_shape=shapes,
        scratch_shapes=[
            pltpu.VMEM((hc, 4, rows, cols), jnp.bfloat16),
            pltpu.VMEM(taps.shape, taps.dtype),
            pltpu.VMEM((hc, rows, 2 * cols), jnp.bfloat16),
            pltpu.SemaphoreType.DMA((hc, 4)),
            pltpu.SemaphoreType.DMA,
            pltpu.SemaphoreType.DMA((len(shapes),)),
        ],
        compiler_params=params(56),
        cost_estimate=cost(20 * rows * cols * hc, 12 * rows * cols * hc),
        name="gate_other",
    )(feats, before, taps, grad_out)


def signs(first, rows):
    odd = (lax.broadcasted_iota(jnp.int32, (rows, 1), 0) + first) % 2
    return 1.0 - 2.0 * odd.astype(jnp.float32)


def filter_home_kernel(scale, filt_ref, high_ref, low_ref, near_ref, far_ref):
    size = filt_ref.shape[0] // 2

    def spectrum(part):
        now = part * scale
        high = now.astype(jnp.bfloat16)
        low = (now - high.astype(jnp.float32)).astype(jnp.bfloat16)
        return dot(high_ref[...], high) + dot(high_ref[...], low) + dot(low_ref[...], high)

    near = spectrum(filt_ref[:size, :])
    far = spectrum(filt_ref[size:, :])
    near_ref[...] = near
    sign = signs(0, size)
    far_ref[:size, :] = far[:size] - sign * near[size:]
    far_ref[size:, :] = far[size:] + sign * near[:size]


def prepare_kernel(hc, count, scale, *refs):
    filters, refs = refs[:3], refs[3:]
    gate_in, refs = refs[:4], refs[4:]
    gate_out, refs = refs[:hc], refs[hc:]
    gate_kernel(hc, count, 0, *gate_in, *gate_out, *refs[2:])
    filter_home_kernel(scale, *filters, *refs[:2])


def prepare(filt, high, low, feats, before, taps, grad_out, scale, count):
    rows = feats.shape[0]
    length, cols = filt.shape
    hc = count // 2
    shapes = [jax.ShapeDtypeStruct((rows, 2 * cols), jnp.bfloat16)] * hc
    spectra = [jax.ShapeDtypeStruct((length, cols), jnp.float32)] * 2
    hbm = pl.BlockSpec(memory_space=pl.ANY)
    vmem = pl.BlockSpec(memory_space=pltpu.VMEM)
    return pl.pallas_call(
        functools.partial(prepare_kernel, hc, count, scale),
        in_specs=[vmem] * 3 + [hbm, vmem, hbm, hbm],
        out_specs=[hbm] * hc + [vmem] * 2,
        out_shape=shapes + spectra,
        scratch_shapes=[
            pltpu.VMEM((hc, 4, rows, cols), jnp.bfloat16),
            pltpu.VMEM(taps.shape, taps.dtype),
            pltpu.VMEM((hc, rows, 2 * cols), jnp.bfloat16),
            pltpu.SemaphoreType.DMA((hc, 4)),
            pltpu.SemaphoreType.DMA,
            pltpu.SemaphoreType.DMA((len(shapes),)),
        ],
        compiler_params=params(56),
        cost_estimate=cost(8 * length * length * cols, 20 * length * cols),
        name="prepare",
    )(filt, high, low, feats, before, taps, grad_out)


def times(a_re, a_im, b_re, b_im):
    return a_re * b_re - a_im * b_im, a_re * b_im + a_im * b_re


def conj_times(a_re, a_im, b_re, b_im):
    return a_re * b_re + a_im * b_im, a_re * b_im - a_im * b_re


def spectral_kernel(hc, rows, home, scale, *refs):
    tables, refs = refs[: 4 if home else 5], refs[4 if home else 5 :]
    pieces, refs = refs[:hc], refs[hc:]
    crosses = ()
    if home:
        crosses, refs = refs[:hc], refs[hc:]
    outs, refs = refs[: 1 if home else hc], refs[1 if home else hc :]
    cross_outs = ()
    if home:
        cross_outs, refs = refs[:hc], refs[hc:]
    sums, refs = refs[:2], refs[2:]
    held, refs = refs[: len(tables)], refs[len(tables) :]
    data, spec, prod, res, corr, piece_sem, table_sem, out_sem, corr_sem = refs[:9]
    forward_ref, inverse_ref = held[:2]
    near_ref, far_ref = (held[2], held[3]) if home else (refs[-1], None)
    me, half, core = where(hc)
    spot = me % hc
    size = data.shape[0]
    cols = res.shape[1] // (3 if home else 2)

    def place(j):
        return pl.ds(pl.multiple_of((spot ^ j) * rows, rows), rows)

    def load(i):
        return run([pltpu.make_async_copy(tables[i], held[i], table_sem.at[i])])

    forward_copy = load(0)
    piece_copies = run(
        [pltpu.make_async_copy(pieces[j], data.at[place(j), : 2 * cols], piece_sem.at[j]) for j in range(hc)]
    )
    cross_copies = run(
        [
            pltpu.make_async_copy(crosses[j], data.at[place(j), 2 * cols :], piece_sem.at[hc + j])
            for j in range(len(crosses))
        ]
    )
    filter_copies = [copy for i in range(2, len(tables)) for copy in load(i)]
    inverse_copy = load(1)
    finish(forward_copy)
    finish(piece_copies)
    for part in range(data.shape[1] // cols):
        if part == 2:
            finish(cross_copies)
        here = slice(part * cols, (part + 1) * cols)
        spec[:, here] = dot(forward_ref[...], data[:, here])
    finish(filter_copies)
    if not home:
        low_ref, mine_ref, theirs_ref = held[2:]
        share = mine_ref.shape[0]
        mine = pl.ds(pl.multiple_of(core * share, share), share)
        theirs = pl.ds(pl.multiple_of((1 - core) * share, share), share)
        near_ref[...] = (
            dot(forward_ref[:, mine], mine_ref[...])
            + dot(forward_ref[:, theirs], theirs_ref[...])
            + dot(low_ref[:, mine], mine_ref[...])
            + dot(low_ref[:, theirs], theirs_ref[...])
        )

    def products(side):
        def body(i, carry):
            low = pl.ds(pl.multiple_of(i * STEP, STEP), STEP)
            high = pl.ds(pl.multiple_of(size + i * STEP, STEP), STEP)

            def get(part):
                here = slice(part * cols, (part + 1) * cols)
                return spec[low, here], spec[high, here]

            def put(part, value):
                here = slice(part * cols, (part + 1) * cols)
                prod[low, here] = value[0].astype(jnp.bfloat16)
                prod[high, here] = value[1].astype(jnp.bfloat16)

            g, d = get(0), get(1)
            h = near_ref[low, :], near_ref[high, :]
            conv = times(*h, *g)
            grad = conj_times(*h, *d)
            corr = conj_times(*g, *d)
            if home:
                f = far_ref[low, :], far_ref[high, :]
                gx, dx = (g, get(2)) if side == 0 else (get(2), d)
                far_conv = times(*f, *gx)
                far_grad = conj_times(*f, *dx)
                if side == 0:
                    grad = (grad[0] + far_grad[0], grad[1] + far_grad[1])
                else:
                    conv = (conv[0] + far_conv[0], conv[1] + far_conv[1])
                put(2, far_conv if side == 0 else far_grad)
                far_corr = conj_times(*gx, *dx)
                sign = signs(0, STEP)
                corr = (corr[0] + sign * far_corr[1], corr[1] - sign * far_corr[0])
                put(4, far_corr)
                put(3, corr)
            else:
                put(2, corr)
            put(0, conv)
            put(1, grad)
            return carry

        lax.fori_loop(0, size // STEP, body, 0)

    if home:

        @pl.when(half == 0)
        def _():
            products(0)

        @pl.when(half == 1)
        def _():
            products(1)

    else:
        products(0)

    def back(part):
        return dot(inverse_ref[...], prod[:, part * cols : (part + 1) * cols])

    finish(inverse_copy)
    res[:, :cols] = back(0).astype(jnp.bfloat16)
    res[:, cols : 2 * cols] = back(1).astype(jnp.bfloat16)
    if home:
        stores = run([pltpu.make_async_copy(res.at[:, : 2 * cols], outs[0], out_sem.at[0])])
    else:
        stores = run(
            [pltpu.make_async_copy(res.at[place(j), : 2 * cols], outs[j], out_sem.at[j]) for j in range(hc)]
        )
    if home:
        res[:, 2 * cols :] = back(2).astype(jnp.bfloat16)
        stores += run(
            [
                pltpu.make_async_copy(res.at[place(j), 2 * cols :], cross_outs[j], out_sem.at[hc + j])
                for j in range(hc)
            ]
        )
    quarter = size // 2
    for x in range(2 if home else 1):
        corr[x] = back((3 if home else 2) + x) * scale
        for i, which in enumerate((1 - core, core)):
            lags = pl.ds(pl.multiple_of(which * quarter, quarter), quarter)
            stores += run(
                [
                    pltpu.make_async_copy(
                        corr.at[x, lags], sums[i].at[x * quarter : (x + 1) * quarter], corr_sem.at[x, i]
                    )
                ]
            )
    finish(stores)


def spectral(forward, inverse, filters, pieces, crosses, scale):
    hc = len(pieces)
    rows, width = pieces[0].shape
    cols = width // 2
    size = hc * rows
    home = len(crosses) > 0
    hbm = pl.BlockSpec(memory_space=pl.ANY)
    tables = [forward, inverse, *filters]
    arrived = [*pieces, *crosses]
    ins = 3 if home else 2
    parts = 5 if home else 3
    share = jax.ShapeDtypeStruct((size if home else size // 2, cols), jnp.float32)
    sums = [share, share]
    if home:
        shapes = [jax.ShapeDtypeStruct((size, width), jnp.bfloat16)]
        shapes = shapes + [jax.ShapeDtypeStruct((rows, cols), jnp.bfloat16)] * hc
    else:
        shapes = [jax.ShapeDtypeStruct((rows, width), jnp.bfloat16)] * hc
    return pl.pallas_call(
        functools.partial(spectral_kernel, hc, rows, home, scale),
        in_specs=[hbm] * (len(tables) + len(arrived)),
        out_specs=[hbm] * (len(shapes) + len(sums)),
        out_shape=shapes + sums,
        scratch_shapes=[pltpu.VMEM(t.shape, t.dtype) for t in tables]
        + [
            pltpu.VMEM((size, ins * cols), jnp.bfloat16),
            pltpu.VMEM((2 * size, ins * cols), jnp.float32),
            pltpu.VMEM((2 * size, parts * cols), jnp.bfloat16),
            pltpu.VMEM((size, ins * cols), jnp.bfloat16),
            pltpu.VMEM((2 if home else 1, size, cols), jnp.float32),
            pltpu.SemaphoreType.DMA((len(arrived),)),
            pltpu.SemaphoreType.DMA((len(tables),)),
            pltpu.SemaphoreType.DMA((2 * hc,)),
            pltpu.SemaphoreType.DMA((2, 2)),
        ]
        + ([] if home else [pltpu.VMEM((2 * size, cols), jnp.float32)]),
        compiler_params=params(56 if home else 36),
        cost_estimate=cost(4 * size * size * cols * (ins + parts), 8 * size * size + 30 * size * cols),
        name="spectral_home" if home else "spectral_other",
    )(*tables, *arrived)


def final_kernel(hc, count, base, top, aliased, *refs):
    feats_ref, before, grad_ref, taps_ref = refs[:4]
    crosses = ()
    if base > 0:
        pieces, crosses, refs = refs[4 : 4 + hc], refs[4 + hc : 4 + 2 * hc], refs[4 + 2 * hc :]
    else:
        slots = [(lax.axis_index("ctx") % hc) ^ j for j in range(hc)]
        pieces, refs = [refs[4].at[slot] for slot in slots], refs[5:]
    if aliased:
        refs = refs[1:]
    out_ref = last_ref = stage = last = None
    if top:
        first_ref, edge_ref, parts, taps, back, edges, in_sem, small_sem, back_sem, end_sem = refs
        edge = edges.at[1]
    else:
        out_ref, edge_ref, last_ref, parts, taps, back, edge, last, stage = refs[:9]
        in_sem, small_sem, back_sem, end_sem, out_sem = refs[9:]
    me, half, _ = where(hc)
    rows, cols = parts.shape[2:]

    def column(region, j):
        return pl.ds(pl.multiple_of((region * count + (me ^ (base + j))) * cols, cols), cols)

    small = run([pltpu.make_async_copy(taps_ref, taps, small_sem)])
    if top:
        small += run([pltpu.make_async_copy(first_ref, edges.at[0], end_sem.at[1])])
    loads = []
    for j in range(hc):
        copies = [
            pltpu.make_async_copy(source.at[:rows, column(r, j)], parts.at[j, r], in_sem.at[j, r])
            for r, source in enumerate((grad_ref, feats_ref, feats_ref))
        ]
        copies.append(
            pltpu.make_async_copy(pieces[j].at[:rows], back.at[j, :, : 2 * cols], back_sem.at[j])
        )
        if base > 0:
            copies.append(
                pltpu.make_async_copy(crosses[j].at[:rows], back.at[j, :, 2 * cols :], back_sem.at[hc + j])
            )
        loads.append(run(copies))
    finish(small)
    stores = []
    spot = lax.broadcasted_iota(jnp.int32, (rows, 1), 0)
    for j in range(hc):
        finish(loads[j])
        near_taps = [taps[:, column(r, j)] for r in range(3)]
        near_before = [before[:, column(r, j)] for r in range(3)]
        slot = (me ^ (base + j)) % hc
        for strip in strips(cols):

            def unmixed(region, dz):
                edge[slot, region, :, strip] = dz[:2].astype(jnp.bfloat16)
                if top:
                    return
                weights = near_taps[region][:, strip]
                one = jnp.where(spot < rows - 1, pltpu.roll(dz, rows - 1, 0), 0.0)
                two = jnp.where(spot < rows - 2, pltpu.roll(dz, rows - 2, 0), 0.0)
                out = weights[0:1] * dz + weights[1:2] * one + weights[2:3] * two
                last[slot, region, :, strip] = out[rows - 16 :]
                stage[j, region, :, strip] = out.astype(jnp.bfloat16)

            key, value = (
                conv_rows(parts[j, r, :, strip], near_before[r][:, strip], near_taps[r][:, strip])
                for r in (1, 2)
            )
            conv = back[j, :, strip].astype(jnp.float32)
            grad = back[j, :, cols + strip.start : cols + strip.stop].astype(jnp.float32)
            if base > 0:
                extra = back[j, :, 2 * cols + strip.start : 2 * cols + strip.stop].astype(jnp.float32)
                conv = jnp.where(half == 1, conv + extra, conv)
                grad = jnp.where(half == 0, grad + extra, grad)
            unmixed(0, parts[j, 0, :, strip].astype(jnp.float32) * conv)
            unmixed(1, grad * value)
            unmixed(2, grad * key)
        if not top:
            stores += run(
                [
                    pltpu.make_async_copy(stage.at[j, r], out_ref.at[:, column(r, j)], out_sem.at[j, r])
                    for r in range(3)
                ]
            )
    stores += run([pltpu.make_async_copy(edges if top else edge, edge_ref, end_sem.at[0])])
    if not top:
        stores += run([pltpu.make_async_copy(last, last_ref, end_sem.at[1])])
    finish(stores)


def final(feats, before, grad_out, taps, pieces, crosses, so_far, count, base, first=None):
    hc = count // 2
    top = first is not None
    rows = 16 if top else feats.shape[0]
    cols = pieces[0].shape[-1] // 2
    hbm = pl.BlockSpec(memory_space=pl.ANY)
    arrived = [*pieces, *crosses]
    args = [feats, before, grad_out, taps, *arrived]
    aliases = {}
    if top:
        args.append(first)
    if so_far is not None:
        args.append(so_far)
        aliases = {len(args) - 1: 0}
    edge = jax.ShapeDtypeStruct((hc, 3, 2, cols), jnp.bfloat16)
    last = jax.ShapeDtypeStruct((hc, 3, 16, cols), jnp.float32)
    edges = jax.ShapeDtypeStruct((2, *edge.shape), edge.dtype)
    shapes = [edges] if top else [jax.ShapeDtypeStruct(feats.shape, jnp.bfloat16), edge, last]
    scratch = [
        pltpu.VMEM((hc, 3, rows, cols), jnp.bfloat16),
        pltpu.VMEM(taps.shape, taps.dtype),
        pltpu.VMEM((hc, rows, (3 if base > 0 else 2) * cols), jnp.bfloat16),
        pltpu.VMEM(edges.shape if top else edge.shape, edge.dtype),
    ]
    if not top:
        scratch += [
            pltpu.VMEM(last.shape, last.dtype),
            pltpu.VMEM((hc, 3, rows, cols), jnp.bfloat16),
        ]
    scratch += [
        pltpu.SemaphoreType.DMA((hc, 3)),
        pltpu.SemaphoreType.DMA,
        pltpu.SemaphoreType.DMA((2 * hc,)),
        pltpu.SemaphoreType.DMA((2,)),
    ]
    if not top:
        scratch.append(pltpu.SemaphoreType.DMA((hc, 3)))
    name = ("edge_" if top else "final_") + ("other" if base > 0 else "home")
    return pl.pallas_call(
        functools.partial(final_kernel, hc, count, base, top, so_far is not None),
        in_specs=[hbm, pl.BlockSpec(memory_space=pltpu.VMEM)] + [hbm] * (len(args) - 2),
        out_specs=[hbm] * len(shapes),
        scratch_shapes=scratch,
        out_shape=shapes,
        input_output_aliases=aliases,
        compiler_params=params(16 if top or base > 0 else 56),
        cost_estimate=cost(30 * rows * cols * hc, 16 * rows * cols * hc),
        name=name,
    )(*args)


def fix_kernel(hc, taps_ref, edge_ref, lh_ref, lo_ref, *refs):
    own_ref, *sums, _, out_ref, filt_ref, stage, sem = refs
    me, half, _ = where(hc)
    cols = edge_ref.shape[4]
    width = out_ref.shape[1] // 3
    turn = me == hc - 1
    spot = lax.broadcasted_iota(jnp.int32, (16, 1), 0)
    for slot, last in enumerate((lh_ref, lo_ref)):
        mine, swapped = edge_ref.at[slot], edge_ref.at[1 - slot]
        first = jnp.where(half == slot, 0, hc)
        for j in range(hc):
            for region in range(3):
                col = pl.ds(pl.multiple_of(region * width + (first + j) * cols, cols), cols)
                ahead = jnp.where(
                    turn, swapped[j, region].astype(jnp.float32), mine[j, region].astype(jnp.float32)
                )
                one, two = taps_ref[1:2, col], taps_ref[2:3, col]
                add = jnp.where(
                    spot == 14,
                    two * ahead[0:1],
                    jnp.where(spot == 15, one * ahead[0:1] + two * ahead[1:2], 0.0),
                )
                stage[:, col] = (last[j, region] + add).astype(jnp.bfloat16)
    copy = pltpu.make_async_copy(stage, out_ref.at[pl.ds(out_ref.shape[0] - 16, 16)], sem)
    copy.start()
    lags = filt_ref.shape[0]
    total = own_ref[pl.ds(pl.multiple_of((lax.axis_index("dp") // 2) * lags, lags), lags), :]
    for ref in sums:
        total += ref[...].astype(jnp.float32)
    filt_ref[...] = total
    copy.wait()


def fix(taps, edges, last_home, last_other, sums, result):
    hc = edges.shape[1]
    vmem = pl.BlockSpec(memory_space=pltpu.VMEM)
    hbm = pl.BlockSpec(memory_space=pl.ANY)
    return pl.pallas_call(
        functools.partial(fix_kernel, hc),
        in_specs=[vmem] * (4 + len(sums)) + [hbm],
        out_specs=[hbm, vmem],
        out_shape=[
            jax.ShapeDtypeStruct(result.shape, result.dtype),
            jax.ShapeDtypeStruct(sums[-1].shape, jnp.float32),
        ],
        scratch_shapes=[pltpu.VMEM((16, result.shape[1]), jnp.bfloat16), pltpu.SemaphoreType.DMA],
        input_output_aliases={4 + len(sums): 0},
        compiler_params=params(16),
        cost_estimate=cost(16 * 8 * result.shape[1], 128 * result.shape[1]),
        name="fix",
    )(taps, edges, last_home, last_other, *sums, result)


def exchange(pieces, base):
    devices = range(lax.axis_size("ctx"))
    return [
        piece if base + j == 0 else lax.ppermute(piece, "ctx", [(i, i ^ (base + j)) for i in devices])
        for j, piece in enumerate(pieces)
    ]


def within(stacked):
    count = lax.axis_size("ctx")
    groups = [list(range(count // 2)), list(range(count // 2, count))]
    return lax.all_to_all(stacked, "ctx", 0, 0, axis_index_groups=groups, tiled=True)


def half_shards(feats, short_weight, grad_out, filt):
    length, block = filt.shape
    count = lax.axis_size("ctx")
    hc = count // 2
    size = length // 2
    feats, grad_out = feats[0], grad_out[0]
    rows = feats.shape[0]
    high, low = odd_tables(size)
    inverse = np.ascontiguousarray(high.T)
    scale = 1.0 / (math.sqrt(length) * size)
    me = lax.axis_index("ctx")
    dp = lax.axis_index("dp")
    core, x = dp % 2, dp // 2
    quarter = length // 4
    tie = lax.optimization_barrier
    cores = [(i, i ^ 1) for i in range(4)]

    late, source = tie((feats[rows - 2 :], filt))
    before = from_behind(late, "ctx", 1)
    share = size // 2
    part = (lax.dynamic_slice_in_dim(source, core * share, share, 0) * scale).astype(jnp.bfloat16)
    part = lax.ppermute(part, "ctx", [(i, i ^ hc) for i in range(count)])
    gated = gate(feats, before, short_weight, grad_out, count, block, hc)

    ready, gated = tie((before, gated))
    other_pieces, across = exchange(gated[:hc], 0), gated[hc:]
    sent = exchange(across[:1], hc)
    outs = prepare(filt, high, low, feats, ready, short_weight, grad_out, scale, count)
    outs, other_pieces, sent, across, part = tie((outs, other_pieces, sent, across, part))
    near, far = outs[hc:]

    home_pieces = exchange(outs[:hc], 0)
    rest = lax.ppermute(part, "dp", cores)
    sent = list(sent) + exchange(across[1:3], hc + 1)
    outs = spectral(high, inverse, (low, part, rest), other_pieces, (), scale)
    far, outs, home_pieces, sent, across = tie((far, outs, home_pieces, sent, across))

    other_back = exchange(outs[:hc], 0)
    sent = list(sent) + exchange(across[3:], hc + 3)
    send, keep = outs[hc:]
    summed = keep + lax.ppermute(send, "dp", cores)
    crossed = lax.ppermute(summed.astype(jnp.bfloat16), "ctx", [(i, i ^ hc) for i in range(count)])
    outs = spectral(high, inverse, (near, far), home_pieces, sent, scale)
    outs, other_back, crossed = tie((outs, other_back, crossed))

    home_back = within(outs[0].reshape(hc, rows, 2 * block))
    cross_back = exchange(outs[1 : 1 + hc], hc)
    send, keep = outs[1 + hc :]
    came = lax.ppermute(send, "dp", cores)
    result, edge_home, last_home = final(
        feats, before, grad_out, short_weight, [home_back], (), None, count, 0
    )
    keep, came, crossed, edge_home = tie((keep, came, crossed, edge_home))
    crossed = jnp.concatenate([crossed.astype(jnp.float32), jnp.zeros((quarter, block), jnp.float32)], axis=0)
    home_sum = keep + came + crossed
    there = lax.dynamic_slice_in_dim(home_sum, (1 - x) * quarter, quarter, 0).astype(jnp.bfloat16)
    cross_back, edge_home, there = tie((cross_back, edge_home, there))

    (edges,) = final(
        feats, before, grad_out, short_weight, other_back, cross_back, None, count, hc, edge_home
    )
    edges, there = tie((edges, there))
    edges = from_behind(edges, "ctx", -1)
    there = lax.ppermute(there, "dp", [(i, i ^ 2) for i in range(4)])
    result, _, last_other = final(
        feats, before, grad_out, short_weight, other_back, cross_back, result, count, hc
    )
    result, filt_out = fix(short_weight, edges, last_home, last_other, [home_sum, there], result)
    return (result[None], filt_out)


full_precision = lax.Precision.HIGHEST
split_precision = lax.Precision.HIGH


def from_behind(block, axis, distance):
    devices = range(lax.axis_size(axis))
    route = [(i - distance, i) for i in devices if i - distance in devices]
    return lax.ppermute(block, axis, route)


def angle_table(count_rows, count_cols, period):
    product = (
        jnp.arange(count_rows, dtype=jnp.int32)[:, None]
        * jnp.arange(count_cols, dtype=jnp.int32)[None, :]
        % period
    )
    theta = product.astype(jnp.float32) * (2.0 * math.pi / period)
    return (jnp.cos(theta), jnp.sin(theta))


def make_tables(length):
    total = 2 * length
    outer = 128
    inner = total // outer
    half = outer // 2
    freq = jnp.arange(outer, dtype=jnp.int32)[:, None, None]
    spot = (
        jnp.arange(half, dtype=jnp.int32)[None, :, None] * inner
        + jnp.arange(inner, dtype=jnp.int32)[None, None, :]
    )
    theta = (freq * spot % total).astype(jnp.float32) * (2.0 * math.pi / total)
    first = jnp.stack([jnp.cos(theta), -jnp.sin(theta)], axis=0)
    cos_b, sin_b = angle_table(inner, inner, inner)
    forward_b = jnp.stack(
        [jnp.stack([cos_b, -sin_b], axis=1), jnp.stack([sin_b, cos_b], axis=1)], axis=0
    )
    inverse_b = jnp.stack(
        [jnp.stack([cos_b, sin_b], axis=1), jnp.stack([-sin_b, cos_b], axis=1)], axis=0
    )
    return (first, forward_b, inverse_b)


def finish_forward(partial_spec, tables, accuracy):
    return jnp.einsum("sckrb,rbxq->sckxq", partial_spec, tables[1], precision=accuracy)


def data_forward(signal, tables, accuracy):
    first = tables[0]
    inner = first.shape[3]
    seqs, chans, length = signal.shape
    grid = signal.reshape(seqs, chans, length // inner, inner)
    partial_spec = jnp.einsum("rknb,scnb->sckrb", first, grid, precision=accuracy)
    return finish_forward(partial_spec, tables, accuracy)


def filter_forward(columns, tables):
    first = tables[0]
    inner = first.shape[3]
    length, chans = columns.shape
    grid = columns.reshape(length // inner, inner, chans)
    partial_spec = jnp.einsum("rknb,nbc->ckrb", first, grid, precision=full_precision)[None]
    return finish_forward(partial_spec, tables, full_precision)


def start_inverse(spectrum, tables):
    return jnp.einsum("sckxq,xqrb->sckrb", spectrum, tables[2], precision=full_precision)


def data_inverse(spectrum, tables, length):
    partial_sig = start_inverse(spectrum, tables)
    signal = jnp.einsum("sckrb,rknb->scnb", partial_sig, tables[0], precision=full_precision)
    return signal.reshape(signal.shape[0], signal.shape[1], length) / (2.0 * length)


def filter_inverse(spectrum, tables, length):
    partial_sig = start_inverse(spectrum, tables)[0]
    signal = jnp.einsum("ckrb,rknb->nbc", partial_sig, tables[0], precision=full_precision)
    return signal.reshape(length, signal.shape[2]) / (2.0 * length)


def long_spectral(gated_sig, grad_sig, filter_cols, tables, length):
    g_spec = data_forward(gated_sig, tables, split_precision)
    d_spec = data_forward(grad_sig, tables, split_precision)
    h_spec = filter_forward(filter_cols, tables)
    g_re, g_im = (g_spec[:, :, :, 0], g_spec[:, :, :, 1])
    d_re, d_im = (d_spec[:, :, :, 0], d_spec[:, :, :, 1])
    h_re, h_im = (h_spec[:, :, :, 0], h_spec[:, :, :, 1])
    conv_spec = jnp.stack([h_re * g_re - h_im * g_im, h_re * g_im + h_im * g_re], axis=3)
    grad_spec = jnp.stack([h_re * d_re + h_im * d_im, h_re * d_im - h_im * d_re], axis=3)
    prod_re = jnp.sum(g_re * d_re + g_im * d_im, axis=0, keepdims=True)
    prod_im = jnp.sum(g_re * d_im - g_im * d_re, axis=0, keepdims=True)
    prod_spec = jnp.stack([prod_re, prod_im], axis=3)
    conv_out = data_inverse(conv_spec, tables, length)
    gated_grad = data_inverse(grad_spec, tables, length)
    filt_grad = filter_inverse(prod_spec, tables, length)
    return (conv_out, gated_grad, filt_grad)


def long_shards(feats, short_weight, grad_out, filt):
    rows = feats.shape[1]
    width = feats.shape[2] // 3
    length = filt.shape[0]
    block = filt.shape[1]
    ctx_count = lax.axis_size("ctx")
    replicas = lax.axis_size("dp")
    scale_inv = 1.0 / math.sqrt(length)
    tables = make_tables(length)
    prior = from_behind(feats[:, rows - 2 :, :], "ctx", 1)
    extended = jnp.concatenate([prior, feats], axis=1).astype(jnp.float32)
    mixed = (
        short_weight[0] * extended[:, 2:]
        + short_weight[1] * extended[:, 1 : rows + 1]
        + short_weight[2] * extended[:, :rows]
    )
    query_rows = mixed[:, :, :width]
    key_rows = mixed[:, :, width : 2 * width]
    value_rows = mixed[:, :, 2 * width :]
    gated = (key_rows * value_rows).astype(jnp.bfloat16)
    out_grad = grad_out.astype(jnp.float32)
    conv_grad = (out_grad * query_rows).astype(jnp.bfloat16)
    narrow = block // replicas

    def spread(array):
        return array[0].reshape(rows, ctx_count, replicas, narrow).transpose(1, 2, 3, 0)[:, :, None]

    wide_gated, wide_grad = (
        lax.all_to_all(
            lax.all_to_all(spread(gated), "dp", split_axis=1, concat_axis=2, tiled=True),
            "ctx",
            split_axis=0,
            concat_axis=4,
            tiled=True,
        ),
        lax.all_to_all(
            lax.all_to_all(spread(conv_grad), "dp", split_axis=1, concat_axis=2, tiled=True),
            "ctx",
            split_axis=0,
            concat_axis=4,
            tiled=True,
        ),
    )
    wide_gated = wide_gated.reshape(replicas, narrow, length)
    wide_grad = wide_grad.reshape(replicas, narrow, length)
    offset = lax.axis_index("dp") * narrow
    filt_cols = lax.dynamic_slice_in_dim(filt, offset, narrow, 1)
    conv_out, gated_grad, filt_grad = long_spectral(
        wide_gated, wide_grad, filt_cols * scale_inv, tables, length
    )
    back_conv, back_grad = (
        lax.all_to_all(
            lax.all_to_all(
                conv_out.astype(jnp.bfloat16)[None, None],
                "dp",
                split_axis=2,
                concat_axis=1,
                tiled=True,
            ),
            "ctx",
            split_axis=4,
            concat_axis=0,
            tiled=True,
        ),
        lax.all_to_all(
            lax.all_to_all(
                gated_grad.astype(jnp.bfloat16)[None, None],
                "dp",
                split_axis=2,
                concat_axis=1,
                tiled=True,
            ),
            "ctx",
            split_axis=4,
            concat_axis=0,
            tiled=True,
        ),
    )

    def gather_positions(array):
        return (
            array.reshape(ctx_count, replicas, narrow, rows)
            .transpose(3, 0, 1, 2)
            .reshape(1, rows, width)
        )

    conv_rows = gather_positions(back_conv)
    grad_rows = gather_positions(back_grad)
    parts = filt_grad.reshape(replicas, length // replicas, 1, narrow)
    owned = lax.all_to_all(parts, "dp", split_axis=0, concat_axis=2, tiled=True)
    filt_out = owned.reshape(length // replicas, block) * scale_inv
    grad_query = out_grad * conv_rows.astype(jnp.float32)
    grad_key = grad_rows.astype(jnp.float32) * value_rows
    grad_value = grad_rows.astype(jnp.float32) * key_rows
    grad_mixed = jnp.concatenate([grad_query, grad_key, grad_value], axis=2)
    following = from_behind(grad_mixed[:, :2, :].astype(jnp.bfloat16), "ctx", -1).astype(
        jnp.float32
    )
    ahead = jnp.concatenate([grad_mixed, following], axis=1)
    grad_in = (
        short_weight[0] * grad_mixed
        + short_weight[1] * ahead[:, 1 : rows + 1]
        + short_weight[2] * ahead[:, 2 : rows + 2]
    )
    return (grad_in.astype(jnp.bfloat16), filt_out)


def shards(feats, short_weight, grad_out, filt):
    count = lax.axis_size("ctx")
    length, block = filt.shape
    fits = (
        length <= 1024
        and length % (4 * STEP) == 0
        and count > 1
        and count & (count - 1) == 0
        and feats.shape[1] % 128 == 0
        and block % 128 == 0
        and lax.axis_size("dp") == 4
    )
    plan = half_shards if fits else long_shards
    return plan(feats, short_weight, grad_out, filt)


def solution(mesh):
    return jax.shard_map(
        shards,
        mesh=mesh,
        in_specs=(P("dp", "ctx", None), P(), P("dp", "ctx", None), P(None, "ctx")),
        out_specs=(P("dp", "ctx", None), P("dp", "ctx")),
        check_vma=False,
    )
```

```python
import functools
import math

import jax
import jax.numpy as jnp
import numpy as np
from jax import lax
from jax.experimental import pallas as pl
from jax.experimental.pallas import tpu as pltpu
from jax.sharding import PartitionSpec as P

STEP = 128
STRIP = 128


def params(mebibytes):
    return pltpu.CompilerParams(vmem_limit_bytes=mebibytes * 1024 * 1024)


def cost(flops, moved):
    return pl.CostEstimate(flops=flops, bytes_accessed=moved, transcendentals=0)


def odd_tables(size):
    freq = 2 * np.arange(size, dtype=np.int64)[:, None] + 1
    spot = np.arange(size, dtype=np.int64)[None, :]
    theta = (freq * spot % (4 * size)).astype(np.float64) * (2.0 * math.pi / (4 * size))
    full = np.concatenate([np.cos(theta), -np.sin(theta)], axis=0).astype(np.float32)
    high = full.astype(jnp.bfloat16)
    low = (full - high.astype(np.float32)).astype(jnp.bfloat16)
    return high, low


def dot(a, b):
    return jnp.dot(a, b, preferred_element_type=jnp.float32)


def run(copies):
    for copy in copies:
        copy.start()
    return copies


def finish(copies):
    for copy in copies:
        copy.wait()


def behind(values, before):
    spot = lax.broadcasted_iota(jnp.int32, (values.shape[0], 1), 0)
    one = jnp.where(spot == 0, before[1:2], pltpu.roll(values, 1, 0))
    two = jnp.where(spot == 0, before[0:1], jnp.where(spot == 1, before[1:2], pltpu.roll(values, 2, 0)))
    return one, two


def conv_rows(values, before, taps):
    values = values.astype(jnp.float32)
    one, two = behind(values, before.astype(jnp.float32))
    return taps[0:1] * values + taps[1:2] * one + taps[2:3] * two


def where(hc):
    me = lax.axis_index("ctx")
    return me, me // hc, lax.axis_index("dp") % 2


def strips(cols):
    return [slice(c, c + STRIP) for c in range(0, cols, STRIP)]


def gate_kernel(hc, count, base, feats_ref, before, taps_ref, grad_ref, *refs):
    crossing = base > 0
    outs, refs = refs[: hc * (2 if crossing else 1)], refs[hc * (2 if crossing else 1) :]
    parts, taps, stage, in_sem, small_sem, out_sem = refs
    rows, cols = parts.shape[2:]
    me, half, core = where(hc)

    def column(region, j):
        return pl.ds(pl.multiple_of((region * count + (me ^ (base + j))) * cols, cols), cols)

    small = run([pltpu.make_async_copy(taps_ref, taps, small_sem)])
    loads = [
        run(
            [
                pltpu.make_async_copy(feats_ref.at[:, column(r, j)], parts.at[j, r], in_sem.at[j, r])
                for r in range(3)
            ]
            + [pltpu.make_async_copy(grad_ref.at[:, column(0, j)], parts.at[j, 3], in_sem.at[j, 3])]
        )
        for j in range(hc)
    ]
    finish(small)
    stores = []
    for j in range(hc):
        finish(loads[j])
        mine = [(before[:, column(r, j)], taps[:, column(r, j)]) for r in range(3)]
        for strip in strips(cols):
            query, key, value = (
                conv_rows(parts[j, r, :, strip], mine[r][0][:, strip], mine[r][1][:, strip])
                for r in range(3)
            )
            stage[j, :, strip] = (key * value).astype(jnp.bfloat16)
            stage[j, :, cols + strip.start : cols + strip.stop] = (
                parts[j, 3, :, strip].astype(jnp.float32) * query
            ).astype(jnp.bfloat16)
        stores += run([pltpu.make_async_copy(stage.at[j], outs[j], out_sem.at[j])])
        if crossing:
            crossed = stage.at[j, :, pl.ds(pl.multiple_of(half * cols, cols), cols)]
            stores += run([pltpu.make_async_copy(crossed, outs[hc + j], out_sem.at[hc + j])])
    finish(stores)


def gate(feats, before, taps, grad_out, count, cols, base):
    rows = feats.shape[0]
    hc = count // 2
    shapes = [jax.ShapeDtypeStruct((rows, 2 * cols), jnp.bfloat16)] * hc
    shapes = shapes + [jax.ShapeDtypeStruct((rows, cols), jnp.bfloat16)] * hc
    hbm = pl.BlockSpec(memory_space=pl.ANY)
    return pl.pallas_call(
        functools.partial(gate_kernel, hc, count, base),
        in_specs=[hbm, pl.BlockSpec(memory_space=pltpu.VMEM), hbm, hbm],
        out_specs=[hbm] * len(shapes),
        out_shape=shapes,
        scratch_shapes=[
            pltpu.VMEM((hc, 4, rows, cols), jnp.bfloat16),
            pltpu.VMEM(taps.shape, taps.dtype),
            pltpu.VMEM((hc, rows, 2 * cols), jnp.bfloat16),
            pltpu.SemaphoreType.DMA((hc, 4)),
            pltpu.SemaphoreType.DMA,
            pltpu.SemaphoreType.DMA((len(shapes),)),
        ],
        compiler_params=params(56),
        cost_estimate=cost(20 * rows * cols * hc, 12 * rows * cols * hc),
        name="gate_other",
    )(feats, before, taps, grad_out)


def signs(first, rows):
    odd = (lax.broadcasted_iota(jnp.int32, (rows, 1), 0) + first) % 2
    return 1.0 - 2.0 * odd.astype(jnp.float32)


def filter_home_kernel(scale, filt_ref, high_ref, low_ref, near_ref, far_ref):
    size = filt_ref.shape[0] // 2

    def spectrum(part):
        now = part * scale
        high = now.astype(jnp.bfloat16)
        low = (now - high.astype(jnp.float32)).astype(jnp.bfloat16)
        return dot(high_ref[...], high) + dot(high_ref[...], low) + dot(low_ref[...], high)

    near = spectrum(filt_ref[:size, :])
    far = spectrum(filt_ref[size:, :])
    near_ref[...] = near
    sign = signs(0, size)
    far_ref[:size, :] = far[:size] - sign * near[size:]
    far_ref[size:, :] = far[size:] + sign * near[:size]


def prepare_kernel(hc, count, scale, *refs):
    filters, refs = refs[:3], refs[3:]
    gate_in, refs = refs[:4], refs[4:]
    gate_out, refs = refs[:hc], refs[hc:]
    gate_kernel(hc, count, 0, *gate_in, *gate_out, *refs[2:])
    filter_home_kernel(scale, *filters, *refs[:2])


def prepare(filt, high, low, feats, before, taps, grad_out, scale, count):
    rows = feats.shape[0]
    length, cols = filt.shape
    hc = count // 2
    shapes = [jax.ShapeDtypeStruct((rows, 2 * cols), jnp.bfloat16)] * hc
    spectra = [jax.ShapeDtypeStruct((length, cols), jnp.float32)] * 2
    hbm = pl.BlockSpec(memory_space=pl.ANY)
    vmem = pl.BlockSpec(memory_space=pltpu.VMEM)
    return pl.pallas_call(
        functools.partial(prepare_kernel, hc, count, scale),
        in_specs=[vmem] * 3 + [hbm, vmem, hbm, hbm],
        out_specs=[hbm] * hc + [vmem] * 2,
        out_shape=shapes + spectra,
        scratch_shapes=[
            pltpu.VMEM((hc, 4, rows, cols), jnp.bfloat16),
            pltpu.VMEM(taps.shape, taps.dtype),
            pltpu.VMEM((hc, rows, 2 * cols), jnp.bfloat16),
            pltpu.SemaphoreType.DMA((hc, 4)),
            pltpu.SemaphoreType.DMA,
            pltpu.SemaphoreType.DMA((len(shapes),)),
        ],
        compiler_params=params(56),
        cost_estimate=cost(8 * length * length * cols, 20 * length * cols),
        name="prepare",
    )(filt, high, low, feats, before, taps, grad_out)


def times(a_re, a_im, b_re, b_im):
    return a_re * b_re - a_im * b_im, a_re * b_im + a_im * b_re


def conj_times(a_re, a_im, b_re, b_im):
    return a_re * b_re + a_im * b_im, a_re * b_im - a_im * b_re


def spectral_kernel(hc, rows, home, scale, *refs):
    tables, refs = refs[: 4 if home else 5], refs[4 if home else 5 :]
    pieces, refs = refs[:hc], refs[hc:]
    crosses = ()
    if home:
        crosses, refs = refs[:hc], refs[hc:]
    outs, refs = refs[: 1 if home else hc], refs[1 if home else hc :]
    cross_outs = ()
    if home:
        cross_outs, refs = refs[:hc], refs[hc:]
    sums, refs = refs[:2], refs[2:]
    held, refs = refs[: len(tables)], refs[len(tables) :]
    data, spec, prod, res, corr, piece_sem, table_sem, out_sem, corr_sem = refs[:9]
    forward_ref, inverse_ref = held[:2]
    near_ref, far_ref = (held[2], held[3]) if home else (refs[-1], None)
    me, half, core = where(hc)
    spot = me % hc
    size = data.shape[0]
    cols = res.shape[1] // (3 if home else 2)

    def place(j):
        return pl.ds(pl.multiple_of((spot ^ j) * rows, rows), rows)

    def load(i):
        return run([pltpu.make_async_copy(tables[i], held[i], table_sem.at[i])])

    forward_copy = load(0)
    piece_copies = run(
        [pltpu.make_async_copy(pieces[j], data.at[place(j), : 2 * cols], piece_sem.at[j]) for j in range(hc)]
    )
    cross_copies = run(
        [
            pltpu.make_async_copy(crosses[j], data.at[place(j), 2 * cols :], piece_sem.at[hc + j])
            for j in range(len(crosses))
        ]
    )
    filter_copies = [copy for i in range(2, len(tables)) for copy in load(i)]
    inverse_copy = load(1)
    finish(forward_copy)
    finish(piece_copies)
    for part in range(data.shape[1] // cols):
        if part == 2:
            finish(cross_copies)
        here = slice(part * cols, (part + 1) * cols)
        spec[:, here] = dot(forward_ref[...], data[:, here])
    finish(filter_copies)
    if not home:
        low_ref, mine_ref, theirs_ref = held[2:]
        share = mine_ref.shape[0]
        mine = pl.ds(pl.multiple_of(core * share, share), share)
        theirs = pl.ds(pl.multiple_of((1 - core) * share, share), share)
        near_ref[...] = (
            dot(forward_ref[:, mine], mine_ref[...])
            + dot(forward_ref[:, theirs], theirs_ref[...])
            + dot(low_ref[:, mine], mine_ref[...])
            + dot(low_ref[:, theirs], theirs_ref[...])
        )

    def products(side):
        def body(i, carry):
            low = pl.ds(pl.multiple_of(i * STEP, STEP), STEP)
            high = pl.ds(pl.multiple_of(size + i * STEP, STEP), STEP)

            def get(part):
                here = slice(part * cols, (part + 1) * cols)
                return spec[low, here], spec[high, here]

            def put(part, value):
                here = slice(part * cols, (part + 1) * cols)
                prod[low, here] = value[0].astype(jnp.bfloat16)
                prod[high, here] = value[1].astype(jnp.bfloat16)

            g, d = get(0), get(1)
            h = near_ref[low, :], near_ref[high, :]
            conv = times(*h, *g)
            grad = conj_times(*h, *d)
            corr = conj_times(*g, *d)
            if home:
                f = far_ref[low, :], far_ref[high, :]
                gx, dx = (g, get(2)) if side == 0 else (get(2), d)
                far_conv = times(*f, *gx)
                far_grad = conj_times(*f, *dx)
                if side == 0:
                    grad = (grad[0] + far_grad[0], grad[1] + far_grad[1])
                else:
                    conv = (conv[0] + far_conv[0], conv[1] + far_conv[1])
                put(2, far_conv if side == 0 else far_grad)
                far_corr = conj_times(*gx, *dx)
                sign = signs(0, STEP)
                corr = (corr[0] + sign * far_corr[1], corr[1] - sign * far_corr[0])
                put(4, far_corr)
                put(3, corr)
            else:
                put(2, corr)
            put(0, conv)
            put(1, grad)
            return carry

        lax.fori_loop(0, size // STEP, body, 0)

    if home:

        @pl.when(half == 0)
        def _():
            products(0)

        @pl.when(half == 1)
        def _():
            products(1)

    else:
        products(0)

    def back(part):
        return dot(inverse_ref[...], prod[:, part * cols : (part + 1) * cols])

    finish(inverse_copy)
    res[:, :cols] = back(0).astype(jnp.bfloat16)
    res[:, cols : 2 * cols] = back(1).astype(jnp.bfloat16)
    if home:
        stores = run([pltpu.make_async_copy(res.at[:, : 2 * cols], outs[0], out_sem.at[0])])
    else:
        stores = run(
            [pltpu.make_async_copy(res.at[place(j), : 2 * cols], outs[j], out_sem.at[j]) for j in range(hc)]
        )
    if home:
        res[:, 2 * cols :] = back(2).astype(jnp.bfloat16)
        stores += run(
            [
                pltpu.make_async_copy(res.at[place(j), 2 * cols :], cross_outs[j], out_sem.at[hc + j])
                for j in range(hc)
            ]
        )
    quarter = size // 2
    for x in range(2 if home else 1):
        corr[x] = back((3 if home else 2) + x) * scale
        for i, which in enumerate((1 - core, core)):
            lags = pl.ds(pl.multiple_of(which * quarter, quarter), quarter)
            stores += run(
                [
                    pltpu.make_async_copy(
                        corr.at[x, lags], sums[i].at[x * quarter : (x + 1) * quarter], corr_sem.at[x, i]
                    )
                ]
            )
    finish(stores)


def spectral(forward, inverse, filters, pieces, crosses, scale):
    hc = len(pieces)
    rows, width = pieces[0].shape
    cols = width // 2
    size = hc * rows
    home = len(crosses) > 0
    hbm = pl.BlockSpec(memory_space=pl.ANY)
    tables = [forward, inverse, *filters]
    arrived = [*pieces, *crosses]
    ins = 3 if home else 2
    parts = 5 if home else 3
    share = jax.ShapeDtypeStruct((size if home else size // 2, cols), jnp.float32)
    sums = [share, share]
    if home:
        shapes = [jax.ShapeDtypeStruct((size, width), jnp.bfloat16)]
        shapes = shapes + [jax.ShapeDtypeStruct((rows, cols), jnp.bfloat16)] * hc
    else:
        shapes = [jax.ShapeDtypeStruct((rows, width), jnp.bfloat16)] * hc
    return pl.pallas_call(
        functools.partial(spectral_kernel, hc, rows, home, scale),
        in_specs=[hbm] * (len(tables) + len(arrived)),
        out_specs=[hbm] * (len(shapes) + len(sums)),
        out_shape=shapes + sums,
        scratch_shapes=[pltpu.VMEM(t.shape, t.dtype) for t in tables]
        + [
            pltpu.VMEM((size, ins * cols), jnp.bfloat16),
            pltpu.VMEM((2 * size, ins * cols), jnp.float32),
            pltpu.VMEM((2 * size, parts * cols), jnp.bfloat16),
            pltpu.VMEM((size, ins * cols), jnp.bfloat16),
            pltpu.VMEM((2 if home else 1, size, cols), jnp.float32),
            pltpu.SemaphoreType.DMA((len(arrived),)),
            pltpu.SemaphoreType.DMA((len(tables),)),
            pltpu.SemaphoreType.DMA((2 * hc,)),
            pltpu.SemaphoreType.DMA((2, 2)),
        ]
        + ([] if home else [pltpu.VMEM((2 * size, cols), jnp.float32)]),
        compiler_params=params(56 if home else 36),
        cost_estimate=cost(4 * size * size * cols * (ins + parts), 8 * size * size + 30 * size * cols),
        name="spectral_home" if home else "spectral_other",
    )(*tables, *arrived)


def final_kernel(hc, count, base, top, aliased, *refs):
    feats_ref, before, grad_ref, taps_ref = refs[:4]
    crosses = ()
    if base > 0:
        pieces, crosses, refs = refs[4 : 4 + hc], refs[4 + hc : 4 + 2 * hc], refs[4 + 2 * hc :]
    else:
        slots = [(lax.axis_index("ctx") % hc) ^ j for j in range(hc)]
        pieces, refs = [refs[4].at[slot] for slot in slots], refs[5:]
    if aliased:
        refs = refs[1:]
    out_ref = last_ref = stage = last = None
    if top:
        first_ref, edge_ref, parts, taps, back, edges, in_sem, small_sem, back_sem, end_sem = refs
        edge = edges.at[1]
    else:
        out_ref, edge_ref, last_ref, parts, taps, back, edge, last, stage = refs[:9]
        in_sem, small_sem, back_sem, end_sem, out_sem = refs[9:]
    me, half, _ = where(hc)
    rows, cols = parts.shape[2:]

    def column(region, j):
        return pl.ds(pl.multiple_of((region * count + (me ^ (base + j))) * cols, cols), cols)

    small = run([pltpu.make_async_copy(taps_ref, taps, small_sem)])
    if top:
        small += run([pltpu.make_async_copy(first_ref, edges.at[0], end_sem.at[1])])
    loads = []
    for j in range(hc):
        copies = [
            pltpu.make_async_copy(source.at[:rows, column(r, j)], parts.at[j, r], in_sem.at[j, r])
            for r, source in enumerate((grad_ref, feats_ref, feats_ref))
        ]
        copies.append(
            pltpu.make_async_copy(pieces[j].at[:rows], back.at[j, :, : 2 * cols], back_sem.at[j])
        )
        if base > 0:
            copies.append(
                pltpu.make_async_copy(crosses[j].at[:rows], back.at[j, :, 2 * cols :], back_sem.at[hc + j])
            )
        loads.append(run(copies))
    finish(small)
    stores = []
    spot = lax.broadcasted_iota(jnp.int32, (rows, 1), 0)
    for j in range(hc):
        finish(loads[j])
        near_taps = [taps[:, column(r, j)] for r in range(3)]
        near_before = [before[:, column(r, j)] for r in range(3)]
        slot = (me ^ (base + j)) % hc
        for strip in strips(cols):

            def unmixed(region, dz):
                edge[slot, region, :, strip] = dz[:2].astype(jnp.bfloat16)
                if top:
                    return
                weights = near_taps[region][:, strip]
                one = jnp.where(spot < rows - 1, pltpu.roll(dz, rows - 1, 0), 0.0)
                two = jnp.where(spot < rows - 2, pltpu.roll(dz, rows - 2, 0), 0.0)
                out = weights[0:1] * dz + weights[1:2] * one + weights[2:3] * two
                last[slot, region, :, strip] = out[rows - 16 :]
                stage[j, region, :, strip] = out.astype(jnp.bfloat16)

            key, value = (
                conv_rows(parts[j, r, :, strip], near_before[r][:, strip], near_taps[r][:, strip])
                for r in (1, 2)
            )
            conv = back[j, :, strip].astype(jnp.float32)
            grad = back[j, :, cols + strip.start : cols + strip.stop].astype(jnp.float32)
            if base > 0:
                extra = back[j, :, 2 * cols + strip.start : 2 * cols + strip.stop].astype(jnp.float32)
                conv = jnp.where(half == 1, conv + extra, conv)
                grad = jnp.where(half == 0, grad + extra, grad)
            unmixed(0, parts[j, 0, :, strip].astype(jnp.float32) * conv)
            unmixed(1, grad * value)
            unmixed(2, grad * key)
        if not top:
            stores += run(
                [
                    pltpu.make_async_copy(stage.at[j, r], out_ref.at[:, column(r, j)], out_sem.at[j, r])
                    for r in range(3)
                ]
            )
    stores += run([pltpu.make_async_copy(edges if top else edge, edge_ref, end_sem.at[0])])
    if not top:
        stores += run([pltpu.make_async_copy(last, last_ref, end_sem.at[1])])
    finish(stores)


def final(feats, before, grad_out, taps, pieces, crosses, so_far, count, base, first=None):
    hc = count // 2
    top = first is not None
    rows = 16 if top else feats.shape[0]
    cols = pieces[0].shape[-1] // 2
    hbm = pl.BlockSpec(memory_space=pl.ANY)
    arrived = [*pieces, *crosses]
    args = [feats, before, grad_out, taps, *arrived]
    aliases = {}
    if top:
        args.append(first)
    if so_far is not None:
        args.append(so_far)
        aliases = {len(args) - 1: 0}
    edge = jax.ShapeDtypeStruct((hc, 3, 2, cols), jnp.bfloat16)
    last = jax.ShapeDtypeStruct((hc, 3, 16, cols), jnp.float32)
    edges = jax.ShapeDtypeStruct((2, *edge.shape), edge.dtype)
    shapes = [edges] if top else [jax.ShapeDtypeStruct(feats.shape, jnp.bfloat16), edge, last]
    scratch = [
        pltpu.VMEM((hc, 3, rows, cols), jnp.bfloat16),
        pltpu.VMEM(taps.shape, taps.dtype),
        pltpu.VMEM((hc, rows, (3 if base > 0 else 2) * cols), jnp.bfloat16),
        pltpu.VMEM(edges.shape if top else edge.shape, edge.dtype),
    ]
    if not top:
        scratch += [
            pltpu.VMEM(last.shape, last.dtype),
            pltpu.VMEM((hc, 3, rows, cols), jnp.bfloat16),
        ]
    scratch += [
        pltpu.SemaphoreType.DMA((hc, 3)),
        pltpu.SemaphoreType.DMA,
        pltpu.SemaphoreType.DMA((2 * hc,)),
        pltpu.SemaphoreType.DMA((2,)),
    ]
    if not top:
        scratch.append(pltpu.SemaphoreType.DMA((hc, 3)))
    name = ("edge_" if top else "final_") + ("other" if base > 0 else "home")
    return pl.pallas_call(
        functools.partial(final_kernel, hc, count, base, top, so_far is not None),
        in_specs=[hbm, pl.BlockSpec(memory_space=pltpu.VMEM)] + [hbm] * (len(args) - 2),
        out_specs=[hbm] * len(shapes),
        scratch_shapes=scratch,
        out_shape=shapes,
        input_output_aliases=aliases,
        compiler_params=params(16 if top or base > 0 else 56),
        cost_estimate=cost(30 * rows * cols * hc, 16 * rows * cols * hc),
        name=name,
    )(*args)


def fix_kernel(hc, taps_ref, edge_ref, lh_ref, lo_ref, *refs):
    own_ref, *sums, _, out_ref, filt_ref, stage, sem = refs
    me, half, _ = where(hc)
    cols = edge_ref.shape[4]
    width = out_ref.shape[1] // 3
    turn = me == hc - 1
    spot = lax.broadcasted_iota(jnp.int32, (16, 1), 0)
    for slot, last in enumerate((lh_ref, lo_ref)):
        mine, swapped = edge_ref.at[slot], edge_ref.at[1 - slot]
        first = jnp.where(half == slot, 0, hc)
        for j in range(hc):
            for region in range(3):
                col = pl.ds(pl.multiple_of(region * width + (first + j) * cols, cols), cols)
                ahead = jnp.where(
                    turn, swapped[j, region].astype(jnp.float32), mine[j, region].astype(jnp.float32)
                )
                one, two = taps_ref[1:2, col], taps_ref[2:3, col]
                add = jnp.where(
                    spot == 14,
                    two * ahead[0:1],
                    jnp.where(spot == 15, one * ahead[0:1] + two * ahead[1:2], 0.0),
                )
                stage[:, col] = (last[j, region] + add).astype(jnp.bfloat16)
    copy = pltpu.make_async_copy(stage, out_ref.at[pl.ds(out_ref.shape[0] - 16, 16)], sem)
    copy.start()
    lags = filt_ref.shape[0]
    total = own_ref[pl.ds(pl.multiple_of((lax.axis_index("dp") // 2) * lags, lags), lags), :]
    for ref in sums:
        total += ref[...].astype(jnp.float32)
    filt_ref[...] = total
    copy.wait()


def fix(taps, edges, last_home, last_other, sums, result):
    hc = edges.shape[1]
    vmem = pl.BlockSpec(memory_space=pltpu.VMEM)
    hbm = pl.BlockSpec(memory_space=pl.ANY)
    return pl.pallas_call(
        functools.partial(fix_kernel, hc),
        in_specs=[vmem] * (4 + len(sums)) + [hbm],
        out_specs=[hbm, vmem],
        out_shape=[
            jax.ShapeDtypeStruct(result.shape, result.dtype),
            jax.ShapeDtypeStruct(sums[-1].shape, jnp.float32),
        ],
        scratch_shapes=[pltpu.VMEM((16, result.shape[1]), jnp.bfloat16), pltpu.SemaphoreType.DMA],
        input_output_aliases={4 + len(sums): 0},
        compiler_params=params(16),
        cost_estimate=cost(16 * 8 * result.shape[1], 128 * result.shape[1]),
        name="fix",
    )(taps, edges, last_home, last_other, *sums, result)


def exchange(pieces, base):
    devices = range(lax.axis_size("ctx"))
    return [
        piece if base + j == 0 else lax.ppermute(piece, "ctx", [(i, i ^ (base + j)) for i in devices])
        for j, piece in enumerate(pieces)
    ]


def within(stacked):
    count = lax.axis_size("ctx")
    groups = [list(range(count // 2)), list(range(count // 2, count))]
    return lax.all_to_all(stacked, "ctx", 0, 0, axis_index_groups=groups, tiled=True)


def half_shards(feats, short_weight, grad_out, filt):
    length, block = filt.shape
    count = lax.axis_size("ctx")
    hc = count // 2
    size = length // 2
    feats, grad_out = feats[0], grad_out[0]
    rows = feats.shape[0]
    high, low = odd_tables(size)
    inverse = np.ascontiguousarray(high.T)
    scale = 1.0 / (math.sqrt(length) * size)
    me = lax.axis_index("ctx")
    dp = lax.axis_index("dp")
    core, x = dp % 2, dp // 2
    quarter = length // 4
    tie = lax.optimization_barrier
    cores = [(i, i ^ 1) for i in range(4)]

    late, source = tie((feats[rows - 2 :], filt))
    before = from_behind(late, "ctx", 1)
    share = size // 2
    part = (lax.dynamic_slice_in_dim(source, core * share, share, 0) * scale).astype(jnp.bfloat16)
    part = lax.ppermute(part, "ctx", [(i, i ^ hc) for i in range(count)])
    gated = gate(feats, before, short_weight, grad_out, count, block, hc)

    ready, gated = tie((before, gated))
    other_pieces, across = exchange(gated[:hc], 0), gated[hc:]
    sent = exchange(across[:1], hc)
    outs = prepare(filt, high, low, feats, ready, short_weight, grad_out, scale, count)
    outs, other_pieces, sent, across, part = tie((outs, other_pieces, sent, across, part))
    near, far = outs[hc:]

    home_pieces = exchange(outs[:hc], 0)
    rest = lax.ppermute(part, "dp", cores)
    sent = list(sent) + exchange(across[1:3], hc + 1)
    outs = spectral(high, inverse, (low, part, rest), other_pieces, (), scale)
    far, outs, home_pieces, sent, across = tie((far, outs, home_pieces, sent, across))

    other_back = exchange(outs[:hc], 0)
    sent = list(sent) + exchange(across[3:], hc + 3)
    send, keep = outs[hc:]
    summed = keep + lax.ppermute(send, "dp", cores)
    eighth = quarter // 2
    other = lax.dynamic_slice_in_dim(summed, (1 - x) * eighth, eighth, 0).astype(jnp.bfloat16)
    other = lax.ppermute(other, "dp", [(i, i ^ 2) for i in range(4)]).astype(jnp.float32)
    summed = lax.dynamic_slice_in_dim(summed, x * eighth, eighth, 0) + other
    crossed = lax.ppermute(summed.astype(jnp.bfloat16), "ctx", [(i, i ^ hc) for i in range(count)])
    outs = spectral(high, inverse, (near, far), home_pieces, sent, scale)
    outs, other_back, crossed = tie((outs, other_back, crossed))

    home_back = within(outs[0].reshape(hc, rows, 2 * block))
    cross_back = exchange(outs[1 : 1 + hc], hc)
    send, keep = outs[1 + hc :]
    came = lax.ppermute(send, "dp", cores)
    result, edge_home, last_home = final(
        feats, before, grad_out, short_weight, [home_back], (), None, count, 0
    )
    keep, came, crossed, edge_home = tie((keep, came, crossed, edge_home))
    crossed = crossed.astype(jnp.float32)
    spots = [jnp.where(x == i, crossed, 0.0) for i in range(2)]
    crossed = jnp.concatenate([*spots, jnp.zeros((quarter, block), jnp.float32)], axis=0)
    home_sum = keep + came + crossed
    there = lax.dynamic_slice_in_dim(home_sum, (1 - x) * quarter, quarter, 0).astype(jnp.bfloat16)
    cross_back, edge_home, there = tie((cross_back, edge_home, there))

    (edges,) = final(
        feats, before, grad_out, short_weight, other_back, cross_back, None, count, hc, edge_home
    )
    edges, there = tie((edges, there))
    edges = from_behind(edges, "ctx", -1)
    there = lax.ppermute(there, "dp", [(i, i ^ 2) for i in range(4)])
    result, _, last_other = final(
        feats, before, grad_out, short_weight, other_back, cross_back, result, count, hc
    )
    result, filt_out = fix(short_weight, edges, last_home, last_other, [home_sum, there], result)
    return (result[None], filt_out)


full_precision = lax.Precision.HIGHEST
split_precision = lax.Precision.HIGH


def from_behind(block, axis, distance):
    devices = range(lax.axis_size(axis))
    route = [(i - distance, i) for i in devices if i - distance in devices]
    return lax.ppermute(block, axis, route)


def angle_table(count_rows, count_cols, period):
    product = (
        jnp.arange(count_rows, dtype=jnp.int32)[:, None]
        * jnp.arange(count_cols, dtype=jnp.int32)[None, :]
        % period
    )
    theta = product.astype(jnp.float32) * (2.0 * math.pi / period)
    return (jnp.cos(theta), jnp.sin(theta))


def make_tables(length):
    total = 2 * length
    outer = 128
    inner = total // outer
    half = outer // 2
    freq = jnp.arange(outer, dtype=jnp.int32)[:, None, None]
    spot = (
        jnp.arange(half, dtype=jnp.int32)[None, :, None] * inner
        + jnp.arange(inner, dtype=jnp.int32)[None, None, :]
    )
    theta = (freq * spot % total).astype(jnp.float32) * (2.0 * math.pi / total)
    first = jnp.stack([jnp.cos(theta), -jnp.sin(theta)], axis=0)
    cos_b, sin_b = angle_table(inner, inner, inner)
    forward_b = jnp.stack(
        [jnp.stack([cos_b, -sin_b], axis=1), jnp.stack([sin_b, cos_b], axis=1)], axis=0
    )
    inverse_b = jnp.stack(
        [jnp.stack([cos_b, sin_b], axis=1), jnp.stack([-sin_b, cos_b], axis=1)], axis=0
    )
    return (first, forward_b, inverse_b)


def finish_forward(partial_spec, tables, accuracy):
    return jnp.einsum("sckrb,rbxq->sckxq", partial_spec, tables[1], precision=accuracy)


def data_forward(signal, tables, accuracy):
    first = tables[0]
    inner = first.shape[3]
    seqs, chans, length = signal.shape
    grid = signal.reshape(seqs, chans, length // inner, inner)
    partial_spec = jnp.einsum("rknb,scnb->sckrb", first, grid, precision=accuracy)
    return finish_forward(partial_spec, tables, accuracy)


def filter_forward(columns, tables):
    first = tables[0]
    inner = first.shape[3]
    length, chans = columns.shape
    grid = columns.reshape(length // inner, inner, chans)
    partial_spec = jnp.einsum("rknb,nbc->ckrb", first, grid, precision=full_precision)[None]
    return finish_forward(partial_spec, tables, full_precision)


def start_inverse(spectrum, tables):
    return jnp.einsum("sckxq,xqrb->sckrb", spectrum, tables[2], precision=full_precision)


def data_inverse(spectrum, tables, length):
    partial_sig = start_inverse(spectrum, tables)
    signal = jnp.einsum("sckrb,rknb->scnb", partial_sig, tables[0], precision=full_precision)
    return signal.reshape(signal.shape[0], signal.shape[1], length) / (2.0 * length)


def filter_inverse(spectrum, tables, length):
    partial_sig = start_inverse(spectrum, tables)[0]
    signal = jnp.einsum("ckrb,rknb->nbc", partial_sig, tables[0], precision=full_precision)
    return signal.reshape(length, signal.shape[2]) / (2.0 * length)


def long_spectral(gated_sig, grad_sig, filter_cols, tables, length):
    g_spec = data_forward(gated_sig, tables, split_precision)
    d_spec = data_forward(grad_sig, tables, split_precision)
    h_spec = filter_forward(filter_cols, tables)
    g_re, g_im = (g_spec[:, :, :, 0], g_spec[:, :, :, 1])
    d_re, d_im = (d_spec[:, :, :, 0], d_spec[:, :, :, 1])
    h_re, h_im = (h_spec[:, :, :, 0], h_spec[:, :, :, 1])
    conv_spec = jnp.stack([h_re * g_re - h_im * g_im, h_re * g_im + h_im * g_re], axis=3)
    grad_spec = jnp.stack([h_re * d_re + h_im * d_im, h_re * d_im - h_im * d_re], axis=3)
    prod_re = jnp.sum(g_re * d_re + g_im * d_im, axis=0, keepdims=True)
    prod_im = jnp.sum(g_re * d_im - g_im * d_re, axis=0, keepdims=True)
    prod_spec = jnp.stack([prod_re, prod_im], axis=3)
    conv_out = data_inverse(conv_spec, tables, length)
    gated_grad = data_inverse(grad_spec, tables, length)
    filt_grad = filter_inverse(prod_spec, tables, length)
    return (conv_out, gated_grad, filt_grad)


def long_shards(feats, short_weight, grad_out, filt):
    rows = feats.shape[1]
    width = feats.shape[2] // 3
    length = filt.shape[0]
    block = filt.shape[1]
    ctx_count = lax.axis_size("ctx")
    replicas = lax.axis_size("dp")
    scale_inv = 1.0 / math.sqrt(length)
    tables = make_tables(length)
    prior = from_behind(feats[:, rows - 2 :, :], "ctx", 1)
    extended = jnp.concatenate([prior, feats], axis=1).astype(jnp.float32)
    mixed = (
        short_weight[0] * extended[:, 2:]
        + short_weight[1] * extended[:, 1 : rows + 1]
        + short_weight[2] * extended[:, :rows]
    )
    query_rows = mixed[:, :, :width]
    key_rows = mixed[:, :, width : 2 * width]
    value_rows = mixed[:, :, 2 * width :]
    gated = (key_rows * value_rows).astype(jnp.bfloat16)
    out_grad = grad_out.astype(jnp.float32)
    conv_grad = (out_grad * query_rows).astype(jnp.bfloat16)
    narrow = block // replicas

    def spread(array):
        return array[0].reshape(rows, ctx_count, replicas, narrow).transpose(1, 2, 3, 0)[:, :, None]

    wide_gated, wide_grad = (
        lax.all_to_all(
            lax.all_to_all(spread(gated), "dp", split_axis=1, concat_axis=2, tiled=True),
            "ctx",
            split_axis=0,
            concat_axis=4,
            tiled=True,
        ),
        lax.all_to_all(
            lax.all_to_all(spread(conv_grad), "dp", split_axis=1, concat_axis=2, tiled=True),
            "ctx",
            split_axis=0,
            concat_axis=4,
            tiled=True,
        ),
    )
    wide_gated = wide_gated.reshape(replicas, narrow, length)
    wide_grad = wide_grad.reshape(replicas, narrow, length)
    offset = lax.axis_index("dp") * narrow
    filt_cols = lax.dynamic_slice_in_dim(filt, offset, narrow, 1)
    conv_out, gated_grad, filt_grad = long_spectral(
        wide_gated, wide_grad, filt_cols * scale_inv, tables, length
    )
    back_conv, back_grad = (
        lax.all_to_all(
            lax.all_to_all(
                conv_out.astype(jnp.bfloat16)[None, None],
                "dp",
                split_axis=2,
                concat_axis=1,
                tiled=True,
            ),
            "ctx",
            split_axis=4,
            concat_axis=0,
            tiled=True,
        ),
        lax.all_to_all(
            lax.all_to_all(
                gated_grad.astype(jnp.bfloat16)[None, None],
                "dp",
                split_axis=2,
                concat_axis=1,
                tiled=True,
            ),
            "ctx",
            split_axis=4,
            concat_axis=0,
            tiled=True,
        ),
    )

    def gather_positions(array):
        return (
            array.reshape(ctx_count, replicas, narrow, rows)
            .transpose(3, 0, 1, 2)
            .reshape(1, rows, width)
        )

    conv_rows = gather_positions(back_conv)
    grad_rows = gather_positions(back_grad)
    parts = filt_grad.reshape(replicas, length // replicas, 1, narrow)
    owned = lax.all_to_all(parts, "dp", split_axis=0, concat_axis=2, tiled=True)
    filt_out = owned.reshape(length // replicas, block) * scale_inv
    grad_query = out_grad * conv_rows.astype(jnp.float32)
    grad_key = grad_rows.astype(jnp.float32) * value_rows
    grad_value = grad_rows.astype(jnp.float32) * key_rows
    grad_mixed = jnp.concatenate([grad_query, grad_key, grad_value], axis=2)
    following = from_behind(grad_mixed[:, :2, :].astype(jnp.bfloat16), "ctx", -1).astype(
        jnp.float32
    )
    ahead = jnp.concatenate([grad_mixed, following], axis=1)
    grad_in = (
        short_weight[0] * grad_mixed
        + short_weight[1] * ahead[:, 1 : rows + 1]
        + short_weight[2] * ahead[:, 2 : rows + 2]
    )
    return (grad_in.astype(jnp.bfloat16), filt_out)


def shards(feats, short_weight, grad_out, filt):
    count = lax.axis_size("ctx")
    length, block = filt.shape
    fits = (
        length <= 1024
        and length % (4 * STEP) == 0
        and count > 1
        and count & (count - 1) == 0
        and feats.shape[1] % 128 == 0
        and block % 128 == 0
        and lax.axis_size("dp") == 4
    )
    plan = half_shards if fits else long_shards
    return plan(feats, short_weight, grad_out, filt)


def solution(mesh):
    return jax.shard_map(
        shards,
        mesh=mesh,
        in_specs=(P("dp", "ctx", None), P(), P("dp", "ctx", None), P(None, "ctx")),
        out_specs=(P("dp", "ctx", None), P("dp", "ctx")),
        check_vma=False,
    )
```

```python
import functools
import math

import jax
import jax.numpy as jnp
import numpy as np
from jax import lax
from jax.experimental import pallas as pl
from jax.experimental.pallas import tpu as pltpu
from jax.sharding import PartitionSpec as P

STEP = 128
STRIP = 128


def params(mebibytes):
    return pltpu.CompilerParams(vmem_limit_bytes=mebibytes * 1024 * 1024)


def cost(flops, moved):
    return pl.CostEstimate(flops=flops, bytes_accessed=moved, transcendentals=0)


def odd_tables(size):
    freq = 2 * np.arange(size, dtype=np.int64)[:, None] + 1
    spot = np.arange(size, dtype=np.int64)[None, :]
    theta = (freq * spot % (4 * size)).astype(np.float64) * (2.0 * math.pi / (4 * size))
    full = np.concatenate([np.cos(theta), -np.sin(theta)], axis=0).astype(np.float32)
    high = full.astype(jnp.bfloat16)
    low = (full - high.astype(np.float32)).astype(jnp.bfloat16)
    return high, low


def dot(a, b):
    return jnp.dot(a, b, preferred_element_type=jnp.float32)


def run(copies):
    for copy in copies:
        copy.start()
    return copies


def finish(copies):
    for copy in copies:
        copy.wait()


def behind(values, before):
    spot = lax.broadcasted_iota(jnp.int32, (values.shape[0], 1), 0)
    one = jnp.where(spot == 0, before[1:2], pltpu.roll(values, 1, 0))
    two = jnp.where(spot == 0, before[0:1], jnp.where(spot == 1, before[1:2], pltpu.roll(values, 2, 0)))
    return one, two


def conv_rows(values, before, taps):
    values = values.astype(jnp.float32)
    one, two = behind(values, before.astype(jnp.float32))
    return taps[0:1] * values + taps[1:2] * one + taps[2:3] * two


def where(hc):
    me = lax.axis_index("ctx")
    return me, me // hc, lax.axis_index("dp") % 2


def strips(cols):
    return [slice(c, c + STRIP) for c in range(0, cols, STRIP)]


def gate_kernel(hc, count, base, feats_ref, before, taps_ref, grad_ref, *refs):
    crossing = base > 0
    outs, refs = refs[: hc * (2 if crossing else 1)], refs[hc * (2 if crossing else 1) :]
    parts, taps, stage, in_sem, small_sem, out_sem = refs
    rows, cols = parts.shape[2:]
    me, half, core = where(hc)

    def column(region, j):
        return pl.ds(pl.multiple_of((region * count + (me ^ (base + j))) * cols, cols), cols)

    small = run([pltpu.make_async_copy(taps_ref, taps, small_sem)])
    loads = [
        run(
            [
                pltpu.make_async_copy(feats_ref.at[:, column(r, j)], parts.at[j, r], in_sem.at[j, r])
                for r in range(3)
            ]
            + [pltpu.make_async_copy(grad_ref.at[:, column(0, j)], parts.at[j, 3], in_sem.at[j, 3])]
        )
        for j in range(hc)
    ]
    finish(small)
    stores = []
    for j in range(hc):
        finish(loads[j])
        mine = [(before[:, column(r, j)], taps[:, column(r, j)]) for r in range(3)]
        for strip in strips(cols):
            query, key, value = (
                conv_rows(parts[j, r, :, strip], mine[r][0][:, strip], mine[r][1][:, strip])
                for r in range(3)
            )
            stage[j, :, strip] = (key * value).astype(jnp.bfloat16)
            stage[j, :, cols + strip.start : cols + strip.stop] = (
                parts[j, 3, :, strip].astype(jnp.float32) * query
            ).astype(jnp.bfloat16)
        stores += run([pltpu.make_async_copy(stage.at[j], outs[j], out_sem.at[j])])
        if crossing:
            crossed = stage.at[j, :, pl.ds(pl.multiple_of(half * cols, cols), cols)]
            stores += run([pltpu.make_async_copy(crossed, outs[hc + j], out_sem.at[hc + j])])
    finish(stores)


def gate(feats, before, taps, grad_out, count, cols, base):
    rows = feats.shape[0]
    hc = count // 2
    shapes = [jax.ShapeDtypeStruct((rows, 2 * cols), jnp.bfloat16)] * hc
    shapes = shapes + [jax.ShapeDtypeStruct((rows, cols), jnp.bfloat16)] * hc
    hbm = pl.BlockSpec(memory_space=pl.ANY)
    return pl.pallas_call(
        functools.partial(gate_kernel, hc, count, base),
        in_specs=[hbm, pl.BlockSpec(memory_space=pltpu.VMEM), hbm, hbm],
        out_specs=[hbm] * len(shapes),
        out_shape=shapes,
        scratch_shapes=[
            pltpu.VMEM((hc, 4, rows, cols), jnp.bfloat16),
            pltpu.VMEM(taps.shape, taps.dtype),
            pltpu.VMEM((hc, rows, 2 * cols), jnp.bfloat16),
            pltpu.SemaphoreType.DMA((hc, 4)),
            pltpu.SemaphoreType.DMA,
            pltpu.SemaphoreType.DMA((len(shapes),)),
        ],
        compiler_params=params(56),
        cost_estimate=cost(20 * rows * cols * hc, 12 * rows * cols * hc),
        name="gate_other",
    )(feats, before, taps, grad_out)


def signs(first, rows):
    odd = (lax.broadcasted_iota(jnp.int32, (rows, 1), 0) + first) % 2
    return 1.0 - 2.0 * odd.astype(jnp.float32)


def filter_home_kernel(scale, filt_ref, high_ref, low_ref, near_ref, far_ref):
    size = filt_ref.shape[0] // 2

    def spectrum(part):
        now = part * scale
        high = now.astype(jnp.bfloat16)
        low = (now - high.astype(jnp.float32)).astype(jnp.bfloat16)
        return dot(high_ref[...], high) + dot(high_ref[...], low) + dot(low_ref[...], high)

    near = spectrum(filt_ref[:size, :])
    far = spectrum(filt_ref[size:, :])
    near_ref[...] = near
    sign = signs(0, size)
    far_ref[:size, :] = far[:size] - sign * near[size:]
    far_ref[size:, :] = far[size:] + sign * near[:size]


def prepare_kernel(hc, count, scale, *refs):
    filters, refs = refs[:3], refs[3:]
    gate_in, refs = refs[:4], refs[4:]
    gate_out, refs = refs[:hc], refs[hc:]
    gate_kernel(hc, count, 0, *gate_in, *gate_out, *refs[2:])
    filter_home_kernel(scale, *filters, *refs[:2])


def prepare(filt, high, low, feats, before, taps, grad_out, scale, count):
    rows = feats.shape[0]
    length, cols = filt.shape
    hc = count // 2
    shapes = [jax.ShapeDtypeStruct((rows, 2 * cols), jnp.bfloat16)] * hc
    spectra = [jax.ShapeDtypeStruct((length, cols), jnp.float32)] * 2
    hbm = pl.BlockSpec(memory_space=pl.ANY)
    vmem = pl.BlockSpec(memory_space=pltpu.VMEM)
    return pl.pallas_call(
        functools.partial(prepare_kernel, hc, count, scale),
        in_specs=[vmem] * 3 + [hbm, vmem, hbm, hbm],
        out_specs=[hbm] * hc + [vmem] * 2,
        out_shape=shapes + spectra,
        scratch_shapes=[
            pltpu.VMEM((hc, 4, rows, cols), jnp.bfloat16),
            pltpu.VMEM(taps.shape, taps.dtype),
            pltpu.VMEM((hc, rows, 2 * cols), jnp.bfloat16),
            pltpu.SemaphoreType.DMA((hc, 4)),
            pltpu.SemaphoreType.DMA,
            pltpu.SemaphoreType.DMA((len(shapes),)),
        ],
        compiler_params=params(56),
        cost_estimate=cost(8 * length * length * cols, 20 * length * cols),
        name="prepare",
    )(filt, high, low, feats, before, taps, grad_out)


def times(a_re, a_im, b_re, b_im):
    return a_re * b_re - a_im * b_im, a_re * b_im + a_im * b_re


def conj_times(a_re, a_im, b_re, b_im):
    return a_re * b_re + a_im * b_im, a_re * b_im - a_im * b_re


def spectral_kernel(hc, rows, home, scale, *refs):
    tables, refs = refs[: 4 if home else 5], refs[4 if home else 5 :]
    pieces, refs = refs[:hc], refs[hc:]
    crosses = ()
    if home:
        crosses, refs = refs[:hc], refs[hc:]
    outs, refs = refs[: 1 if home else hc], refs[1 if home else hc :]
    cross_outs = ()
    if home:
        cross_outs, refs = refs[:hc], refs[hc:]
    sums, refs = refs[:2], refs[2:]
    held, refs = refs[: len(tables)], refs[len(tables) :]
    data, spec, prod, res, corr, piece_sem, table_sem, out_sem, corr_sem = refs[:9]
    forward_ref, inverse_ref = held[:2]
    near_ref, far_ref = (held[2], held[3]) if home else (refs[-1], None)
    me, half, core = where(hc)
    spot = me % hc
    size = data.shape[0]
    cols = res.shape[1] // (3 if home else 2)

    def place(j):
        return pl.ds(pl.multiple_of((spot ^ j) * rows, rows), rows)

    def load(i):
        return run([pltpu.make_async_copy(tables[i], held[i], table_sem.at[i])])

    forward_copy = load(0)
    piece_copies = run(
        [pltpu.make_async_copy(pieces[j], data.at[place(j), : 2 * cols], piece_sem.at[j]) for j in range(hc)]
    )
    cross_copies = run(
        [
            pltpu.make_async_copy(crosses[j], data.at[place(j), 2 * cols :], piece_sem.at[hc + j])
            for j in range(len(crosses))
        ]
    )
    filter_copies = [copy for i in range(2, len(tables)) for copy in load(i)]
    inverse_copy = load(1)
    finish(forward_copy)
    finish(piece_copies)
    for part in range(data.shape[1] // cols):
        if part == 2:
            finish(cross_copies)
        here = slice(part * cols, (part + 1) * cols)
        spec[:, here] = dot(forward_ref[...], data[:, here])
    finish(filter_copies)
    if not home:
        low_ref, mine_ref, theirs_ref = held[2:]
        share = mine_ref.shape[0]
        mine = pl.ds(pl.multiple_of(core * share, share), share)
        theirs = pl.ds(pl.multiple_of((1 - core) * share, share), share)
        near_ref[...] = (
            dot(forward_ref[:, mine], mine_ref[...])
            + dot(forward_ref[:, theirs], theirs_ref[...])
            + dot(low_ref[:, mine], mine_ref[...])
            + dot(low_ref[:, theirs], theirs_ref[...])
        )

    def products(side):
        def body(i, carry):
            low = pl.ds(pl.multiple_of(i * STEP, STEP), STEP)
            high = pl.ds(pl.multiple_of(size + i * STEP, STEP), STEP)

            def get(part):
                here = slice(part * cols, (part + 1) * cols)
                return spec[low, here], spec[high, here]

            def put(part, value):
                here = slice(part * cols, (part + 1) * cols)
                prod[low, here] = value[0].astype(jnp.bfloat16)
                prod[high, here] = value[1].astype(jnp.bfloat16)

            g, d = get(0), get(1)
            h = near_ref[low, :], near_ref[high, :]
            conv = times(*h, *g)
            grad = conj_times(*h, *d)
            corr = conj_times(*g, *d)
            if home:
                f = far_ref[low, :], far_ref[high, :]
                gx, dx = (g, get(2)) if side == 0 else (get(2), d)
                far_conv = times(*f, *gx)
                far_grad = conj_times(*f, *dx)
                if side == 0:
                    grad = (grad[0] + far_grad[0], grad[1] + far_grad[1])
                else:
                    conv = (conv[0] + far_conv[0], conv[1] + far_conv[1])
                put(2, far_conv if side == 0 else far_grad)
                far_corr = conj_times(*gx, *dx)
                sign = signs(0, STEP)
                corr = (corr[0] + sign * far_corr[1], corr[1] - sign * far_corr[0])
                put(4, far_corr)
                put(3, corr)
            else:
                put(2, corr)
            put(0, conv)
            put(1, grad)
            return carry

        lax.fori_loop(0, size // STEP, body, 0)

    if home:

        @pl.when(half == 0)
        def _():
            products(0)

        @pl.when(half == 1)
        def _():
            products(1)

    else:
        products(0)

    def back(part):
        return dot(inverse_ref[...], prod[:, part * cols : (part + 1) * cols])

    finish(inverse_copy)
    res[:, :cols] = back(0).astype(jnp.bfloat16)
    res[:, cols : 2 * cols] = back(1).astype(jnp.bfloat16)
    if home:
        stores = run([pltpu.make_async_copy(res.at[:, : 2 * cols], outs[0], out_sem.at[0])])
    else:
        stores = run(
            [pltpu.make_async_copy(res.at[place(j), : 2 * cols], outs[j], out_sem.at[j]) for j in range(hc)]
        )
    if home:
        res[:, 2 * cols :] = back(2).astype(jnp.bfloat16)
        stores += run(
            [
                pltpu.make_async_copy(res.at[place(j), 2 * cols :], cross_outs[j], out_sem.at[hc + j])
                for j in range(hc)
            ]
        )
    quarter = size // 2
    for x in range(2 if home else 1):
        corr[x] = back((3 if home else 2) + x) * scale
        for i, which in enumerate((1 - core, core)):
            lags = pl.ds(pl.multiple_of(which * quarter, quarter), quarter)
            stores += run(
                [
                    pltpu.make_async_copy(
                        corr.at[x, lags], sums[i].at[x * quarter : (x + 1) * quarter], corr_sem.at[x, i]
                    )
                ]
            )
    finish(stores)


def spectral(forward, inverse, filters, pieces, crosses, scale):
    hc = len(pieces)
    rows, width = pieces[0].shape
    cols = width // 2
    size = hc * rows
    home = len(crosses) > 0
    hbm = pl.BlockSpec(memory_space=pl.ANY)
    tables = [forward, inverse, *filters]
    arrived = [*pieces, *crosses]
    ins = 3 if home else 2
    parts = 5 if home else 3
    share = jax.ShapeDtypeStruct((size if home else size // 2, cols), jnp.float32)
    sums = [share, share]
    if home:
        shapes = [jax.ShapeDtypeStruct((size, width), jnp.bfloat16)]
        shapes = shapes + [jax.ShapeDtypeStruct((rows, cols), jnp.bfloat16)] * hc
    else:
        shapes = [jax.ShapeDtypeStruct((rows, width), jnp.bfloat16)] * hc
    return pl.pallas_call(
        functools.partial(spectral_kernel, hc, rows, home, scale),
        in_specs=[hbm] * (len(tables) + len(arrived)),
        out_specs=[hbm] * (len(shapes) + len(sums)),
        out_shape=shapes + sums,
        scratch_shapes=[pltpu.VMEM(t.shape, t.dtype) for t in tables]
        + [
            pltpu.VMEM((size, ins * cols), jnp.bfloat16),
            pltpu.VMEM((2 * size, ins * cols), jnp.float32),
            pltpu.VMEM((2 * size, parts * cols), jnp.bfloat16),
            pltpu.VMEM((size, ins * cols), jnp.bfloat16),
            pltpu.VMEM((2 if home else 1, size, cols), jnp.float32),
            pltpu.SemaphoreType.DMA((len(arrived),)),
            pltpu.SemaphoreType.DMA((len(tables),)),
            pltpu.SemaphoreType.DMA((2 * hc,)),
            pltpu.SemaphoreType.DMA((2, 2)),
        ]
        + ([] if home else [pltpu.VMEM((2 * size, cols), jnp.float32)]),
        compiler_params=params(56 if home else 36),
        cost_estimate=cost(4 * size * size * cols * (ins + parts), 8 * size * size + 30 * size * cols),
        name="spectral_home" if home else "spectral_other",
    )(*tables, *arrived)


def final_kernel(hc, count, base, top, aliased, *refs):
    feats_ref, before, grad_ref, taps_ref = refs[:4]
    crosses = ()
    if base > 0:
        pieces, crosses, refs = refs[4 : 4 + hc], refs[4 + hc : 4 + 2 * hc], refs[4 + 2 * hc :]
    else:
        slots = [(lax.axis_index("ctx") % hc) ^ j for j in range(hc)]
        pieces, refs = [refs[4].at[slot] for slot in slots], refs[5:]
    if aliased:
        refs = refs[1:]
    out_ref = last_ref = stage = last = None
    if top:
        first_ref, edge_ref, parts, taps, back, edges, in_sem, small_sem, back_sem, end_sem = refs
        edge = edges.at[1]
    else:
        out_ref, edge_ref, last_ref, parts, taps, back, edge, last, stage = refs[:9]
        in_sem, small_sem, back_sem, end_sem, out_sem = refs[9:]
    me, half, _ = where(hc)
    rows, cols = parts.shape[2:]

    def column(region, j):
        return pl.ds(pl.multiple_of((region * count + (me ^ (base + j))) * cols, cols), cols)

    small = run([pltpu.make_async_copy(taps_ref, taps, small_sem)])
    if top:
        small += run([pltpu.make_async_copy(first_ref, edges.at[0], end_sem.at[1])])
    loads = []
    for j in range(hc):
        copies = [
            pltpu.make_async_copy(source.at[:rows, column(r, j)], parts.at[j, r], in_sem.at[j, r])
            for r, source in enumerate((grad_ref, feats_ref, feats_ref))
        ]
        copies.append(
            pltpu.make_async_copy(pieces[j].at[:rows], back.at[j, :, : 2 * cols], back_sem.at[j])
        )
        if base > 0:
            copies.append(
                pltpu.make_async_copy(crosses[j].at[:rows], back.at[j, :, 2 * cols :], back_sem.at[hc + j])
            )
        loads.append(run(copies))
    finish(small)
    stores = []
    spot = lax.broadcasted_iota(jnp.int32, (rows, 1), 0)
    for j in range(hc):
        finish(loads[j])
        near_taps = [taps[:, column(r, j)] for r in range(3)]
        near_before = [before[:, column(r, j)] for r in range(3)]
        slot = (me ^ (base + j)) % hc
        for strip in strips(cols):

            def unmixed(region, dz):
                edge[slot, region, :, strip] = dz[:2].astype(jnp.bfloat16)
                if top:
                    return
                weights = near_taps[region][:, strip]
                one = jnp.where(spot < rows - 1, pltpu.roll(dz, rows - 1, 0), 0.0)
                two = jnp.where(spot < rows - 2, pltpu.roll(dz, rows - 2, 0), 0.0)
                out = weights[0:1] * dz + weights[1:2] * one + weights[2:3] * two
                last[slot, region, :, strip] = out[rows - 16 :]
                stage[j, region, :, strip] = out.astype(jnp.bfloat16)

            key, value = (
                conv_rows(parts[j, r, :, strip], near_before[r][:, strip], near_taps[r][:, strip])
                for r in (1, 2)
            )
            conv = back[j, :, strip].astype(jnp.float32)
            grad = back[j, :, cols + strip.start : cols + strip.stop].astype(jnp.float32)
            if base > 0:
                extra = back[j, :, 2 * cols + strip.start : 2 * cols + strip.stop].astype(jnp.float32)
                conv = jnp.where(half == 1, conv + extra, conv)
                grad = jnp.where(half == 0, grad + extra, grad)
            unmixed(0, parts[j, 0, :, strip].astype(jnp.float32) * conv)
            unmixed(1, grad * value)
            unmixed(2, grad * key)
        if not top:
            stores += run(
                [
                    pltpu.make_async_copy(stage.at[j, r], out_ref.at[:, column(r, j)], out_sem.at[j, r])
                    for r in range(3)
                ]
            )
    stores += run([pltpu.make_async_copy(edges if top else edge, edge_ref, end_sem.at[0])])
    if not top:
        stores += run([pltpu.make_async_copy(last, last_ref, end_sem.at[1])])
    finish(stores)


def final(feats, before, grad_out, taps, pieces, crosses, so_far, count, base, first=None):
    hc = count // 2
    top = first is not None
    rows = 16 if top else feats.shape[0]
    cols = pieces[0].shape[-1] // 2
    hbm = pl.BlockSpec(memory_space=pl.ANY)
    arrived = [*pieces, *crosses]
    args = [feats, before, grad_out, taps, *arrived]
    aliases = {}
    if top:
        args.append(first)
    if so_far is not None:
        args.append(so_far)
        aliases = {len(args) - 1: 0}
    edge = jax.ShapeDtypeStruct((hc, 3, 2, cols), jnp.bfloat16)
    last = jax.ShapeDtypeStruct((hc, 3, 16, cols), jnp.float32)
    edges = jax.ShapeDtypeStruct((2, *edge.shape), edge.dtype)
    shapes = [edges] if top else [jax.ShapeDtypeStruct(feats.shape, jnp.bfloat16), edge, last]
    scratch = [
        pltpu.VMEM((hc, 3, rows, cols), jnp.bfloat16),
        pltpu.VMEM(taps.shape, taps.dtype),
        pltpu.VMEM((hc, rows, (3 if base > 0 else 2) * cols), jnp.bfloat16),
        pltpu.VMEM(edges.shape if top else edge.shape, edge.dtype),
    ]
    if not top:
        scratch += [
            pltpu.VMEM(last.shape, last.dtype),
            pltpu.VMEM((hc, 3, rows, cols), jnp.bfloat16),
        ]
    scratch += [
        pltpu.SemaphoreType.DMA((hc, 3)),
        pltpu.SemaphoreType.DMA,
        pltpu.SemaphoreType.DMA((2 * hc,)),
        pltpu.SemaphoreType.DMA((2,)),
    ]
    if not top:
        scratch.append(pltpu.SemaphoreType.DMA((hc, 3)))
    name = ("edge_" if top else "final_") + ("other" if base > 0 else "home")
    return pl.pallas_call(
        functools.partial(final_kernel, hc, count, base, top, so_far is not None),
        in_specs=[hbm, pl.BlockSpec(memory_space=pltpu.VMEM)] + [hbm] * (len(args) - 2),
        out_specs=[hbm] * len(shapes),
        scratch_shapes=scratch,
        out_shape=shapes,
        input_output_aliases=aliases,
        compiler_params=params(16 if top or base > 0 else 56),
        cost_estimate=cost(30 * rows * cols * hc, 16 * rows * cols * hc),
        name=name,
    )(*args)


def fix_kernel(hc, taps_ref, edge_ref, lh_ref, lo_ref, *refs):
    own_ref, *sums, _, out_ref, filt_ref, stage, sem = refs
    me, half, _ = where(hc)
    cols = edge_ref.shape[4]
    width = out_ref.shape[1] // 3
    turn = me == hc - 1
    spot = lax.broadcasted_iota(jnp.int32, (16, 1), 0)
    for slot, last in enumerate((lh_ref, lo_ref)):
        mine, swapped = edge_ref.at[slot], edge_ref.at[1 - slot]
        first = jnp.where(half == slot, 0, hc)
        for j in range(hc):
            for region in range(3):
                col = pl.ds(pl.multiple_of(region * width + (first + j) * cols, cols), cols)
                ahead = jnp.where(
                    turn, swapped[j, region].astype(jnp.float32), mine[j, region].astype(jnp.float32)
                )
                one, two = taps_ref[1:2, col], taps_ref[2:3, col]
                add = jnp.where(
                    spot == 14,
                    two * ahead[0:1],
                    jnp.where(spot == 15, one * ahead[0:1] + two * ahead[1:2], 0.0),
                )
                stage[:, col] = (last[j, region] + add).astype(jnp.bfloat16)
    copy = pltpu.make_async_copy(stage, out_ref.at[pl.ds(out_ref.shape[0] - 16, 16)], sem)
    copy.start()
    lags = filt_ref.shape[0]
    total = own_ref[pl.ds(pl.multiple_of((lax.axis_index("dp") // 2) * lags, lags), lags), :]
    for ref in sums:
        total += ref[...].astype(jnp.float32)
    filt_ref[...] = total
    copy.wait()


def fix(taps, edges, last_home, last_other, sums, result):
    hc = edges.shape[1]
    vmem = pl.BlockSpec(memory_space=pltpu.VMEM)
    hbm = pl.BlockSpec(memory_space=pl.ANY)
    return pl.pallas_call(
        functools.partial(fix_kernel, hc),
        in_specs=[vmem] * (4 + len(sums)) + [hbm],
        out_specs=[hbm, vmem],
        out_shape=[
            jax.ShapeDtypeStruct(result.shape, result.dtype),
            jax.ShapeDtypeStruct(sums[-1].shape, jnp.float32),
        ],
        scratch_shapes=[pltpu.VMEM((16, result.shape[1]), jnp.bfloat16), pltpu.SemaphoreType.DMA],
        input_output_aliases={4 + len(sums): 0},
        compiler_params=params(16),
        cost_estimate=cost(16 * 8 * result.shape[1], 128 * result.shape[1]),
        name="fix",
    )(taps, edges, last_home, last_other, *sums, result)


def exchange(pieces, base):
    devices = range(lax.axis_size("ctx"))
    return [
        piece if base + j == 0 else lax.ppermute(piece, "ctx", [(i, i ^ (base + j)) for i in devices])
        for j, piece in enumerate(pieces)
    ]


def within(stacked):
    count = lax.axis_size("ctx")
    groups = [list(range(count // 2)), list(range(count // 2, count))]
    return lax.all_to_all(stacked, "ctx", 0, 0, axis_index_groups=groups, tiled=True)


def half_shards(feats, short_weight, grad_out, filt):
    length, block = filt.shape
    count = lax.axis_size("ctx")
    hc = count // 2
    size = length // 2
    feats, grad_out = feats[0], grad_out[0]
    rows = feats.shape[0]
    high, low = odd_tables(size)
    inverse = np.ascontiguousarray(high.T)
    scale = 1.0 / (math.sqrt(length) * size)
    me = lax.axis_index("ctx")
    dp = lax.axis_index("dp")
    core, x = dp % 2, dp // 2
    quarter = length // 4
    tie = lax.optimization_barrier
    cores = [(i, i ^ 1) for i in range(4)]

    late, source = tie((feats[rows - 2 :], filt))
    before = from_behind(late, "ctx", 1)
    share = size // 2
    part = (lax.dynamic_slice_in_dim(source, core * share, share, 0) * scale).astype(jnp.bfloat16)
    part = lax.ppermute(part, "ctx", [(i, i ^ hc) for i in range(count)])
    gated = gate(feats, before, short_weight, grad_out, count, block, hc)

    ready, gated = tie((before, gated))
    other_pieces, across = exchange(gated[:hc], 0), gated[hc:]
    outs = prepare(filt, high, low, feats, ready, short_weight, grad_out, scale, count)
    outs, other_pieces, across, part = tie((outs, other_pieces, across, part))
    near, far = outs[hc:]

    home_pieces = exchange(outs[:hc], 0)
    rest = lax.ppermute(part, "dp", cores)
    sent = exchange(across[:2], hc)
    outs = spectral(high, inverse, (low, part, rest), other_pieces, (), scale)
    far, outs, home_pieces, sent, across = tie((far, outs, home_pieces, sent, across))

    other_back = exchange(outs[:hc], 0)
    sent = list(sent) + exchange(across[2:], hc + 2)
    send, keep = outs[hc:]
    summed = keep + lax.ppermute(send, "dp", cores)
    crossed = lax.ppermute(summed.astype(jnp.bfloat16), "ctx", [(i, i ^ hc) for i in range(count)])
    outs = spectral(high, inverse, (near, far), home_pieces, sent, scale)
    outs, other_back, crossed = tie((outs, other_back, crossed))

    home_back = within(outs[0].reshape(hc, rows, 2 * block))
    cross_back = exchange(outs[1 : 1 + hc], hc)
    send, keep = outs[1 + hc :]
    came = lax.ppermute(send, "dp", cores)
    result, edge_home, last_home = final(
        feats, before, grad_out, short_weight, [home_back], (), None, count, 0
    )
    keep, came, crossed, edge_home = tie((keep, came, crossed, edge_home))
    crossed = jnp.concatenate([crossed.astype(jnp.float32), jnp.zeros((quarter, block), jnp.float32)], axis=0)
    home_sum = keep + came + crossed
    there = lax.dynamic_slice_in_dim(home_sum, (1 - x) * quarter, quarter, 0).astype(jnp.bfloat16)
    cross_back, edge_home, there = tie((cross_back, edge_home, there))

    (edges,) = final(
        feats, before, grad_out, short_weight, other_back, cross_back, None, count, hc, edge_home
    )
    edges, there = tie((edges, there))
    edges = from_behind(edges, "ctx", -1)
    there = lax.ppermute(there, "dp", [(i, i ^ 2) for i in range(4)])
    result, _, last_other = final(
        feats, before, grad_out, short_weight, other_back, cross_back, result, count, hc
    )
    result, filt_out = fix(short_weight, edges, last_home, last_other, [home_sum, there], result)
    return (result[None], filt_out)


full_precision = lax.Precision.HIGHEST
split_precision = lax.Precision.HIGH


def from_behind(block, axis, distance):
    devices = range(lax.axis_size(axis))
    route = [(i - distance, i) for i in devices if i - distance in devices]
    return lax.ppermute(block, axis, route)


def angle_table(count_rows, count_cols, period):
    product = (
        jnp.arange(count_rows, dtype=jnp.int32)[:, None]
        * jnp.arange(count_cols, dtype=jnp.int32)[None, :]
        % period
    )
    theta = product.astype(jnp.float32) * (2.0 * math.pi / period)
    return (jnp.cos(theta), jnp.sin(theta))


def make_tables(length):
    total = 2 * length
    outer = 128
    inner = total // outer
    half = outer // 2
    freq = jnp.arange(outer, dtype=jnp.int32)[:, None, None]
    spot = (
        jnp.arange(half, dtype=jnp.int32)[None, :, None] * inner
        + jnp.arange(inner, dtype=jnp.int32)[None, None, :]
    )
    theta = (freq * spot % total).astype(jnp.float32) * (2.0 * math.pi / total)
    first = jnp.stack([jnp.cos(theta), -jnp.sin(theta)], axis=0)
    cos_b, sin_b = angle_table(inner, inner, inner)
    forward_b = jnp.stack(
        [jnp.stack([cos_b, -sin_b], axis=1), jnp.stack([sin_b, cos_b], axis=1)], axis=0
    )
    inverse_b = jnp.stack(
        [jnp.stack([cos_b, sin_b], axis=1), jnp.stack([-sin_b, cos_b], axis=1)], axis=0
    )
    return (first, forward_b, inverse_b)


def finish_forward(partial_spec, tables, accuracy):
    return jnp.einsum("sckrb,rbxq->sckxq", partial_spec, tables[1], precision=accuracy)


def data_forward(signal, tables, accuracy):
    first = tables[0]
    inner = first.shape[3]
    seqs, chans, length = signal.shape
    grid = signal.reshape(seqs, chans, length // inner, inner)
    partial_spec = jnp.einsum("rknb,scnb->sckrb", first, grid, precision=accuracy)
    return finish_forward(partial_spec, tables, accuracy)


def filter_forward(columns, tables):
    first = tables[0]
    inner = first.shape[3]
    length, chans = columns.shape
    grid = columns.reshape(length // inner, inner, chans)
    partial_spec = jnp.einsum("rknb,nbc->ckrb", first, grid, precision=full_precision)[None]
    return finish_forward(partial_spec, tables, full_precision)


def start_inverse(spectrum, tables):
    return jnp.einsum("sckxq,xqrb->sckrb", spectrum, tables[2], precision=full_precision)


def data_inverse(spectrum, tables, length):
    partial_sig = start_inverse(spectrum, tables)
    signal = jnp.einsum("sckrb,rknb->scnb", partial_sig, tables[0], precision=full_precision)
    return signal.reshape(signal.shape[0], signal.shape[1], length) / (2.0 * length)


def filter_inverse(spectrum, tables, length):
    partial_sig = start_inverse(spectrum, tables)[0]
    signal = jnp.einsum("ckrb,rknb->nbc", partial_sig, tables[0], precision=full_precision)
    return signal.reshape(length, signal.shape[2]) / (2.0 * length)


def long_spectral(gated_sig, grad_sig, filter_cols, tables, length):
    g_spec = data_forward(gated_sig, tables, split_precision)
    d_spec = data_forward(grad_sig, tables, split_precision)
    h_spec = filter_forward(filter_cols, tables)
    g_re, g_im = (g_spec[:, :, :, 0], g_spec[:, :, :, 1])
    d_re, d_im = (d_spec[:, :, :, 0], d_spec[:, :, :, 1])
    h_re, h_im = (h_spec[:, :, :, 0], h_spec[:, :, :, 1])
    conv_spec = jnp.stack([h_re * g_re - h_im * g_im, h_re * g_im + h_im * g_re], axis=3)
    grad_spec = jnp.stack([h_re * d_re + h_im * d_im, h_re * d_im - h_im * d_re], axis=3)
    prod_re = jnp.sum(g_re * d_re + g_im * d_im, axis=0, keepdims=True)
    prod_im = jnp.sum(g_re * d_im - g_im * d_re, axis=0, keepdims=True)
    prod_spec = jnp.stack([prod_re, prod_im], axis=3)
    conv_out = data_inverse(conv_spec, tables, length)
    gated_grad = data_inverse(grad_spec, tables, length)
    filt_grad = filter_inverse(prod_spec, tables, length)
    return (conv_out, gated_grad, filt_grad)


def long_shards(feats, short_weight, grad_out, filt):
    rows = feats.shape[1]
    width = feats.shape[2] // 3
    length = filt.shape[0]
    block = filt.shape[1]
    ctx_count = lax.axis_size("ctx")
    replicas = lax.axis_size("dp")
    scale_inv = 1.0 / math.sqrt(length)
    tables = make_tables(length)
    prior = from_behind(feats[:, rows - 2 :, :], "ctx", 1)
    extended = jnp.concatenate([prior, feats], axis=1).astype(jnp.float32)
    mixed = (
        short_weight[0] * extended[:, 2:]
        + short_weight[1] * extended[:, 1 : rows + 1]
        + short_weight[2] * extended[:, :rows]
    )
    query_rows = mixed[:, :, :width]
    key_rows = mixed[:, :, width : 2 * width]
    value_rows = mixed[:, :, 2 * width :]
    gated = (key_rows * value_rows).astype(jnp.bfloat16)
    out_grad = grad_out.astype(jnp.float32)
    conv_grad = (out_grad * query_rows).astype(jnp.bfloat16)
    narrow = block // replicas

    def spread(array):
        return array[0].reshape(rows, ctx_count, replicas, narrow).transpose(1, 2, 3, 0)[:, :, None]

    wide_gated, wide_grad = (
        lax.all_to_all(
            lax.all_to_all(spread(gated), "dp", split_axis=1, concat_axis=2, tiled=True),
            "ctx",
            split_axis=0,
            concat_axis=4,
            tiled=True,
        ),
        lax.all_to_all(
            lax.all_to_all(spread(conv_grad), "dp", split_axis=1, concat_axis=2, tiled=True),
            "ctx",
            split_axis=0,
            concat_axis=4,
            tiled=True,
        ),
    )
    wide_gated = wide_gated.reshape(replicas, narrow, length)
    wide_grad = wide_grad.reshape(replicas, narrow, length)
    offset = lax.axis_index("dp") * narrow
    filt_cols = lax.dynamic_slice_in_dim(filt, offset, narrow, 1)
    conv_out, gated_grad, filt_grad = long_spectral(
        wide_gated, wide_grad, filt_cols * scale_inv, tables, length
    )
    back_conv, back_grad = (
        lax.all_to_all(
            lax.all_to_all(
                conv_out.astype(jnp.bfloat16)[None, None],
                "dp",
                split_axis=2,
                concat_axis=1,
                tiled=True,
            ),
            "ctx",
            split_axis=4,
            concat_axis=0,
            tiled=True,
        ),
        lax.all_to_all(
            lax.all_to_all(
                gated_grad.astype(jnp.bfloat16)[None, None],
                "dp",
                split_axis=2,
                concat_axis=1,
                tiled=True,
            ),
            "ctx",
            split_axis=4,
            concat_axis=0,
            tiled=True,
        ),
    )

    def gather_positions(array):
        return (
            array.reshape(ctx_count, replicas, narrow, rows)
            .transpose(3, 0, 1, 2)
            .reshape(1, rows, width)
        )

    conv_rows = gather_positions(back_conv)
    grad_rows = gather_positions(back_grad)
    parts = filt_grad.reshape(replicas, length // replicas, 1, narrow)
    owned = lax.all_to_all(parts, "dp", split_axis=0, concat_axis=2, tiled=True)
    filt_out = owned.reshape(length // replicas, block) * scale_inv
    grad_query = out_grad * conv_rows.astype(jnp.float32)
    grad_key = grad_rows.astype(jnp.float32) * value_rows
    grad_value = grad_rows.astype(jnp.float32) * key_rows
    grad_mixed = jnp.concatenate([grad_query, grad_key, grad_value], axis=2)
    following = from_behind(grad_mixed[:, :2, :].astype(jnp.bfloat16), "ctx", -1).astype(
        jnp.float32
    )
    ahead = jnp.concatenate([grad_mixed, following], axis=1)
    grad_in = (
        short_weight[0] * grad_mixed
        + short_weight[1] * ahead[:, 1 : rows + 1]
        + short_weight[2] * ahead[:, 2 : rows + 2]
    )
    return (grad_in.astype(jnp.bfloat16), filt_out)


def shards(feats, short_weight, grad_out, filt):
    count = lax.axis_size("ctx")
    length, block = filt.shape
    fits = (
        length <= 1024
        and length % (4 * STEP) == 0
        and count > 1
        and count & (count - 1) == 0
        and feats.shape[1] % 128 == 0
        and block % 128 == 0
        and lax.axis_size("dp") == 4
    )
    plan = half_shards if fits else long_shards
    return plan(feats, short_weight, grad_out, filt)


def solution(mesh):
    return jax.shard_map(
        shards,
        mesh=mesh,
        in_specs=(P("dp", "ctx", None), P(), P("dp", "ctx", None), P(None, "ctx")),
        out_specs=(P("dp", "ctx", None), P("dp", "ctx")),
        check_vma=False,
    )
```

```python
import functools
import math

import jax
import jax.numpy as jnp
import numpy as np
from jax import lax
from jax.experimental import pallas as pl
from jax.experimental.pallas import tpu as pltpu
from jax.sharding import PartitionSpec as P

STEP = 128
STRIP = 128


def params(mebibytes):
    return pltpu.CompilerParams(vmem_limit_bytes=mebibytes * 1024 * 1024)


def cost(flops, moved):
    return pl.CostEstimate(flops=flops, bytes_accessed=moved, transcendentals=0)


def odd_tables(size):
    freq = 2 * np.arange(size, dtype=np.int64)[:, None] + 1
    spot = np.arange(size, dtype=np.int64)[None, :]
    theta = (freq * spot % (4 * size)).astype(np.float64) * (2.0 * math.pi / (4 * size))
    full = np.concatenate([np.cos(theta), -np.sin(theta)], axis=0).astype(np.float32)
    high = full.astype(jnp.bfloat16)
    low = (full - high.astype(np.float32)).astype(jnp.bfloat16)
    return high, low


def dot(a, b):
    return jnp.dot(a, b, preferred_element_type=jnp.float32)


def run(copies):
    for copy in copies:
        copy.start()
    return copies


def finish(copies):
    for copy in copies:
        copy.wait()


def behind(values, before):
    spot = lax.broadcasted_iota(jnp.int32, (values.shape[0], 1), 0)
    one = jnp.where(spot == 0, before[1:2], pltpu.roll(values, 1, 0))
    two = jnp.where(spot == 0, before[0:1], jnp.where(spot == 1, before[1:2], pltpu.roll(values, 2, 0)))
    return one, two


def conv_rows(values, before, taps):
    values = values.astype(jnp.float32)
    one, two = behind(values, before.astype(jnp.float32))
    return taps[0:1] * values + taps[1:2] * one + taps[2:3] * two


def where(hc):
    me = lax.axis_index("ctx")
    return me, me // hc, lax.axis_index("dp") % 2


def strips(cols):
    return [slice(c, c + STRIP) for c in range(0, cols, STRIP)]


def gate_kernel(hc, count, base, feats_ref, before, taps_ref, grad_ref, *refs):
    crossing = base > 0
    outs, refs = refs[: hc * (2 if crossing else 1)], refs[hc * (2 if crossing else 1) :]
    parts, taps, stage, in_sem, small_sem, out_sem = refs
    rows, cols = parts.shape[2:]
    me, half, core = where(hc)

    def column(region, j):
        return pl.ds(pl.multiple_of((region * count + (me ^ (base + j))) * cols, cols), cols)

    small = run([pltpu.make_async_copy(taps_ref, taps, small_sem)])
    loads = [
        run(
            [
                pltpu.make_async_copy(feats_ref.at[:, column(r, j)], parts.at[j, r], in_sem.at[j, r])
                for r in range(3)
            ]
            + [pltpu.make_async_copy(grad_ref.at[:, column(0, j)], parts.at[j, 3], in_sem.at[j, 3])]
        )
        for j in range(hc)
    ]
    finish(small)
    stores = []
    for j in range(hc):
        finish(loads[j])
        mine = [(before[:, column(r, j)], taps[:, column(r, j)]) for r in range(3)]
        for strip in strips(cols):
            query, key, value = (
                conv_rows(parts[j, r, :, strip], mine[r][0][:, strip], mine[r][1][:, strip])
                for r in range(3)
            )
            stage[j, :, strip] = (key * value).astype(jnp.bfloat16)
            stage[j, :, cols + strip.start : cols + strip.stop] = (
                parts[j, 3, :, strip].astype(jnp.float32) * query
            ).astype(jnp.bfloat16)
        stores += run([pltpu.make_async_copy(stage.at[j], outs[j], out_sem.at[j])])
        if crossing:
            crossed = stage.at[j, :, pl.ds(pl.multiple_of(half * cols, cols), cols)]
            stores += run([pltpu.make_async_copy(crossed, outs[hc + j], out_sem.at[hc + j])])
    finish(stores)


def gate(feats, before, taps, grad_out, count, cols, base):
    rows = feats.shape[0]
    hc = count // 2
    shapes = [jax.ShapeDtypeStruct((rows, 2 * cols), jnp.bfloat16)] * hc
    shapes = shapes + [jax.ShapeDtypeStruct((rows, cols), jnp.bfloat16)] * hc
    hbm = pl.BlockSpec(memory_space=pl.ANY)
    return pl.pallas_call(
        functools.partial(gate_kernel, hc, count, base),
        in_specs=[hbm, pl.BlockSpec(memory_space=pltpu.VMEM), hbm, hbm],
        out_specs=[hbm] * len(shapes),
        out_shape=shapes,
        scratch_shapes=[
            pltpu.VMEM((hc, 4, rows, cols), jnp.bfloat16),
            pltpu.VMEM(taps.shape, taps.dtype),
            pltpu.VMEM((hc, rows, 2 * cols), jnp.bfloat16),
            pltpu.SemaphoreType.DMA((hc, 4)),
            pltpu.SemaphoreType.DMA,
            pltpu.SemaphoreType.DMA((len(shapes),)),
        ],
        compiler_params=params(56),
        cost_estimate=cost(20 * rows * cols * hc, 12 * rows * cols * hc),
        name="gate_other",
    )(feats, before, taps, grad_out)


def signs(first, rows):
    odd = (lax.broadcasted_iota(jnp.int32, (rows, 1), 0) + first) % 2
    return 1.0 - 2.0 * odd.astype(jnp.float32)


def filter_home_kernel(scale, filt_ref, high_ref, low_ref, near_ref, far_ref):
    size = filt_ref.shape[0] // 2

    def spectrum(part):
        now = part * scale
        high = now.astype(jnp.bfloat16)
        low = (now - high.astype(jnp.float32)).astype(jnp.bfloat16)
        return dot(high_ref[...], high) + dot(high_ref[...], low) + dot(low_ref[...], high)

    near = spectrum(filt_ref[:size, :])
    far = spectrum(filt_ref[size:, :])
    near_ref[...] = near
    sign = signs(0, size)
    far_ref[:size, :] = far[:size] - sign * near[size:]
    far_ref[size:, :] = far[size:] + sign * near[:size]


def prepare_kernel(hc, count, scale, *refs):
    filters, refs = refs[:3], refs[3:]
    gate_in, refs = refs[:4], refs[4:]
    gate_out, refs = refs[:hc], refs[hc:]
    gate_kernel(hc, count, 0, *gate_in, *gate_out, *refs[2:])
    filter_home_kernel(scale, *filters, *refs[:2])


def prepare(filt, high, low, feats, before, taps, grad_out, scale, count):
    rows = feats.shape[0]
    length, cols = filt.shape
    hc = count // 2
    shapes = [jax.ShapeDtypeStruct((rows, 2 * cols), jnp.bfloat16)] * hc
    spectra = [jax.ShapeDtypeStruct((length, cols), jnp.float32)] * 2
    hbm = pl.BlockSpec(memory_space=pl.ANY)
    vmem = pl.BlockSpec(memory_space=pltpu.VMEM)
    return pl.pallas_call(
        functools.partial(prepare_kernel, hc, count, scale),
        in_specs=[vmem] * 3 + [hbm, vmem, hbm, hbm],
        out_specs=[hbm] * hc + [vmem] * 2,
        out_shape=shapes + spectra,
        scratch_shapes=[
            pltpu.VMEM((hc, 4, rows, cols), jnp.bfloat16),
            pltpu.VMEM(taps.shape, taps.dtype),
            pltpu.VMEM((hc, rows, 2 * cols), jnp.bfloat16),
            pltpu.SemaphoreType.DMA((hc, 4)),
            pltpu.SemaphoreType.DMA,
            pltpu.SemaphoreType.DMA((len(shapes),)),
        ],
        compiler_params=params(56),
        cost_estimate=cost(8 * length * length * cols, 20 * length * cols),
        name="prepare",
    )(filt, high, low, feats, before, taps, grad_out)


def times(a_re, a_im, b_re, b_im):
    return a_re * b_re - a_im * b_im, a_re * b_im + a_im * b_re


def conj_times(a_re, a_im, b_re, b_im):
    return a_re * b_re + a_im * b_im, a_re * b_im - a_im * b_re


def spectral_kernel(hc, rows, home, scale, *refs):
    tables, refs = refs[: 4 if home else 5], refs[4 if home else 5 :]
    pieces, refs = refs[:hc], refs[hc:]
    crosses = ()
    if home:
        crosses, refs = refs[:hc], refs[hc:]
    outs, refs = refs[: 1 if home else hc], refs[1 if home else hc :]
    cross_outs = ()
    if home:
        cross_outs, refs = refs[:hc], refs[hc:]
    sums, refs = refs[:2], refs[2:]
    held, refs = refs[: len(tables)], refs[len(tables) :]
    data, spec, prod, res, corr, piece_sem, table_sem, out_sem, corr_sem = refs[:9]
    forward_ref, inverse_ref = held[:2]
    near_ref, far_ref = (held[2], held[3]) if home else (refs[-1], None)
    me, half, core = where(hc)
    spot = me % hc
    size = data.shape[0]
    cols = res.shape[1] // (3 if home else 2)

    def place(j):
        return pl.ds(pl.multiple_of((spot ^ j) * rows, rows), rows)

    def load(i):
        return run([pltpu.make_async_copy(tables[i], held[i], table_sem.at[i])])

    forward_copy = load(0)
    piece_copies = run(
        [pltpu.make_async_copy(pieces[j], data.at[place(j), : 2 * cols], piece_sem.at[j]) for j in range(hc)]
    )
    cross_copies = run(
        [
            pltpu.make_async_copy(crosses[j], data.at[place(j), 2 * cols :], piece_sem.at[hc + j])
            for j in range(len(crosses))
        ]
    )
    filter_copies = [copy for i in range(2, len(tables)) for copy in load(i)]
    inverse_copy = load(1)
    finish(forward_copy)
    finish(piece_copies)
    for part in range(data.shape[1] // cols):
        if part == 2:
            finish(cross_copies)
        here = slice(part * cols, (part + 1) * cols)
        spec[:, here] = dot(forward_ref[...], data[:, here])
    finish(filter_copies)
    if not home:
        low_ref, mine_ref, theirs_ref = held[2:]
        share = mine_ref.shape[0]
        mine = pl.ds(pl.multiple_of(core * share, share), share)
        theirs = pl.ds(pl.multiple_of((1 - core) * share, share), share)
        near_ref[...] = (
            dot(forward_ref[:, mine], mine_ref[...])
            + dot(forward_ref[:, theirs], theirs_ref[...])
            + dot(low_ref[:, mine], mine_ref[...])
            + dot(low_ref[:, theirs], theirs_ref[...])
        )

    def products(side):
        def body(i, carry):
            low = pl.ds(pl.multiple_of(i * STEP, STEP), STEP)
            high = pl.ds(pl.multiple_of(size + i * STEP, STEP), STEP)

            def get(part):
                here = slice(part * cols, (part + 1) * cols)
                return spec[low, here], spec[high, here]

            def put(part, value):
                here = slice(part * cols, (part + 1) * cols)
                prod[low, here] = value[0].astype(jnp.bfloat16)
                prod[high, here] = value[1].astype(jnp.bfloat16)

            g, d = get(0), get(1)
            h = near_ref[low, :], near_ref[high, :]
            conv = times(*h, *g)
            grad = conj_times(*h, *d)
            corr = conj_times(*g, *d)
            if home:
                f = far_ref[low, :], far_ref[high, :]
                gx, dx = (g, get(2)) if side == 0 else (get(2), d)
                far_conv = times(*f, *gx)
                far_grad = conj_times(*f, *dx)
                if side == 0:
                    grad = (grad[0] + far_grad[0], grad[1] + far_grad[1])
                else:
                    conv = (conv[0] + far_conv[0], conv[1] + far_conv[1])
                put(2, far_conv if side == 0 else far_grad)
                far_corr = conj_times(*gx, *dx)
                sign = signs(0, STEP)
                corr = (corr[0] + sign * far_corr[1], corr[1] - sign * far_corr[0])
                put(4, far_corr)
                put(3, corr)
            else:
                put(2, corr)
            put(0, conv)
            put(1, grad)
            return carry

        lax.fori_loop(0, size // STEP, body, 0)

    if home:

        @pl.when(half == 0)
        def _():
            products(0)

        @pl.when(half == 1)
        def _():
            products(1)

    else:
        products(0)

    def back(part):
        return dot(inverse_ref[...], prod[:, part * cols : (part + 1) * cols])

    finish(inverse_copy)
    res[:, :cols] = back(0).astype(jnp.bfloat16)
    res[:, cols : 2 * cols] = back(1).astype(jnp.bfloat16)
    if home:
        stores = run([pltpu.make_async_copy(res.at[:, : 2 * cols], outs[0], out_sem.at[0])])
    else:
        stores = run(
            [pltpu.make_async_copy(res.at[place(j), : 2 * cols], outs[j], out_sem.at[j]) for j in range(hc)]
        )
    if home:
        res[:, 2 * cols :] = back(2).astype(jnp.bfloat16)
        stores += run(
            [
                pltpu.make_async_copy(res.at[place(j), 2 * cols :], cross_outs[j], out_sem.at[hc + j])
                for j in range(hc)
            ]
        )
    quarter = size // 2
    for x in range(2 if home else 1):
        corr[x] = back((3 if home else 2) + x) * scale
        for i, which in enumerate((1 - core, core)):
            lags = pl.ds(pl.multiple_of(which * quarter, quarter), quarter)
            stores += run(
                [
                    pltpu.make_async_copy(
                        corr.at[x, lags], sums[i].at[x * quarter : (x + 1) * quarter], corr_sem.at[x, i]
                    )
                ]
            )
    finish(stores)


def spectral(forward, inverse, filters, pieces, crosses, scale):
    hc = len(pieces)
    rows, width = pieces[0].shape
    cols = width // 2
    size = hc * rows
    home = len(crosses) > 0
    hbm = pl.BlockSpec(memory_space=pl.ANY)
    tables = [forward, inverse, *filters]
    arrived = [*pieces, *crosses]
    ins = 3 if home else 2
    parts = 5 if home else 3
    share = jax.ShapeDtypeStruct((size if home else size // 2, cols), jnp.float32)
    sums = [share, share]
    if home:
        shapes = [jax.ShapeDtypeStruct((size, width), jnp.bfloat16)]
        shapes = shapes + [jax.ShapeDtypeStruct((rows, cols), jnp.bfloat16)] * hc
    else:
        shapes = [jax.ShapeDtypeStruct((rows, width), jnp.bfloat16)] * hc
    return pl.pallas_call(
        functools.partial(spectral_kernel, hc, rows, home, scale),
        in_specs=[hbm] * (len(tables) + len(arrived)),
        out_specs=[hbm] * (len(shapes) + len(sums)),
        out_shape=shapes + sums,
        scratch_shapes=[pltpu.VMEM(t.shape, t.dtype) for t in tables]
        + [
            pltpu.VMEM((size, ins * cols), jnp.bfloat16),
            pltpu.VMEM((2 * size, ins * cols), jnp.float32),
            pltpu.VMEM((2 * size, parts * cols), jnp.bfloat16),
            pltpu.VMEM((size, ins * cols), jnp.bfloat16),
            pltpu.VMEM((2 if home else 1, size, cols), jnp.float32),
            pltpu.SemaphoreType.DMA((len(arrived),)),
            pltpu.SemaphoreType.DMA((len(tables),)),
            pltpu.SemaphoreType.DMA((2 * hc,)),
            pltpu.SemaphoreType.DMA((2, 2)),
        ]
        + ([] if home else [pltpu.VMEM((2 * size, cols), jnp.float32)]),
        compiler_params=params(56 if home else 36),
        cost_estimate=cost(4 * size * size * cols * (ins + parts), 8 * size * size + 30 * size * cols),
        name="spectral_home" if home else "spectral_other",
    )(*tables, *arrived)


def final_kernel(hc, count, base, top, aliased, *refs):
    feats_ref, before, grad_ref, taps_ref = refs[:4]
    crosses = ()
    if base > 0:
        pieces, crosses, refs = refs[4 : 4 + hc], refs[4 + hc : 4 + 2 * hc], refs[4 + 2 * hc :]
    else:
        slots = [(lax.axis_index("ctx") % hc) ^ j for j in range(hc)]
        pieces, refs = [refs[4].at[slot] for slot in slots], refs[5:]
    if aliased:
        refs = refs[1:]
    out_ref = last_ref = stage = last = None
    if top:
        first_ref, edge_ref, parts, taps, back, edges, in_sem, small_sem, back_sem, end_sem = refs
        edge = edges.at[1]
    else:
        out_ref, edge_ref, last_ref, parts, taps, back, edge, last, stage = refs[:9]
        in_sem, small_sem, back_sem, end_sem, out_sem = refs[9:]
    me, half, _ = where(hc)
    rows, cols = parts.shape[2:]

    def column(region, j):
        return pl.ds(pl.multiple_of((region * count + (me ^ (base + j))) * cols, cols), cols)

    small = run([pltpu.make_async_copy(taps_ref, taps, small_sem)])
    if top:
        small += run([pltpu.make_async_copy(first_ref, edges.at[0], end_sem.at[1])])
    loads = []
    for j in range(hc):
        copies = [
            pltpu.make_async_copy(source.at[:rows, column(r, j)], parts.at[j, r], in_sem.at[j, r])
            for r, source in enumerate((grad_ref, feats_ref, feats_ref))
        ]
        copies.append(
            pltpu.make_async_copy(pieces[j].at[:rows], back.at[j, :, : 2 * cols], back_sem.at[j])
        )
        if base > 0:
            copies.append(
                pltpu.make_async_copy(crosses[j].at[:rows], back.at[j, :, 2 * cols :], back_sem.at[hc + j])
            )
        loads.append(run(copies))
    finish(small)
    stores = []
    spot = lax.broadcasted_iota(jnp.int32, (rows, 1), 0)
    for j in range(hc):
        finish(loads[j])
        near_taps = [taps[:, column(r, j)] for r in range(3)]
        near_before = [before[:, column(r, j)] for r in range(3)]
        slot = (me ^ (base + j)) % hc
        for strip in strips(cols):

            def unmixed(region, dz):
                edge[slot, region, :, strip] = dz[:2].astype(jnp.bfloat16)
                if top:
                    return
                weights = near_taps[region][:, strip]
                one = jnp.where(spot < rows - 1, pltpu.roll(dz, rows - 1, 0), 0.0)
                two = jnp.where(spot < rows - 2, pltpu.roll(dz, rows - 2, 0), 0.0)
                out = weights[0:1] * dz + weights[1:2] * one + weights[2:3] * two
                last[slot, region, :, strip] = out[rows - 16 :]
                stage[j, region, :, strip] = out.astype(jnp.bfloat16)

            key, value = (
                conv_rows(parts[j, r, :, strip], near_before[r][:, strip], near_taps[r][:, strip])
                for r in (1, 2)
            )
            conv = back[j, :, strip].astype(jnp.float32)
            grad = back[j, :, cols + strip.start : cols + strip.stop].astype(jnp.float32)
            if base > 0:
                extra = back[j, :, 2 * cols + strip.start : 2 * cols + strip.stop].astype(jnp.float32)
                conv = jnp.where(half == 1, conv + extra, conv)
                grad = jnp.where(half == 0, grad + extra, grad)
            unmixed(0, parts[j, 0, :, strip].astype(jnp.float32) * conv)
            unmixed(1, grad * value)
            unmixed(2, grad * key)
        if not top:
            stores += run(
                [
                    pltpu.make_async_copy(stage.at[j, r], out_ref.at[:, column(r, j)], out_sem.at[j, r])
                    for r in range(3)
                ]
            )
    stores += run([pltpu.make_async_copy(edges if top else edge, edge_ref, end_sem.at[0])])
    if not top:
        stores += run([pltpu.make_async_copy(last, last_ref, end_sem.at[1])])
    finish(stores)


def final(feats, before, grad_out, taps, pieces, crosses, so_far, count, base, first=None):
    hc = count // 2
    top = first is not None
    rows = 16 if top else feats.shape[0]
    cols = pieces[0].shape[-1] // 2
    hbm = pl.BlockSpec(memory_space=pl.ANY)
    arrived = [*pieces, *crosses]
    args = [feats, before, grad_out, taps, *arrived]
    aliases = {}
    if top:
        args.append(first)
    if so_far is not None:
        args.append(so_far)
        aliases = {len(args) - 1: 0}
    edge = jax.ShapeDtypeStruct((hc, 3, 2, cols), jnp.bfloat16)
    last = jax.ShapeDtypeStruct((hc, 3, 16, cols), jnp.float32)
    edges = jax.ShapeDtypeStruct((2, *edge.shape), edge.dtype)
    shapes = [edges] if top else [jax.ShapeDtypeStruct(feats.shape, jnp.bfloat16), edge, last]
    scratch = [
        pltpu.VMEM((hc, 3, rows, cols), jnp.bfloat16),
        pltpu.VMEM(taps.shape, taps.dtype),
        pltpu.VMEM((hc, rows, (3 if base > 0 else 2) * cols), jnp.bfloat16),
        pltpu.VMEM(edges.shape if top else edge.shape, edge.dtype),
    ]
    if not top:
        scratch += [
            pltpu.VMEM(last.shape, last.dtype),
            pltpu.VMEM((hc, 3, rows, cols), jnp.bfloat16),
        ]
    scratch += [
        pltpu.SemaphoreType.DMA((hc, 3)),
        pltpu.SemaphoreType.DMA,
        pltpu.SemaphoreType.DMA((2 * hc,)),
        pltpu.SemaphoreType.DMA((2,)),
    ]
    if not top:
        scratch.append(pltpu.SemaphoreType.DMA((hc, 3)))
    name = ("edge_" if top else "final_") + ("other" if base > 0 else "home")
    return pl.pallas_call(
        functools.partial(final_kernel, hc, count, base, top, so_far is not None),
        in_specs=[hbm, pl.BlockSpec(memory_space=pltpu.VMEM)] + [hbm] * (len(args) - 2),
        out_specs=[hbm] * len(shapes),
        scratch_shapes=scratch,
        out_shape=shapes,
        input_output_aliases=aliases,
        compiler_params=params(16 if top or base > 0 else 56),
        cost_estimate=cost(30 * rows * cols * hc, 16 * rows * cols * hc),
        name=name,
    )(*args)


def fix_kernel(hc, taps_ref, edge_ref, lh_ref, lo_ref, *refs):
    own_ref, *sums, _, out_ref, filt_ref, stage, sem = refs
    me, half, _ = where(hc)
    cols = edge_ref.shape[4]
    width = out_ref.shape[1] // 3
    turn = me == hc - 1
    spot = lax.broadcasted_iota(jnp.int32, (16, 1), 0)
    for slot, last in enumerate((lh_ref, lo_ref)):
        mine, swapped = edge_ref.at[slot], edge_ref.at[1 - slot]
        first = jnp.where(half == slot, 0, hc)
        for j in range(hc):
            for region in range(3):
                col = pl.ds(pl.multiple_of(region * width + (first + j) * cols, cols), cols)
                ahead = jnp.where(
                    turn, swapped[j, region].astype(jnp.float32), mine[j, region].astype(jnp.float32)
                )
                one, two = taps_ref[1:2, col], taps_ref[2:3, col]
                add = jnp.where(
                    spot == 14,
                    two * ahead[0:1],
                    jnp.where(spot == 15, one * ahead[0:1] + two * ahead[1:2], 0.0),
                )
                stage[:, col] = (last[j, region] + add).astype(jnp.bfloat16)
    copy = pltpu.make_async_copy(stage, out_ref.at[pl.ds(out_ref.shape[0] - 16, 16)], sem)
    copy.start()
    lags = filt_ref.shape[0]
    total = own_ref[pl.ds(pl.multiple_of((lax.axis_index("dp") // 2) * lags, lags), lags), :]
    for ref in sums:
        total += ref[...].astype(jnp.float32)
    filt_ref[...] = total
    copy.wait()


def fix(taps, edges, last_home, last_other, sums, result):
    hc = edges.shape[1]
    vmem = pl.BlockSpec(memory_space=pltpu.VMEM)
    hbm = pl.BlockSpec(memory_space=pl.ANY)
    return pl.pallas_call(
        functools.partial(fix_kernel, hc),
        in_specs=[vmem] * (4 + len(sums)) + [hbm],
        out_specs=[hbm, vmem],
        out_shape=[
            jax.ShapeDtypeStruct(result.shape, result.dtype),
            jax.ShapeDtypeStruct(sums[-1].shape, jnp.float32),
        ],
        scratch_shapes=[pltpu.VMEM((16, result.shape[1]), jnp.bfloat16), pltpu.SemaphoreType.DMA],
        input_output_aliases={4 + len(sums): 0},
        compiler_params=params(16),
        cost_estimate=cost(16 * 8 * result.shape[1], 128 * result.shape[1]),
        name="fix",
    )(taps, edges, last_home, last_other, *sums, result)


def exchange(pieces, base):
    devices = range(lax.axis_size("ctx"))
    return [
        piece if base + j == 0 else lax.ppermute(piece, "ctx", [(i, i ^ (base + j)) for i in devices])
        for j, piece in enumerate(pieces)
    ]


def within(stacked):
    count = lax.axis_size("ctx")
    groups = [list(range(count // 2)), list(range(count // 2, count))]
    return lax.all_to_all(stacked, "ctx", 0, 0, axis_index_groups=groups, tiled=True)


def half_shards(feats, short_weight, grad_out, filt):
    length, block = filt.shape
    count = lax.axis_size("ctx")
    hc = count // 2
    size = length // 2
    feats, grad_out = feats[0], grad_out[0]
    rows = feats.shape[0]
    high, low = odd_tables(size)
    inverse = np.ascontiguousarray(high.T)
    scale = 1.0 / (math.sqrt(length) * size)
    me = lax.axis_index("ctx")
    dp = lax.axis_index("dp")
    core, x = dp % 2, dp // 2
    quarter = length // 4
    tie = lax.optimization_barrier
    cores = [(i, i ^ 1) for i in range(4)]

    late, source = tie((feats[rows - 2 :], filt))
    before = from_behind(late, "ctx", 1)
    share = size // 2
    part = (lax.dynamic_slice_in_dim(source, core * share, share, 0) * scale).astype(jnp.bfloat16)
    part = lax.ppermute(part, "ctx", [(i, i ^ hc) for i in range(count)])
    gated = gate(feats, before, short_weight, grad_out, count, block, hc)

    ready, gated = tie((before, gated))
    other_pieces, across = exchange(gated[:hc], 0), gated[hc:]
    outs = prepare(filt, high, low, feats, ready, short_weight, grad_out, scale, count)
    outs, other_pieces, across, part = tie((outs, other_pieces, across, part))
    near, far = outs[hc:]

    home_pieces = exchange(outs[:hc], 0)
    rest = lax.ppermute(part, "dp", cores)
    far_sent = exchange(across[2:], hc + 2)
    outs = spectral(high, inverse, (low, part, rest), other_pieces, (), scale)
    far, outs, home_pieces, far_sent, across = tie((far, outs, home_pieces, far_sent, across))

    other_back = exchange(outs[:hc], 0)
    sent = exchange(across[:2], hc) + list(far_sent)
    send, keep = outs[hc:]
    summed = keep + lax.ppermute(send, "dp", cores)
    crossed = lax.ppermute(summed.astype(jnp.bfloat16), "ctx", [(i, i ^ hc) for i in range(count)])
    outs = spectral(high, inverse, (near, far), home_pieces, sent, scale)
    outs, other_back, crossed = tie((outs, other_back, crossed))

    home_back = within(outs[0].reshape(hc, rows, 2 * block))
    cross_back = exchange(outs[1 : 1 + hc], hc)
    send, keep = outs[1 + hc :]
    came = lax.ppermute(send, "dp", cores)
    result, edge_home, last_home = final(
        feats, before, grad_out, short_weight, [home_back], (), None, count, 0
    )
    keep, came, crossed, edge_home = tie((keep, came, crossed, edge_home))
    crossed = jnp.concatenate([crossed.astype(jnp.float32), jnp.zeros((quarter, block), jnp.float32)], axis=0)
    home_sum = keep + came + crossed
    there = lax.dynamic_slice_in_dim(home_sum, (1 - x) * quarter, quarter, 0).astype(jnp.bfloat16)
    cross_back, edge_home, there = tie((cross_back, edge_home, there))

    (edges,) = final(
        feats, before, grad_out, short_weight, other_back, cross_back, None, count, hc, edge_home
    )
    edges, there = tie((edges, there))
    edges = from_behind(edges, "ctx", -1)
    there = lax.ppermute(there, "dp", [(i, i ^ 2) for i in range(4)])
    result, _, last_other = final(
        feats, before, grad_out, short_weight, other_back, cross_back, result, count, hc
    )
    result, filt_out = fix(short_weight, edges, last_home, last_other, [home_sum, there], result)
    return (result[None], filt_out)


full_precision = lax.Precision.HIGHEST
split_precision = lax.Precision.HIGH


def from_behind(block, axis, distance):
    devices = range(lax.axis_size(axis))
    route = [(i - distance, i) for i in devices if i - distance in devices]
    return lax.ppermute(block, axis, route)


def angle_table(count_rows, count_cols, period):
    product = (
        jnp.arange(count_rows, dtype=jnp.int32)[:, None]
        * jnp.arange(count_cols, dtype=jnp.int32)[None, :]
        % period
    )
    theta = product.astype(jnp.float32) * (2.0 * math.pi / period)
    return (jnp.cos(theta), jnp.sin(theta))


def make_tables(length):
    total = 2 * length
    outer = 128
    inner = total // outer
    half = outer // 2
    freq = jnp.arange(outer, dtype=jnp.int32)[:, None, None]
    spot = (
        jnp.arange(half, dtype=jnp.int32)[None, :, None] * inner
        + jnp.arange(inner, dtype=jnp.int32)[None, None, :]
    )
    theta = (freq * spot % total).astype(jnp.float32) * (2.0 * math.pi / total)
    first = jnp.stack([jnp.cos(theta), -jnp.sin(theta)], axis=0)
    cos_b, sin_b = angle_table(inner, inner, inner)
    forward_b = jnp.stack(
        [jnp.stack([cos_b, -sin_b], axis=1), jnp.stack([sin_b, cos_b], axis=1)], axis=0
    )
    inverse_b = jnp.stack(
        [jnp.stack([cos_b, sin_b], axis=1), jnp.stack([-sin_b, cos_b], axis=1)], axis=0
    )
    return (first, forward_b, inverse_b)


def finish_forward(partial_spec, tables, accuracy):
    return jnp.einsum("sckrb,rbxq->sckxq", partial_spec, tables[1], precision=accuracy)


def data_forward(signal, tables, accuracy):
    first = tables[0]
    inner = first.shape[3]
    seqs, chans, length = signal.shape
    grid = signal.reshape(seqs, chans, length // inner, inner)
    partial_spec = jnp.einsum("rknb,scnb->sckrb", first, grid, precision=accuracy)
    return finish_forward(partial_spec, tables, accuracy)


def filter_forward(columns, tables):
    first = tables[0]
    inner = first.shape[3]
    length, chans = columns.shape
    grid = columns.reshape(length // inner, inner, chans)
    partial_spec = jnp.einsum("rknb,nbc->ckrb", first, grid, precision=full_precision)[None]
    return finish_forward(partial_spec, tables, full_precision)


def start_inverse(spectrum, tables):
    return jnp.einsum("sckxq,xqrb->sckrb", spectrum, tables[2], precision=full_precision)


def data_inverse(spectrum, tables, length):
    partial_sig = start_inverse(spectrum, tables)
    signal = jnp.einsum("sckrb,rknb->scnb", partial_sig, tables[0], precision=full_precision)
    return signal.reshape(signal.shape[0], signal.shape[1], length) / (2.0 * length)


def filter_inverse(spectrum, tables, length):
    partial_sig = start_inverse(spectrum, tables)[0]
    signal = jnp.einsum("ckrb,rknb->nbc", partial_sig, tables[0], precision=full_precision)
    return signal.reshape(length, signal.shape[2]) / (2.0 * length)


def long_spectral(gated_sig, grad_sig, filter_cols, tables, length):
    g_spec = data_forward(gated_sig, tables, split_precision)
    d_spec = data_forward(grad_sig, tables, split_precision)
    h_spec = filter_forward(filter_cols, tables)
    g_re, g_im = (g_spec[:, :, :, 0], g_spec[:, :, :, 1])
    d_re, d_im = (d_spec[:, :, :, 0], d_spec[:, :, :, 1])
    h_re, h_im = (h_spec[:, :, :, 0], h_spec[:, :, :, 1])
    conv_spec = jnp.stack([h_re * g_re - h_im * g_im, h_re * g_im + h_im * g_re], axis=3)
    grad_spec = jnp.stack([h_re * d_re + h_im * d_im, h_re * d_im - h_im * d_re], axis=3)
    prod_re = jnp.sum(g_re * d_re + g_im * d_im, axis=0, keepdims=True)
    prod_im = jnp.sum(g_re * d_im - g_im * d_re, axis=0, keepdims=True)
    prod_spec = jnp.stack([prod_re, prod_im], axis=3)
    conv_out = data_inverse(conv_spec, tables, length)
    gated_grad = data_inverse(grad_spec, tables, length)
    filt_grad = filter_inverse(prod_spec, tables, length)
    return (conv_out, gated_grad, filt_grad)


def long_shards(feats, short_weight, grad_out, filt):
    rows = feats.shape[1]
    width = feats.shape[2] // 3
    length = filt.shape[0]
    block = filt.shape[1]
    ctx_count = lax.axis_size("ctx")
    replicas = lax.axis_size("dp")
    scale_inv = 1.0 / math.sqrt(length)
    tables = make_tables(length)
    prior = from_behind(feats[:, rows - 2 :, :], "ctx", 1)
    extended = jnp.concatenate([prior, feats], axis=1).astype(jnp.float32)
    mixed = (
        short_weight[0] * extended[:, 2:]
        + short_weight[1] * extended[:, 1 : rows + 1]
        + short_weight[2] * extended[:, :rows]
    )
    query_rows = mixed[:, :, :width]
    key_rows = mixed[:, :, width : 2 * width]
    value_rows = mixed[:, :, 2 * width :]
    gated = (key_rows * value_rows).astype(jnp.bfloat16)
    out_grad = grad_out.astype(jnp.float32)
    conv_grad = (out_grad * query_rows).astype(jnp.bfloat16)
    narrow = block // replicas

    def spread(array):
        return array[0].reshape(rows, ctx_count, replicas, narrow).transpose(1, 2, 3, 0)[:, :, None]

    wide_gated, wide_grad = (
        lax.all_to_all(
            lax.all_to_all(spread(gated), "dp", split_axis=1, concat_axis=2, tiled=True),
            "ctx",
            split_axis=0,
            concat_axis=4,
            tiled=True,
        ),
        lax.all_to_all(
            lax.all_to_all(spread(conv_grad), "dp", split_axis=1, concat_axis=2, tiled=True),
            "ctx",
            split_axis=0,
            concat_axis=4,
            tiled=True,
        ),
    )
    wide_gated = wide_gated.reshape(replicas, narrow, length)
    wide_grad = wide_grad.reshape(replicas, narrow, length)
    offset = lax.axis_index("dp") * narrow
    filt_cols = lax.dynamic_slice_in_dim(filt, offset, narrow, 1)
    conv_out, gated_grad, filt_grad = long_spectral(
        wide_gated, wide_grad, filt_cols * scale_inv, tables, length
    )
    back_conv, back_grad = (
        lax.all_to_all(
            lax.all_to_all(
                conv_out.astype(jnp.bfloat16)[None, None],
                "dp",
                split_axis=2,
                concat_axis=1,
                tiled=True,
            ),
            "ctx",
            split_axis=4,
            concat_axis=0,
            tiled=True,
        ),
        lax.all_to_all(
            lax.all_to_all(
                gated_grad.astype(jnp.bfloat16)[None, None],
                "dp",
                split_axis=2,
                concat_axis=1,
                tiled=True,
            ),
            "ctx",
            split_axis=4,
            concat_axis=0,
            tiled=True,
        ),
    )

    def gather_positions(array):
        return (
            array.reshape(ctx_count, replicas, narrow, rows)
            .transpose(3, 0, 1, 2)
            .reshape(1, rows, width)
        )

    conv_rows = gather_positions(back_conv)
    grad_rows = gather_positions(back_grad)
    parts = filt_grad.reshape(replicas, length // replicas, 1, narrow)
    owned = lax.all_to_all(parts, "dp", split_axis=0, concat_axis=2, tiled=True)
    filt_out = owned.reshape(length // replicas, block) * scale_inv
    grad_query = out_grad * conv_rows.astype(jnp.float32)
    grad_key = grad_rows.astype(jnp.float32) * value_rows
    grad_value = grad_rows.astype(jnp.float32) * key_rows
    grad_mixed = jnp.concatenate([grad_query, grad_key, grad_value], axis=2)
    following = from_behind(grad_mixed[:, :2, :].astype(jnp.bfloat16), "ctx", -1).astype(
        jnp.float32
    )
    ahead = jnp.concatenate([grad_mixed, following], axis=1)
    grad_in = (
        short_weight[0] * grad_mixed
        + short_weight[1] * ahead[:, 1 : rows + 1]
        + short_weight[2] * ahead[:, 2 : rows + 2]
    )
    return (grad_in.astype(jnp.bfloat16), filt_out)


def shards(feats, short_weight, grad_out, filt):
    count = lax.axis_size("ctx")
    length, block = filt.shape
    fits = (
        length <= 1024
        and length % (4 * STEP) == 0
        and count > 1
        and count & (count - 1) == 0
        and feats.shape[1] % 128 == 0
        and block % 128 == 0
        and lax.axis_size("dp") == 4
    )
    plan = half_shards if fits else long_shards
    return plan(feats, short_weight, grad_out, filt)


def solution(mesh):
    return jax.shard_map(
        shards,
        mesh=mesh,
        in_specs=(P("dp", "ctx", None), P(), P("dp", "ctx", None), P(None, "ctx")),
        out_specs=(P("dp", "ctx", None), P("dp", "ctx")),
        check_vma=False,
    )
```
